32 devices in a mesh: fsdp: 8 (over z, x), dp: 4 (over y, core).
Axes of the slice: x: 2, y: 2, z: 4, core: 2. Of those that a mesh axis runs over, the one named last changes fastest.
Arguments:
- hidden_in: bfloat16 [64, 512, 1088], P(('fsdp', 'dp')), may hold values from -6 to 6
- cotangent: bfloat16 [64, 512, 1088], P(('fsdp', 'dp')), may hold values from -6 to 6
- lengths: int32 [64], P(('fsdp', 'dp')), may hold values from 1 to 512, as said below
- qkv_weight: float32 [1088, 3264], P('fsdp'), may hold values from -0.1875 to 0.1875
- qkv_mean: float32 [1088, 3264], P('fsdp'), may hold values from -40 to 40
- qkv_square: float32 [1088, 3264], P('fsdp'), may hold values from 3.41325 to 13.653
- out_weight: float32 [1088, 1088], P('fsdp'), may hold values from -0.75 to 0.75
- out_mean: float32 [1088, 1088], P('fsdp'), may hold values from -12 to 12
- out_square: float32 [1088, 1088], P('fsdp'), may hold values from 0.314019 to 1.22877
- up_weight: float32 [1088, 4352], P(None, 'fsdp'), may hold values from -0.1875 to 0.1875
- up_mean: float32 [1088, 4352], P(None, 'fsdp'), may hold values from -24 to 24
- up_square: float32 [1088, 4352], P(None, 'fsdp'), may hold values from 1.22877 to 4.91508
- down_weight: float32 [4352, 1088], P('fsdp'), may hold values from -0.09375 to 0.09375
- down_mean: float32 [4352, 1088], P('fsdp'), may hold values from -48 to 48
- down_square: float32 [4352, 1088], P('fsdp'), may hold values from 5.73426 to 23.2101
- vectors: float32 [8, 1088], P(None, 'fsdp'), may hold values from -1.2 to 1.4, as said below
- vectors_mean: float32 [8, 1088], P(None, 'fsdp'), may hold values from -64 to 64
- vectors_square: float32 [8, 1088], P(None, 'fsdp'), may hold values from 8.73792 to 35.4978
- upbias: float32 [4352], P('fsdp'), may hold values from -1.25 to 1.25
- upbias_mean: float32 [4352], P('fsdp'), may hold values from -24 to 24
- upbias_square: float32 [4352], P('fsdp'), may hold values from 1.22877 to 4.91508
Outputs:
- output: bfloat16 [64, 512, 1088], P(('fsdp', 'dp'))
- input_grad: float32 [64, 512, 1088], P(('fsdp', 'dp'))
- qkv_next: float32 [1088, 3264], P('fsdp')
- qkvmean_next: float32 [1088, 3264], P('fsdp')
- qkvsquare_next: float32 [1088, 3264], P('fsdp')
- out_next: float32 [1088, 1088], P('fsdp')
- outmean_next: float32 [1088, 1088], P('fsdp')
- outsquare_next: float32 [1088, 1088], P('fsdp')
- up_next: float32 [1088, 4352], P(None, 'fsdp')
- upmean_next: float32 [1088, 4352], P(None, 'fsdp')
- upsquare_next: float32 [1088, 4352], P(None, 'fsdp')
- down_next: float32 [4352, 1088], P('fsdp')
- downmean_next: float32 [4352, 1088], P('fsdp')
- downsquare_next: float32 [4352, 1088], P('fsdp')
- vectors_next: float32 [8, 1088], P(None, 'fsdp')
- vectorsmean_next: float32 [8, 1088], P(None, 'fsdp')
- vectorssquare_next: float32 [8, 1088], P(None, 'fsdp')
- upbias_next: float32 [4352], P('fsdp')
- upbiasmean_next: float32 [4352], P('fsdp')
- upbiassquare_next: float32 [4352], P('fsdp')
The draws below stay inside these ranges and needn't reach their ends.
Inputs may be any that keep to these rules, and one draw needn't show every extreme that they name: `lengths`: every block holds one sequence of 1 to 512 tokens at its start; some block holds exactly 512. `vectors`: rows 0 and 5 are positive gains; the other rows are biases of both signs.
All inputs are finite; a program needn't handle non-finite values.
Results may differ from the reference program's by a relative error of at most 0.0095.
The reference program's roundings to bfloat16 on the way count: a program that leaves them out, or rounds other values in their place, can miss the bound.
Values may be sent and summed in bfloat16 or wider, within the bound.
No kernel may reach another device: no remote copies, remote signals or barrier semaphores. Data moves between devices by JAX's collectives and lax.ppermute only.
A program may use at most 320 MiB of HBM per device.

```python
import math
import jax
import jax.numpy as jnp
from jax import lax

D = 1088
HEADS = 17
HDIM = 64
FF = 4352
BLOCK = 512
SLOTS = 2
STEP = 10
SHARDS = 8
REPLICAS = 4
NBLK = 64


def draw_lengths(key, part):
    key = jax.random.fold_in(key, 11)
    blocks = jnp.arange(NBLK, dtype=jnp.int32)
    device = blocks // SLOTS
    shard_index = device // REPLICAS
    replica_index = device % REPLICAS
    ceiling = BLOCK * (SHARDS - 1 + 2 * shard_index) * (REPLICAS - 1 + 2 * replica_index) // (9 * (SHARDS - 1) * (REPLICAS - 1))
    ceiling = jnp.maximum(ceiling, 1)
    floor_len = jnp.maximum(7 * ceiling // 8, 1)
    sampled = jax.random.randint(key, (NBLK,), floor_len, ceiling + 1)
    return jnp.where(blocks == NBLK - 1, BLOCK, sampled).astype(jnp.int32)


def draw_vectors(key, part):
    key = jax.random.fold_in(key, 23)
    key_scale, key_offset = jax.random.split(key)
    row_ids = jnp.arange(8, dtype=jnp.int32)[:, None]
    is_scale = (row_ids == 0) | (row_ids == 5)
    scales = jax.random.uniform(key_scale, (8, D), jnp.float32, 0.7, 1.3)
    offsets = jnp.clip(0.2 * jax.random.normal(key_offset, (8, D), jnp.float32), -1.2, 1.2)
    return jnp.where(is_scale, scales, offsets).astype(jnp.float32)


def block_scale(stream_key, extent, pieces, low, top_value):
    loudness, own = 1.0, jax.random.fold_in(stream_key, 6)
    for position, blocks in pieces:
        heights = jnp.exp(jax.random.uniform(jax.random.fold_in(own, position), (blocks,), jnp.float32, low / len(pieces), top_value / len(pieces)))
        loudness = loudness * jnp.repeat(heights, extent[position] // blocks).reshape([-1 if axis == position else 1 for axis in range(len(extent))])
    return loudness


def normal_values(own_key, dims, scale, bound, pieces=(), kind=jnp.bfloat16):
    values = scale * jax.random.normal(own_key, dims, jnp.float32)
    if pieces:
        values = values * block_scale(own_key, dims, pieces, -0.22, 0.18)
    return jnp.clip(values, -bound, bound).astype(kind)


def setup_inputs(seed: int = 0) -> dict:
    splits = jax.random.split(jax.random.key(seed), 22)
    return {
        "hidden_in": normal_values(splits[0], (NBLK, BLOCK, D), 1.0, 6.0, ((0, 32),)),
        "cotangent": normal_values(splits[1], (NBLK, BLOCK, D), 1.0, 6.0, ((0, 32),)),
        "lengths": draw_lengths(jax.random.fold_in(splits[21], 71), 0),
        "qkv_weight": normal_values(splits[3], (D, 3 * D), D ** -0.5, 0.1875, ((0, 8),), jnp.float32),
        "qkv_mean": normal_values(splits[4], (D, 3 * D), (0.056 * (NBLK * BLOCK * 5 // 12) ** 0.5), 40.0, ((0, 8),), jnp.float32),
        "qkv_square": jnp.clip(jnp.exp(math.log(13.653) - 1.3862944 * jax.random.uniform(splits[5], (D, 3 * D), jnp.float32) ** block_scale(splits[5], (D, 3 * D), ((0, 8),), -0.2, 0.2)), 3.41325, 13.653),
        "out_weight": normal_values(splits[6], (D, D), (D // 16) ** -0.5, 0.75, ((0, 8),), jnp.float32),
        "out_mean": normal_values(splits[7], (D, D), (0.017 * (NBLK * BLOCK * 5 // 12) ** 0.5), 12.0, ((0, 8),), jnp.float32),
        "out_square": jnp.clip(jnp.exp(math.log(1.22877) - 1.3643155 * jax.random.uniform(splits[8], (D, D), jnp.float32) ** block_scale(splits[8], (D, D), ((0, 8),), -0.2, 0.2)), 0.314019, 1.22877),
        "up_weight": normal_values(splits[9], (D, FF), D ** -0.5, 0.1875, ((1, 8),), jnp.float32),
        "up_mean": normal_values(splits[10], (D, FF), (0.033 * (NBLK * BLOCK * 5 // 12) ** 0.5), 24.0, ((1, 8),), jnp.float32),
        "up_square": jnp.clip(jnp.exp(math.log(4.91508) - 1.3862944 * jax.random.uniform(splits[11], (D, FF), jnp.float32) ** block_scale(splits[11], (D, FF), ((1, 8),), -0.2, 0.2)), 1.22877, 4.91508),
        "down_weight": normal_values(splits[12], (FF, D), FF ** -0.5, 0.09375, ((0, 8),), jnp.float32),
        "down_mean": normal_values(splits[13], (FF, D), (0.072 * (NBLK * BLOCK * 5 // 12) ** 0.5), 48.0, ((0, 8),), jnp.float32),
        "down_square": jnp.clip(jnp.exp(math.log(23.2101) - 1.39812881 * jax.random.uniform(splits[14], (FF, D), jnp.float32) ** block_scale(splits[14], (FF, D), ((0, 8),), -0.2, 0.2)), 5.73426, 23.2101),
        "vectors": draw_vectors(jax.random.fold_in(splits[21], 71), 0),
        "vectors_mean": normal_values(splits[16], (8, D), (0.089 * (NBLK * BLOCK * 5 // 12) ** 0.5), 64.0, ((1, 8),), jnp.float32),
        "vectors_square": jnp.clip(jnp.exp(math.log(35.4978) - 1.4017985 * jax.random.uniform(splits[17], (8, D), jnp.float32) ** block_scale(splits[17], (8, D), ((1, 8),), -0.2, 0.2)), 8.73792, 35.4978),
        "upbias": normal_values(splits[18], (FF,), 0.2, 1.25, ((0, 8),), jnp.float32),
        "upbias_mean": normal_values(splits[19], (FF,), (0.033 * (NBLK * BLOCK * 5 // 12) ** 0.5), 24.0, ((0, 8),), jnp.float32),
        "upbias_square": jnp.clip(jnp.exp(math.log(4.91508) - 1.3862944 * jax.random.uniform(splits[20], (FF,), jnp.float32) ** block_scale(splits[20], (FF,), ((0, 8),), -0.2, 0.2)), 1.22877, 4.91508),
    }


@jax.custom_vjp
def low(v):
    return lax.optimization_barrier(v.astype(jnp.bfloat16)).astype(jnp.float32)

@jax.custom_vjp
def low_back(v):
    return v

def low_keep(v):
    return (low(v), None)

def low_pass(kept, grad):
    return (grad,)

def back_keep(v):
    return (v, None)

def back_low(kept, grad):
    return (low(grad),)
low.defvjp(low_keep, low_pass)
low_back.defvjp(back_keep, back_low)
norm_eps = 1e-05
beta_first = 0.9
beta_second = 0.999
adam_floor = 1e-08
step_rates = (0.05, 0.2, 0.05, 0.03, 0.5, 0.3)
decay_rates = (0.1, 0.1, 0.1, 0.1, 0.0, 0.0)
exact_mode = lax.Precision.HIGHEST

def layer_norm(values, scales, offset):
    center = values - lax.optimization_barrier(jnp.mean(values, axis=-1, keepdims=True))
    inverse = lax.rsqrt(lax.optimization_barrier(jnp.mean(center * center, axis=-1, keepdims=True)) + norm_eps)
    return center * inverse * scales + offset

def attend(triple):
    queries, key_rows, values_in = triple
    scores = jnp.einsum('qhd,khd->hqk', queries, key_rows, precision=exact_mode) * (1.0 / math.sqrt(HDIM))
    scores = low_back(scores)
    rows_at = lax.broadcasted_iota(jnp.int32, scores.shape, 1)
    cols_at = lax.broadcasted_iota(jnp.int32, scores.shape, 2)
    scores = jnp.where(rows_at >= cols_at, scores, -1e+30)
    row_top = lax.optimization_barrier(jnp.max(scores, axis=-1, keepdims=True))
    powers = jnp.exp(scores - row_top)
    attn_probs = powers / lax.optimization_barrier(jnp.sum(powers, axis=-1, keepdims=True))
    return jnp.einsum('hqk,khd->qhd', low(attn_probs), values_in, precision=exact_mode)

def group_forward(params, tokens, row_valid):
    qkv_w, out_w, up_w, down_w, vec_w, bias_w = [low(member) for member in params]
    seq_count = tokens.shape[0]
    flat_rows = tokens.reshape(seq_count * BLOCK, D)
    normed = low(layer_norm(flat_rows, vec_w[0], vec_w[1]))
    bias_row = jnp.concatenate([vec_w[2], jnp.zeros((D,), jnp.float32), vec_w[3]])
    qkv_rows = low(low_back(jnp.dot(normed, qkv_w, precision=exact_mode) + bias_row))
    qkv_rows = qkv_rows.reshape(seq_count, BLOCK, 3, HEADS, HDIM)
    context = lax.map(jax.checkpoint(attend), (qkv_rows[:, :, 0], qkv_rows[:, :, 1], qkv_rows[:, :, 2]))
    context = low(low_back(context.reshape(seq_count * BLOCK, D)))
    branch = low_back(jnp.dot(context, out_w, precision=exact_mode) + vec_w[4])
    residual = flat_rows + branch
    second = low(layer_norm(residual, vec_w[5], vec_w[6]))
    up_pre = low_back(jnp.dot(second, up_w, precision=exact_mode) + bias_w)
    active = low(jax.nn.gelu(up_pre, approximate=True))
    result = residual + jnp.dot(active, down_w, precision=exact_mode) + vec_w[7]
    return (result * row_valid.reshape(seq_count * BLOCK, 1)).reshape(seq_count, BLOCK, D)

def adam_update(weight, mean_old, square_old, gradient, step_rate, decay_rate):
    mean_new = beta_first * mean_old + (1.0 - beta_first) * gradient
    square_new = beta_second * square_old + (1.0 - beta_second) * gradient * gradient
    mean_hat = mean_new / (1.0 - beta_first ** STEP)
    square_hat = square_new / (1.0 - beta_second ** STEP)
    weight_new = weight - step_rate * (mean_hat / (jnp.sqrt(square_hat) + adam_floor) + decay_rate * weight)
    return (weight_new, mean_new, square_new)

def reference(hidden_in, cotangent, lengths, qkv_weight, qkv_mean, qkv_square, out_weight, out_mean, out_square, up_weight, up_mean, up_square, down_weight, down_mean, down_square, vectors, vectors_mean, vectors_square, upbias, upbias_mean, upbias_square):
    masters = (qkv_weight, out_weight, up_weight, down_weight, vectors, upbias)
    first_moments = (qkv_mean, out_mean, up_mean, down_mean, vectors_mean, upbias_mean)
    squares = (qkv_square, out_square, up_square, down_square, vectors_square, upbias_square)
    tokens = hidden_in.astype(jnp.float32).reshape(NBLK // 8, 8, BLOCK, D)
    cotangents = cotangent.astype(jnp.float32).reshape(NBLK // 8, 8, BLOCK, D)
    positions = jnp.arange(BLOCK, dtype=jnp.int32)
    row_valid = (positions[None, :] < lengths[:, None]).astype(jnp.float32).reshape(NBLK // 8, 8, BLOCK)

    def group_step(totals, inputs):
        block_data, block_back, block_keep = inputs

        def forward(params, values):
            return group_forward(params, values, block_keep)
        result, pullback = jax.vjp(forward, masters, block_data)
        param_grads, data_grad = pullback(block_back)
        return (jax.tree.map(jnp.add, totals, param_grads), (result, data_grad))
    empty_sums = tuple((jnp.zeros_like(member) for member in masters))
    totals, (results, data_grads) = lax.scan(group_step, empty_sums, (tokens, cotangents, row_valid))
    output = results.reshape(NBLK, BLOCK, D).astype(jnp.bfloat16)
    input_grad = data_grads.reshape(NBLK, BLOCK, D)
    updates = []
    for group_index in range(6):
        updates.extend(adam_update(masters[group_index], first_moments[group_index], squares[group_index], totals[group_index], step_rates[group_index], decay_rates[group_index]))
    return (output, input_grad, updates[0], updates[1], updates[2], updates[3], updates[4], updates[5], updates[6], updates[7], updates[8], updates[9], updates[10], updates[11], updates[12], updates[13], updates[14], updates[15], updates[16], updates[17])
```

```python
import functools
import math

import jax
import jax.numpy as jnp
from jax import lax
from jax.experimental import pallas as pl
from jax.experimental.pallas import tpu as pltpu
from jax.sharding import PartitionSpec as P

D = 1088
HEADS = 17
HDIM = 64
BLOCK = 512
STEP = 10
EXTRA = 8

norm_eps = 1e-05
beta_first = 0.9
beta_second = 0.999
adam_floor = 1e-08
step_rates = (0.05, 0.2, 0.05, 0.03, 0.5, 0.3)
decay_rates = (0.1, 0.1, 0.1, 0.1, 0.0, 0.0)

AXES = ("fsdp", "dp")
f32 = jnp.float32
bf16 = jnp.bfloat16


class Grid:
    def __init__(self):
        self.shards = lax.axis_size("fsdp")
        self.replicas = lax.axis_size("dp")
        self.zs = self.shards // 2
        self.ys = self.replicas // 2
        f, r = lax.axis_index("fsdp"), lax.axis_index("dp")
        self.z, self.x = f // 2, f % 2
        self.y, self.c = r // 2, r % 2
        self.r = r

    def move(self, value, dz=0, dx=0, dy=0, dc=0):
        pairs = []
        for z in range(self.zs):
            for x in range(2):
                for y in range(2):
                    for c in range(2):
                        here = (2 * z + x) * 4 + 2 * y + c
                        there = (2 * ((z + dz) % self.zs) + (x ^ dx)) * 4 + 2 * (y ^ dy) + (c ^ dc)
                        pairs.append((here, there))
        return lax.ppermute(value, AXES, pairs)


def after(value, *others):
    return lax.optimization_barrier((value,) + others)[0]


def take(value, at, axis=0):
    return lax.dynamic_index_in_dim(value, at, axis, keepdims=False)


def assemble_kernel(zs, *refs):
    pieces, out, sem = refs[:-2], refs[-2], refs[-1]
    f, r = lax.axis_index("fsdp"), lax.axis_index("dp")
    z, x, y, c = f // 2, f % 2, r // 2, r % 2
    copies = []
    number = 0
    for dc in range(2):
        for dy in range(2):
            for dx in range(2):
                for half in range(2):
                    piece = pieces[number]
                    number += 1
                    for k in range(zs // 2):
                        at_z = lax.rem(z - (half * (zs // 2) + k) + zs, zs)
                        owner = 2 * (y ^ dy) + (c ^ dc)
                        copies.append(
                            pltpu.make_async_copy(
                                piece.at[k],
                                out.at[owner, 2 * at_z + (x ^ dx)],
                                sem,
                            )
                        )
    for copy in copies:
        copy.start()
    for copy in copies:
        copy.wait()


def assemble(grid, pieces, rows):
    return pl.pallas_call(
        functools.partial(assemble_kernel, grid.zs),
        out_shape=jax.ShapeDtypeStruct((4, grid.shards, rows, D), bf16),
        in_specs=[pl.BlockSpec(memory_space=pl.ANY)] * len(pieces),
        out_specs=pl.BlockSpec(memory_space=pl.ANY),
        scratch_shapes=[pltpu.SemaphoreType.DMA(())],
        name="assemble",
    )(*pieces)


def gather_z(grid, unit):
    got = [unit] + [grid.move(unit, dz=k) for k in range(1, grid.zs)]
    half = grid.zs // 2
    return [jnp.stack(got[:half]), jnp.stack(got[half:])]


def gather_xy(grid, halves):
    over_x = [grid.move(h, dx=1) for h in halves]
    over_y = [grid.move(h, dy=1) for h in halves]
    diagonal = [grid.move(over_y[0], dx=1), grid.move(over_x[1], dy=1)]
    return halves + over_x + over_y + diagonal


def gather_core(grid, pieces):
    return pieces + [grid.move(p, dc=1) for p in pieces]


def reduce_group(grid, grads):
    n = grads.shape[2]
    zs, half = grid.zs, grid.zs // 2
    view = grads.reshape(2, 2, zs, 2, n, D)
    z, x, y, c = grid.z, grid.x, grid.y, grid.c
    theirs = take(view, 1 - c, 1)
    mine = take(view, c, 1)
    slabs = []
    for part in range(2):
        low, high = part * half, (part + 1) * half
        got = grid.move(theirs[:, low:high], dc=1)
        total = (mine[:, low:high].astype(f32) + got.astype(f32)).astype(bf16)
        far = take(total, 1 - y, 0)
        near = take(total, y, 0)
        diagonal = take(far, 1 - x, 1)
        to_y = take(far, x, 1)
        to_x = take(near, 1 - x, 1)
        own = take(near, x, 1)
        if part == 0:
            passed = grid.move(diagonal, dx=1)
            to_y = (to_y.astype(f32) + passed.astype(f32)).astype(bf16)
        else:
            passed = grid.move(diagonal, dy=1)
            to_x = (to_x.astype(f32) + passed.astype(f32)).astype(bf16)
        got_x = grid.move(to_x, dx=1)
        got_y = grid.move(to_y, dy=1)
        slabs.append((own.astype(f32) + got_x.astype(f32) + got_y.astype(f32)).astype(bf16))
    slab = jnp.concatenate(slabs)
    total = take(slab, z).astype(f32)
    for k in range(1, zs):
        total = total + grid.move(take(slab, (z + k) % zs), dz=k).astype(f32)
    return total.astype(bf16)


def share_unit(grid, unit):
    over_c = grid.move(unit, dc=1)
    over_y = grid.move(unit, dy=1)
    over_yc = grid.move(over_y, dc=1)
    both = jnp.stack([unit, over_c, over_y, over_yc])
    return [take(both, jnp.bitwise_xor(grid.r, r)) for r in range(4)]


def reduce_small(grid, value):
    value = value + grid.move(value, dc=1)
    value = value + grid.move(value, dy=1)
    value = value + grid.move(value, dx=1)
    parts = [value] + [grid.move(value, dz=k) for k in range(1, grid.zs)]
    return sum(parts[1:], parts[0])


def norm_forward(values, scales, offset):
    center = values - jnp.mean(values, axis=-1, keepdims=True)
    inverse = lax.rsqrt(jnp.mean(center * center, axis=-1, keepdims=True) + norm_eps)
    norm_hat = center * inverse
    return (norm_hat * scales + offset, norm_hat, inverse)


def norm_backward(gradient, norm_hat, inverse, scales):
    hat_grad = gradient * scales
    value_grad = inverse * (
        hat_grad
        - jnp.mean(hat_grad, axis=-1, keepdims=True)
        - norm_hat * jnp.mean(hat_grad * norm_hat, axis=-1, keepdims=True)
    )
    return (value_grad, jnp.sum(gradient * norm_hat, axis=0), jnp.sum(gradient, axis=0))


def causal_scores(queries, key_rows):
    scores = jnp.einsum("qhd,khd->hqk", queries, key_rows, preferred_element_type=f32) * (
        1.0 / math.sqrt(HDIM)
    )
    rows_at = lax.broadcasted_iota(jnp.int32, scores.shape, 1)
    cols_at = lax.broadcasted_iota(jnp.int32, scores.shape, 2)
    return jnp.where(rows_at >= cols_at, scores, -1e30)


def attend_forward(triple):
    queries, key_rows, values_in = triple
    scores = causal_scores(queries, key_rows)
    row_top = jnp.max(scores, axis=-1, keepdims=True)
    powers = jnp.exp(scores - row_top)
    row_total = jnp.sum(powers, axis=-1, keepdims=True)
    attn_probs = (powers / row_total).astype(bf16)
    context = jnp.einsum("hqk,khd->qhd", attn_probs, values_in, preferred_element_type=f32)
    return (context.astype(bf16), (row_top + jnp.log(row_total))[..., 0])


def attend_backward(pieces):
    queries, key_rows, values_in, logsum, context_grad = pieces
    scores = causal_scores(queries, key_rows)
    attn_probs = jnp.exp(scores - logsum[..., None])
    prob_grad = jnp.einsum("qhd,khd->hqk", context_grad, values_in, preferred_element_type=f32)
    values_grad = jnp.einsum(
        "hqk,qhd->khd", attn_probs.astype(bf16), context_grad, preferred_element_type=f32
    )
    inner_sum = jnp.sum(attn_probs * prob_grad, axis=-1, keepdims=True)
    score_grad = (attn_probs * (prob_grad - inner_sum)).astype(bf16)
    scale_factor = 1.0 / math.sqrt(HDIM)
    query_grad = jnp.einsum("hqk,khd->qhd", score_grad, key_rows, preferred_element_type=f32)
    keys_grad = jnp.einsum("hqk,qhd->khd", score_grad, queries, preferred_element_type=f32)
    return (
        (query_grad * scale_factor).astype(bf16),
        (keys_grad * scale_factor).astype(bf16),
        values_grad.astype(bf16),
    )


def adam_update(weight, mean_old, square_old, gradient, step_rate, decay_rate):
    mean_new = beta_first * mean_old + (1.0 - beta_first) * gradient
    square_new = beta_second * square_old + (1.0 - beta_second) * gradient * gradient
    mean_hat = mean_new / (1.0 - beta_first**STEP)
    square_hat = square_new / (1.0 - beta_second**STEP)
    weight_new = weight - step_rate * (
        mean_hat / (jnp.sqrt(square_hat) + adam_floor) + decay_rate * weight
    )
    return (weight_new, mean_new, square_new)


def per_device(
    hidden_in,
    cotangent,
    lengths,
    qkv_weight,
    qkv_mean,
    qkv_square,
    out_weight,
    out_mean,
    out_square,
    up_weight,
    up_mean,
    up_square,
    down_weight,
    down_mean,
    down_square,
    vectors,
    vectors_mean,
    vectors_square,
    upbias,
    upbias_mean,
    upbias_square,
):
    shards = (qkv_weight, out_weight, up_weight, down_weight, vectors, upbias)
    first_moments = (qkv_mean, out_mean, up_mean, down_mean, vectors_mean, upbias_mean)
    squares = (qkv_square, out_square, up_square, down_square, vectors_square, upbias_square)
    grid = Grid()
    n = D // grid.shards
    slots = hidden_in.shape[0]
    row_count = slots * BLOCK
    ff = 4 * D

    attn_units = jnp.stack(
        [qkv_weight[:, :D], qkv_weight[:, D : 2 * D], qkv_weight[:, 2 * D :], out_weight]
    )
    attn_unit = take(attn_units, grid.r).astype(bf16)
    small = jnp.concatenate([vectors.reshape(-1), upbias]).astype(bf16)
    small = jnp.pad(small, (0, EXTRA * D - small.shape[0])).reshape(EXTRA, D)
    up_unit = lax.dynamic_slice_in_dim(up_weight, grid.r * n, n, 1).astype(bf16).T
    down_unit = lax.dynamic_slice_in_dim(down_weight, grid.r * n, n, 0).astype(bf16)

    small_half = gather_z(grid, small)
    attn_half = gather_z(grid, after(attn_unit, *small_half))
    up_half = gather_z(grid, after(up_unit, *attn_half))
    down_half = gather_z(grid, after(down_unit, *up_half))
    attn_xy = gather_xy(grid, attn_half)
    attn_pieces = gather_core(grid, attn_xy)
    tied = lax.optimization_barrier(tuple(up_half) + tuple(attn_xy))
    up_xy = gather_xy(grid, list(tied[:2]))
    up_pieces = gather_core(grid, up_xy)
    tied = lax.optimization_barrier(tuple(down_half) + tuple(up_xy))
    down_xy = gather_xy(grid, list(tied[:2]))
    down_pieces = gather_core(grid, down_xy)
    attn_full = assemble(grid, attn_pieces, n)
    up_full = assemble(grid, up_pieces, n).reshape(ff, D)
    down_full = assemble(grid, down_pieces, n).reshape(ff, D)

    own = jnp.concatenate(small_half).reshape(grid.zs, EXTRA * D)[:, : 12 * n]
    other = grid.move(own, dx=1)
    pair = jnp.stack([own, other])
    pair = jnp.stack([take(pair, grid.x), take(pair, 1 - grid.x)])
    order = lax.rem(grid.z - jnp.arange(grid.zs) + grid.zs, grid.zs)
    pair = pair[:, order]
    smalls = pair.transpose(1, 0, 2).reshape(grid.shards, 12 * n)
    vec_values = (
        smalls[:, : 8 * n].reshape(grid.shards, 8, n).transpose(1, 0, 2).reshape(8, D).astype(f32)
    )
    bias_full = (
        smalls[:, 8 * n :].reshape(grid.shards, 4, n).transpose(1, 0, 2).reshape(ff).astype(f32)
    )

    attn_full = attn_full.reshape(4, D, D)
    qkv_full, out_full = attn_full[:3], attn_full[3]

    flat_in = hidden_in.reshape(row_count, D).astype(f32)
    positions = jnp.arange(BLOCK, dtype=jnp.int32)
    row_valid = (positions[None, :] < lengths[:, None]).astype(f32).reshape(row_count, 1)
    normed_one, hat_one, inv_one = norm_forward(flat_in, vec_values[0], vec_values[1])
    normed_low = normed_one.astype(bf16)
    bias_rows = jnp.stack([vec_values[2], jnp.zeros((D,), f32), vec_values[3]])
    qkv_rows = [
        (
            jnp.dot(normed_low, qkv_full[i], preferred_element_type=f32) + bias_rows[i]
        ).astype(bf16).reshape(slots, BLOCK, HEADS, HDIM)
        for i in range(3)
    ]
    context, logsum = lax.map(attend_forward, tuple(qkv_rows))
    context_flat = context.reshape(row_count, D)
    residual = (
        flat_in + jnp.dot(context_flat, out_full, preferred_element_type=f32) + vec_values[4]
    )
    normed_two, hat_two, inv_two = norm_forward(residual, vec_values[5], vec_values[6])
    second_low = normed_two.astype(bf16)
    up_pre = jnp.einsum("nd,fd->nf", second_low, up_full, preferred_element_type=f32) + bias_full
    active, gelu_back = jax.vjp(lambda pre_act: jax.nn.gelu(pre_act, approximate=True), up_pre)
    active_low = active.astype(bf16)
    down_out = jnp.dot(active_low, down_full, preferred_element_type=f32) + vec_values[7]
    output = ((residual + down_out) * row_valid).astype(bf16).reshape(slots, BLOCK, D)

    grad_out = cotangent.reshape(row_count, D).astype(f32) * row_valid
    grad_low = grad_out.astype(bf16)

    def weight_grad(left, right):
        return jnp.einsum("nf,nd->fd", left, right, preferred_element_type=f32).astype(bf16)

    down_grad = weight_grad(active_low, grad_low)
    down_unit_grad = reduce_group(grid, down_grad.reshape(4, grid.shards, n, D))
    down_bias_grad = jnp.sum(grad_out, axis=0)
    active_grad = jnp.einsum("nd,fd->nf", grad_low, down_full, preferred_element_type=f32)
    up_low = gelu_back(active_grad)[0].astype(bf16)
    up_grad = weight_grad(up_low, second_low)
    up_unit_grad = reduce_group(grid, up_grad.reshape(4, grid.shards, n, D))
    upbias_grad = jnp.sum(up_low.astype(f32), axis=0)
    second_grad = jnp.dot(up_low, up_full, preferred_element_type=f32)
    resid_norm_grad, scale_two_grad, offset_two_grad = norm_backward(
        second_grad, hat_two, inv_two, vec_values[5]
    )
    resid_grad = grad_out + resid_norm_grad
    branch_low = resid_grad.astype(bf16)
    out_grad = weight_grad(context_flat, branch_low)
    out_bias_grad = jnp.sum(branch_low.astype(f32), axis=0)
    context_grad = jnp.einsum("ne,de->nd", branch_low, out_full, preferred_element_type=f32)
    context_grad = context_grad.astype(bf16).reshape(slots, BLOCK, HEADS, HDIM)
    rows_grad = lax.map(attend_backward, tuple(qkv_rows) + (logsum, context_grad))
    rows_grad = [part.reshape(row_count, D) for part in rows_grad]
    attn_grad = jnp.stack([weight_grad(normed_low, part) for part in rows_grad] + [out_grad])
    attn_unit_grad = reduce_group(grid, attn_grad.reshape(4, grid.shards, n, D))
    normed_grad = sum(
        jnp.einsum("ne,de->nd", rows_grad[i], qkv_full[i], preferred_element_type=f32)
        for i in range(3)
    )
    input_norm_grad, scale_one_grad, offset_one_grad = norm_backward(
        normed_grad, hat_one, inv_one, vec_values[0]
    )
    input_grad = (resid_grad + input_norm_grad).reshape(slots, BLOCK, D)
    small_grad = jnp.concatenate(
        [
            jnp.stack(
                [
                    scale_one_grad,
                    offset_one_grad,
                    jnp.sum(rows_grad[0].astype(f32), axis=0),
                    jnp.sum(rows_grad[2].astype(f32), axis=0),
                    out_bias_grad,
                    scale_two_grad,
                    offset_two_grad,
                    down_bias_grad,
                ]
            ),
            upbias_grad.reshape(4, D),
        ]
    )
    small_grad = reduce_small(grid, small_grad)
    small_own = lax.dynamic_slice_in_dim(small_grad, (2 * grid.z + grid.x) * n, n, 1)

    down_parts = share_unit(grid, down_unit_grad)
    up_parts = share_unit(grid, up_unit_grad)
    attn_parts = share_unit(grid, attn_unit_grad)
    reduced = (
        jnp.concatenate(attn_parts[:3], axis=1).astype(f32),
        attn_parts[3].astype(f32),
        jnp.concatenate(up_parts).T.astype(f32),
        jnp.concatenate(down_parts).astype(f32),
        small_own[:8],
        small_own[8:].reshape(-1),
    )
    updates = []
    for group_index in range(6):
        updates.extend(
            adam_update(
                shards[group_index],
                first_moments[group_index],
                squares[group_index],
                reduced[group_index],
                step_rates[group_index],
                decay_rates[group_index],
            )
        )
    return (output, input_grad) + tuple(updates)


def solution(mesh):
    tokens = P(("fsdp", "dp"), None, None)
    rows, columns = P("fsdp", None), P(None, "fsdp")
    state = (rows,) * 6 + (columns,) * 3 + (rows,) * 3 + (columns,) * 3 + (P("fsdp"),) * 3
    return jax.shard_map(
        per_device,
        mesh=mesh,
        in_specs=(tokens, tokens, P(("fsdp", "dp"))) + state,
        out_specs=(tokens, tokens) + state,
        check_vma=False,
    )
```

```python
import functools
import math

import jax
import jax.numpy as jnp
from jax import lax
from jax.experimental import pallas as pl
from jax.experimental.pallas import tpu as pltpu
from jax.sharding import PartitionSpec as P

D = 1088
HEADS = 17
HDIM = 64
BLOCK = 512
STEP = 10
EXTRA = 8

norm_eps = 1e-05
beta_first = 0.9
beta_second = 0.999
adam_floor = 1e-08
step_rates = (0.05, 0.2, 0.05, 0.03, 0.5, 0.3)
decay_rates = (0.1, 0.1, 0.1, 0.1, 0.0, 0.0)

AXES = ("fsdp", "dp")
VMEM_LIMIT = 56 * 1024 * 1024
f32 = jnp.float32
bf16 = jnp.bfloat16


class Grid:
    def __init__(self):
        self.shards = lax.axis_size("fsdp")
        self.replicas = lax.axis_size("dp")
        self.zs = self.shards // 2
        self.ys = self.replicas // 2
        f, r = lax.axis_index("fsdp"), lax.axis_index("dp")
        self.z, self.x = f // 2, f % 2
        self.y, self.c = r // 2, r % 2
        self.r = r

    def move(self, value, route):
        pairs = []
        for z in range(self.zs):
            for x in range(2):
                for y in range(2):
                    for c in range(2):
                        to_z, to_x, to_y, to_c = route(z, x, y, c)
                        here = (2 * z + x) * 4 + 2 * y + c
                        pairs.append((here, (2 * to_z + to_x) * 4 + 2 * to_y + to_c))
        return lax.ppermute(value, AXES, pairs)


def over_z(bit):
    return lambda z, x, y, c: (z ^ bit, x, y, c)


def over_x(z, x, y, c):
    return (z, 1 - x, y, c)


def over_y(z, x, y, c):
    return (z, x, 1 - y, c)


def over_core(z, x, y, c):
    return (z, x, y, 1 - c)


def x_then_y(z, x, y, c):
    return (z, 1 - x, y, c) if c == 0 else (z, x, 1 - y, c)


def y_then_x(z, x, y, c):
    return (z, x, 1 - y, c) if c == 0 else (z, 1 - x, y, c)


def after(value, *others):
    return lax.optimization_barrier((value,) + others)[0]


def take(value, at, axis=0):
    return lax.dynamic_index_in_dim(value, at, axis, keepdims=False)


def z_bits(zs):
    return [1 << i for i in range(zs.bit_length() - 1)]


def gather_z(grid, unit):
    held = unit[None]
    for bit in reversed(z_bits(grid.zs)):
        got = grid.move(held, over_z(bit))
        held = jnp.stack([held, got], axis=1).reshape((2 * held.shape[0],) + unit.shape)
    return held


def gather_xy(grid, held):
    got = grid.move(held, y_then_x)
    both = jnp.stack([held, got])
    return (both, grid.move(both, x_then_y))


def gather_core(grid, pieces):
    return tuple(pieces) + tuple(grid.move(p, over_core) for p in pieces)


def assemble_kernel(zs, *refs):
    pieces, (out, held, in_sems, out_sem) = refs[:4], refs[4:]
    f, r = lax.axis_index("fsdp"), lax.axis_index("dp")
    z, x, y, c = f // 2, f % 2, r // 2, r % 2
    first, second = [], []
    for number in range(4):
        dc, late = number // 2, number % 2
        core = c ^ dc
        for early in range(2):
            dx = late + core * (early - late)
            dy = early + core * (late - early)
            owner = 2 * (y ^ dy) + core
            for k in range(zs):
                place = (owner, 2 * (z ^ k) + (x ^ dx))
                sem = in_sems.at[number]
                first.append(pltpu.make_async_copy(pieces[number].at[early, k], held.at[place], sem))
                second.append(pltpu.make_async_copy(held.at[place], out.at[place], out_sem))
    for copy in first:
        copy.start()
    each = len(first) // 4
    for number in range(4):
        for copy in first[number * each : (number + 1) * each]:
            copy.wait()
        for copy in second[number * each : (number + 1) * each]:
            copy.start()
    for copy in second:
        copy.wait()


def assemble(grid, pieces, rows):
    whole = (4, grid.shards, rows, D)
    return pl.pallas_call(
        functools.partial(assemble_kernel, grid.zs),
        out_shape=jax.ShapeDtypeStruct(whole, bf16),
        in_specs=[pl.BlockSpec(memory_space=pl.ANY)] * 4,
        out_specs=pl.BlockSpec(memory_space=pl.ANY),
        scratch_shapes=[
            pltpu.VMEM(whole, bf16),
            pltpu.SemaphoreType.DMA((4,)),
            pltpu.SemaphoreType.DMA(()),
        ],
        compiler_params=pltpu.CompilerParams(vmem_limit_bytes=VMEM_LIMIT),
        cost_estimate=pl.CostEstimate(flops=0, bytes_accessed=20_000_000, transcendentals=0),
        name="assemble",
    )(*pieces)


def add(first, second):
    return (first.astype(f32) + second.astype(f32)).astype(bf16)


def reduce_group(grid, grads):
    n = grads.shape[2]
    zs = grid.zs
    view = grads.reshape(2, 2, zs, 2, n, D)
    x, y, first = grid.x, grid.y, grid.c == 0
    got = grid.move(take(view, 1 - grid.c, 1), over_core)
    total = add(take(view, grid.c, 1), got)
    got = grid.move(jnp.where(first, take(total, 1 - x, 2), take(total, 1 - y, 0).swapaxes(0, 1)), x_then_y)
    total = add(jnp.where(first, take(total, x, 2), take(total, y, 0).swapaxes(0, 1)), got)
    at = jnp.where(first, y, x)
    got = grid.move(take(total, 1 - at), y_then_x)
    total = add(take(total, at), got)
    for bit in z_bits(zs):
        at = (grid.z // bit) % 2
        total = total.reshape(-1, 2, n, D)
        got = grid.move(take(total, 1 - at, 1), over_z(bit))
        total = add(take(total, at, 1), got)
    return total[0]


def share_unit(grid, unit):
    pair = jnp.stack([unit, grid.move(unit, over_y)])
    both = jnp.stack([pair, grid.move(pair, over_core)], axis=1).reshape((4,) + unit.shape)
    return [take(both, jnp.bitwise_xor(grid.r, r)) for r in range(4)]


def reduce_small(grid, value):
    for route in [over_core, over_y, over_x] + [over_z(bit) for bit in z_bits(grid.zs)]:
        value = value + grid.move(value, route)
    return value


def norm_forward(values, scales, offset):
    center = values - jnp.mean(values, axis=-1, keepdims=True)
    inverse = lax.rsqrt(jnp.mean(center * center, axis=-1, keepdims=True) + norm_eps)
    norm_hat = center * inverse
    return (norm_hat * scales + offset, norm_hat, inverse)


def norm_backward(gradient, norm_hat, inverse, scales):
    hat_grad = gradient * scales
    value_grad = inverse * (
        hat_grad
        - jnp.mean(hat_grad, axis=-1, keepdims=True)
        - norm_hat * jnp.mean(hat_grad * norm_hat, axis=-1, keepdims=True)
    )
    return (value_grad, jnp.sum(gradient * norm_hat, axis=0), jnp.sum(gradient, axis=0))


def head_masks(rows):
    lane = lax.broadcasted_iota(jnp.int32, (rows, 128), 1)
    return (lane < HDIM, lane >= HDIM)


def dot_over(left, right, left_at, right_at):
    return lax.dot_general(
        left, right, (((left_at,), (right_at,)), ((), ())), preferred_element_type=f32
    )


def score_tile(keys, queries, tile, size):
    scores = dot_over(keys, queries, 1, 1)
    rows_at = lax.broadcasted_iota(jnp.int32, scores.shape, 0)
    cols_at = lax.broadcasted_iota(jnp.int32, scores.shape, 1) + tile * size
    return jnp.where(rows_at <= cols_at, scores, -1e30)


def attend_kernel(q_ref, k_ref, v_ref, c_ref, lse_ref):
    size = 256
    masks = head_masks(BLOCK)

    def slab(at, width, heads, first):
        columns = pl.ds(at, width)
        values = v_ref[:, columns]
        parts = []
        for h in range(heads):
            parts.append(jnp.where(masks[h], values, 0) if heads > 1 else values)
        for tile in range(BLOCK // size):
            extent = (tile + 1) * size
            keys = k_ref[pl.ds(0, extent), columns]
            queries = q_ref[pl.ds(tile * size, size), columns] * 0.125
            total = None
            for h in range(heads):
                mine = jnp.where(masks[h][:size], queries, 0) if heads > 1 else queries
                scores = score_tile(keys, mine, tile, size)
                top = jnp.max(scores, axis=0, keepdims=True)
                powers = jnp.exp(scores - top)
                norm = jnp.sum(powers, axis=0, keepdims=True)
                probs = (powers * (1.0 / norm)).astype(bf16)
                lse_ref[first + h, :, pl.ds(tile * size, size)] = top + jnp.log(norm)
                piece = dot_over(probs, parts[h][:extent], 0, 0)
                total = piece if total is None else total + piece
            c_ref[pl.ds(tile * size, size), columns] = total.astype(bf16)

    def pair(i, _):
        slab(pl.multiple_of(i * 128, 128), 128, 2, 2 * i)
        return 0

    lax.fori_loop(0, HEADS // 2, pair, 0)
    slab((HEADS - 1) * HDIM, HDIM, 1, HEADS - 1)


def attend_back_kernel(q_ref, k_ref, v_ref, lse_ref, dc_ref, dq_ref, dk_ref, dv_ref):
    size = 256
    masks = head_masks(BLOCK)

    def slab(at, width, heads, first):
        columns = pl.ds(at, width)
        keys_all = k_ref[:, columns]
        key_parts = [jnp.where(masks[h], keys_all, 0) if heads > 1 else keys_all for h in range(heads)]
        dk_total, dv_total = None, None
        for tile in reversed(range(BLOCK // size)):
            extent = (tile + 1) * size
            keys = keys_all[:extent]
            values = v_ref[pl.ds(0, extent), columns]
            queries = q_ref[pl.ds(tile * size, size), columns] * 0.125
            grads = dc_ref[pl.ds(tile * size, size), columns]
            dq_total, dk_tile, dv_tile = None, None, None
            for h in range(heads):
                my_q = jnp.where(masks[h][:size], queries, 0) if heads > 1 else queries
                my_g = jnp.where(masks[h][:size], grads, 0) if heads > 1 else grads
                scores = score_tile(keys, my_q, tile, size)
                probs = jnp.exp(scores - lse_ref[first + h, :, pl.ds(tile * size, size)])
                prob_grad = dot_over(values, my_g, 1, 1)
                inner = jnp.sum(probs * prob_grad, axis=0, keepdims=True)
                score_grad = (probs * (prob_grad - inner)).astype(bf16)
                dv = dot_over(probs.astype(bf16), my_g, 1, 0)
                dk = dot_over(score_grad, my_q, 1, 0)
                dq = dot_over(score_grad, key_parts[h][:extent], 0, 0)
                dv_tile = dv if dv_tile is None else dv_tile + dv
                dk_tile = dk if dk_tile is None else dk_tile + dk
                dq_total = dq if dq_total is None else dq_total + dq
            dq_ref[pl.ds(tile * size, size), columns] = (dq_total * 0.125).astype(bf16)
            if dk_total is None:
                dk_total, dv_total = dk_tile, dv_tile
            else:
                dk_total = jnp.concatenate([dk_total[:extent] + dk_tile, dk_total[extent:]])
                dv_total = jnp.concatenate([dv_total[:extent] + dv_tile, dv_total[extent:]])
        dk_ref[:, columns] = dk_total.astype(bf16)
        dv_ref[:, columns] = dv_total.astype(bf16)

    def pair(i, _):
        slab(pl.multiple_of(i * 128, 128), 128, 2, 2 * i)
        return 0

    lax.fori_loop(0, HEADS // 2, pair, 0)
    slab((HEADS - 1) * HDIM, HDIM, 1, HEADS - 1)


def attend(queries, keys, values):
    rows = queries.shape[0]
    block = pl.BlockSpec((BLOCK, D), lambda i: (i, 0))
    lse = pl.BlockSpec((HEADS, 1, BLOCK), lambda i: (0, 0, i))
    return pl.pallas_call(
        attend_kernel,
        grid=(rows // BLOCK,),
        in_specs=[block] * 3,
        out_specs=[block, lse],
        out_shape=[
            jax.ShapeDtypeStruct((rows, D), bf16),
            jax.ShapeDtypeStruct((HEADS, 1, rows), f32),
        ],
        compiler_params=pltpu.CompilerParams(vmem_limit_bytes=VMEM_LIMIT),
        cost_estimate=pl.CostEstimate(flops=25_000_000_000, bytes_accessed=9_000_000, transcendentals=0),
        name="attend",
    )(queries, keys, values)


def attend_back(queries, keys, values, lse, context_grad):
    rows = queries.shape[0]
    block = pl.BlockSpec((BLOCK, D), lambda i: (i, 0))
    lse_block = pl.BlockSpec((HEADS, 1, BLOCK), lambda i: (0, 0, i))
    return pl.pallas_call(
        attend_back_kernel,
        grid=(rows // BLOCK,),
        in_specs=[block] * 3 + [lse_block, block],
        out_specs=[block] * 3,
        out_shape=[jax.ShapeDtypeStruct((rows, D), bf16)] * 3,
        compiler_params=pltpu.CompilerParams(vmem_limit_bytes=VMEM_LIMIT),
        cost_estimate=pl.CostEstimate(flops=45_000_000_000, bytes_accessed=16_000_000, transcendentals=0),
        name="attend_back",
    )(queries, keys, values, lse, context_grad)


def adam_update(weight, mean_old, square_old, gradient, step_rate, decay_rate):
    mean_new = beta_first * mean_old + (1.0 - beta_first) * gradient
    square_new = beta_second * square_old + (1.0 - beta_second) * gradient * gradient
    mean_hat = mean_new / (1.0 - beta_first**STEP)
    square_hat = square_new / (1.0 - beta_second**STEP)
    weight_new = weight - step_rate * (
        mean_hat / (jnp.sqrt(square_hat) + adam_floor) + decay_rate * weight
    )
    return (weight_new, mean_new, square_new)


def per_device(
    hidden_in,
    cotangent,
    lengths,
    qkv_weight,
    qkv_mean,
    qkv_square,
    out_weight,
    out_mean,
    out_square,
    up_weight,
    up_mean,
    up_square,
    down_weight,
    down_mean,
    down_square,
    vectors,
    vectors_mean,
    vectors_square,
    upbias,
    upbias_mean,
    upbias_square,
):
    shards = (qkv_weight, out_weight, up_weight, down_weight, vectors, upbias)
    first_moments = (qkv_mean, out_mean, up_mean, down_mean, vectors_mean, upbias_mean)
    squares = (qkv_square, out_square, up_square, down_square, vectors_square, upbias_square)
    grid = Grid()
    n = D // grid.shards
    slots = hidden_in.shape[0]
    row_count = slots * BLOCK
    ff = 4 * D

    attn_units = jnp.stack(
        [qkv_weight[:, :D], qkv_weight[:, D : 2 * D], qkv_weight[:, 2 * D :], out_weight]
    )
    attn_unit = take(attn_units, grid.r).astype(bf16)
    small = jnp.concatenate([vectors.reshape(-1), upbias]).astype(bf16)
    small = jnp.pad(small, (0, EXTRA * D - small.shape[0])).reshape(EXTRA, D)
    up_unit = lax.dynamic_slice_in_dim(up_weight, grid.r * n, n, 1).astype(bf16).T
    down_unit = lax.dynamic_slice_in_dim(down_weight, grid.r * n, n, 0).astype(bf16)

    small_z = gather_z(grid, small)
    attn_z = gather_z(grid, attn_unit)
    up_z = gather_z(grid, after(up_unit, attn_z))
    down_z = gather_z(grid, after(down_unit, up_z))
    attn_xy = gather_xy(grid, attn_z)
    attn_pieces = gather_core(grid, attn_xy)
    up_xy = gather_xy(grid, after(up_z, *attn_xy))
    up_pieces = gather_core(grid, up_xy)
    down_xy = gather_xy(grid, after(down_z, *up_xy))
    down_pieces = gather_core(grid, down_xy)
    attn_full = assemble(grid, attn_pieces, n)
    up_full = assemble(grid, up_pieces, n).reshape(ff, D)
    down_full = assemble(grid, down_pieces, n).reshape(ff, D)

    own = small_z.reshape(grid.zs, EXTRA * D)[:, : 12 * n]
    pair = jnp.stack([own, grid.move(own, over_x)])
    pair = jnp.stack([take(pair, grid.x), take(pair, 1 - grid.x)])
    order = jnp.bitwise_xor(grid.z, jnp.arange(grid.zs))
    pair = pair[:, order]
    smalls = pair.transpose(1, 0, 2).reshape(grid.shards, 12 * n)
    vec_values = (
        smalls[:, : 8 * n].reshape(grid.shards, 8, n).transpose(1, 0, 2).reshape(8, D).astype(f32)
    )
    bias_full = (
        smalls[:, 8 * n :].reshape(grid.shards, 4, n).transpose(1, 0, 2).reshape(ff).astype(f32)
    )

    attn_full = attn_full.reshape(4, D, D)
    qkv_full, out_full = attn_full[:3], attn_full[3]

    flat_in = hidden_in.reshape(row_count, D).astype(f32)
    positions = jnp.arange(BLOCK, dtype=jnp.int32)
    row_valid = (positions[None, :] < lengths[:, None]).astype(f32).reshape(row_count, 1)
    normed_one, hat_one, inv_one = norm_forward(flat_in, vec_values[0], vec_values[1])
    normed_low = normed_one.astype(bf16)
    bias_rows = jnp.stack([vec_values[2], jnp.zeros((D,), f32), vec_values[3]])
    qkv_rows = [
        (
            jnp.dot(normed_low, qkv_full[i], preferred_element_type=f32) + bias_rows[i]
        ).astype(bf16)
        for i in range(3)
    ]
    context_flat, logsum = attend(*qkv_rows)
    residual = (
        flat_in + jnp.dot(context_flat, out_full, preferred_element_type=f32) + vec_values[4]
    )
    normed_two, hat_two, inv_two = norm_forward(residual, vec_values[5], vec_values[6])
    second_low = normed_two.astype(bf16)
    up_pre = jnp.einsum("nd,fd->nf", second_low, up_full, preferred_element_type=f32) + bias_full
    active, gelu_back = jax.vjp(lambda pre_act: jax.nn.gelu(pre_act, approximate=True), up_pre)
    active_low = active.astype(bf16)
    down_out = jnp.dot(active_low, down_full, preferred_element_type=f32) + vec_values[7]
    output = ((residual + down_out) * row_valid).astype(bf16).reshape(slots, BLOCK, D)

    grad_out = cotangent.reshape(row_count, D).astype(f32) * row_valid
    grad_low = grad_out.astype(bf16)

    def weight_grad(left, right):
        return jnp.einsum("nf,nd->fd", left, right, preferred_element_type=f32).astype(bf16)

    down_grad = weight_grad(active_low, grad_low)
    down_unit_grad = reduce_group(grid, down_grad.reshape(4, grid.shards, n, D))
    down_bias_grad = jnp.sum(grad_out, axis=0)
    active_grad = jnp.einsum("nd,fd->nf", grad_low, down_full, preferred_element_type=f32)
    up_low = gelu_back(active_grad)[0].astype(bf16)
    up_grad = weight_grad(up_low, second_low)
    up_unit_grad = reduce_group(grid, up_grad.reshape(4, grid.shards, n, D))
    upbias_grad = jnp.sum(up_low.astype(f32), axis=0)
    second_grad = jnp.dot(up_low, up_full, preferred_element_type=f32)
    resid_norm_grad, scale_two_grad, offset_two_grad = norm_backward(
        second_grad, hat_two, inv_two, vec_values[5]
    )
    resid_grad = grad_out + resid_norm_grad
    branch_low = resid_grad.astype(bf16)
    out_grad = weight_grad(context_flat, branch_low)
    out_bias_grad = jnp.sum(branch_low.astype(f32), axis=0)
    context_grad = jnp.einsum("ne,de->nd", branch_low, out_full, preferred_element_type=f32)
    rows_grad = attend_back(*qkv_rows, logsum, context_grad.astype(bf16))
    attn_grad = jnp.stack([weight_grad(normed_low, part) for part in rows_grad] + [out_grad])
    attn_unit_grad = reduce_group(grid, attn_grad.reshape(4, grid.shards, n, D))
    normed_grad = sum(
        jnp.einsum("ne,de->nd", rows_grad[i], qkv_full[i], preferred_element_type=f32)
        for i in range(3)
    )
    input_norm_grad, scale_one_grad, offset_one_grad = norm_backward(
        normed_grad, hat_one, inv_one, vec_values[0]
    )
    input_grad = (resid_grad + input_norm_grad).reshape(slots, BLOCK, D)
    small_grad = jnp.concatenate(
        [
            jnp.stack(
                [
                    scale_one_grad,
                    offset_one_grad,
                    jnp.sum(rows_grad[0].astype(f32), axis=0),
                    jnp.sum(rows_grad[2].astype(f32), axis=0),
                    out_bias_grad,
                    scale_two_grad,
                    offset_two_grad,
                    down_bias_grad,
                ]
            ),
            upbias_grad.reshape(4, D),
        ]
    )
    small_grad = reduce_small(grid, small_grad)
    small_own = lax.dynamic_slice_in_dim(small_grad, (2 * grid.z + grid.x) * n, n, 1)

    down_parts = share_unit(grid, down_unit_grad)
    up_parts = share_unit(grid, up_unit_grad)
    attn_parts = share_unit(grid, attn_unit_grad)
    reduced = (
        jnp.concatenate(attn_parts[:3], axis=1).astype(f32),
        attn_parts[3].astype(f32),
        jnp.concatenate(up_parts).T.astype(f32),
        jnp.concatenate(down_parts).astype(f32),
        small_own[:8],
        small_own[8:].reshape(-1),
    )
    updates = []
    for group_index in range(6):
        updates.extend(
            adam_update(
                shards[group_index],
                first_moments[group_index],
                squares[group_index],
                reduced[group_index],
                step_rates[group_index],
                decay_rates[group_index],
            )
        )
    return (output, input_grad) + tuple(updates)


def solution(mesh):
    tokens = P(("fsdp", "dp"), None, None)
    rows, columns = P("fsdp", None), P(None, "fsdp")
    state = (rows,) * 6 + (columns,) * 3 + (rows,) * 3 + (columns,) * 3 + (P("fsdp"),) * 3
    return jax.shard_map(
        per_device,
        mesh=mesh,
        in_specs=(tokens, tokens, P(("fsdp", "dp"))) + state,
        out_specs=(tokens, tokens) + state,
        check_vma=False,
    )
```

```python
import functools
import math

import jax
import jax.numpy as jnp
from jax import lax
from jax.experimental import pallas as pl
from jax.experimental.pallas import tpu as pltpu
from jax.sharding import PartitionSpec as P

D = 1088
HEADS = 17
HDIM = 64
BLOCK = 512
STEP = 10
EXTRA = 8

norm_eps = 1e-05
beta_first = 0.9
beta_second = 0.999
adam_floor = 1e-08
step_rates = (0.05, 0.2, 0.05, 0.03, 0.5, 0.3)
decay_rates = (0.1, 0.1, 0.1, 0.1, 0.0, 0.0)

AXES = ("fsdp", "dp")
VMEM_LIMIT = 56 * 1024 * 1024
f32 = jnp.float32
bf16 = jnp.bfloat16


class Grid:
    def __init__(self):
        self.shards = lax.axis_size("fsdp")
        self.replicas = lax.axis_size("dp")
        self.zs = self.shards // 2
        self.ys = self.replicas // 2
        f, r = lax.axis_index("fsdp"), lax.axis_index("dp")
        self.z, self.x = f // 2, f % 2
        self.y, self.c = r // 2, r % 2
        self.r = r

    def move(self, value, route):
        pairs = []
        for z in range(self.zs):
            for x in range(2):
                for y in range(2):
                    for c in range(2):
                        to_z, to_x, to_y, to_c = route(z, x, y, c)
                        here = (2 * z + x) * 4 + 2 * y + c
                        pairs.append((here, (2 * to_z + to_x) * 4 + 2 * to_y + to_c))
        return lax.ppermute(value, AXES, pairs)


def over_z(bit):
    return lambda z, x, y, c: (z ^ bit, x, y, c)


def over_x(z, x, y, c):
    return (z, 1 - x, y, c)


def over_y(z, x, y, c):
    return (z, x, 1 - y, c)


def over_core(z, x, y, c):
    return (z, x, y, 1 - c)


def x_then_y(z, x, y, c):
    return (z, 1 - x, y, c) if c == 0 else (z, x, 1 - y, c)


def y_then_x(z, x, y, c):
    return (z, x, 1 - y, c) if c == 0 else (z, 1 - x, y, c)


def after(value, *others):
    return lax.optimization_barrier((value,) + others)[0]


def take(value, at, axis=0):
    return lax.dynamic_index_in_dim(value, at, axis, keepdims=False)


def z_bits(zs):
    return [1 << i for i in range(zs.bit_length() - 1)]


def gather_z(grid, unit):
    held, off = unit[None], [0]
    for bit in reversed(z_bits(grid.zs)[1:]):
        held = jnp.concatenate([held, grid.move(held, over_z(bit))])
        off = off + [z ^ bit for z in off]
    return [held, grid.move(held, over_z(1))], [off, [z ^ 1 for z in off]]


def gather_xy(grid, held):
    both = jnp.stack([held, grid.move(held, y_then_x)])
    return [both, grid.move(both, x_then_y)]


def gather_rest(grid, halves):
    pieces = [p for held in halves for p in gather_xy(grid, held)]
    return pieces, pieces + [grid.move(p, over_core) for p in pieces]


def assemble_kernel(zs, offs, *refs):
    count = 4 * len(offs)
    pieces, (out, held, in_sems, out_sem) = refs[:count], refs[count:]
    f, r = lax.axis_index("fsdp"), lax.axis_index("dp")
    z, x, y, c = f // 2, f % 2, r // 2, r % 2
    first, second = [], []
    for number in range(count):
        dc, late = number // (count // 2), number % 2
        off = offs[(number // 2) % len(offs)]
        core = c ^ dc
        for early in range(2):
            dx = late + core * (early - late)
            dy = early + core * (late - early)
            owner = 2 * (y ^ dy) + core
            for k in range(len(off)):
                place = (owner, 2 * (z ^ off[k]) + (x ^ dx))
                sem = in_sems.at[number]
                first.append(pltpu.make_async_copy(pieces[number].at[early, k], held.at[place], sem))
                second.append(pltpu.make_async_copy(held.at[place], out.at[place], out_sem))
    for copy in first:
        copy.start()
    each = len(first) // count
    for number in range(count):
        for copy in first[number * each : (number + 1) * each]:
            copy.wait()
        for copy in second[number * each : (number + 1) * each]:
            copy.start()
    for copy in second:
        copy.wait()


def assemble(grid, pieces, offs, rows):
    whole = (4, grid.shards, rows, D)
    return pl.pallas_call(
        functools.partial(assemble_kernel, grid.zs, offs),
        out_shape=jax.ShapeDtypeStruct(whole, bf16),
        in_specs=[pl.BlockSpec(memory_space=pl.ANY)] * len(pieces),
        out_specs=pl.BlockSpec(memory_space=pl.ANY),
        scratch_shapes=[
            pltpu.VMEM(whole, bf16),
            pltpu.SemaphoreType.DMA((len(pieces),)),
            pltpu.SemaphoreType.DMA(()),
        ],
        compiler_params=pltpu.CompilerParams(vmem_limit_bytes=VMEM_LIMIT),
        cost_estimate=pl.CostEstimate(flops=0, bytes_accessed=20_000_000, transcendentals=0),
        name="assemble",
    )(*pieces)


def add(first, second):
    return (first.astype(f32) + second.astype(f32)).astype(bf16)


class Reduction:
    def __init__(self, grid, theirs, mine):
        self.grid, self.n = grid, mine.shape[2]
        self.stage = 0
        self.bits = z_bits(grid.zs)
        self.keep, self.sent = mine, theirs
        self.route = over_core

    def step(self):
        grid, n = self.grid, self.n
        total = add(self.keep, grid.move(self.sent, self.route))
        first = grid.c == 0
        x, y = grid.x, grid.y
        if self.stage == 0:
            total = total.reshape(2, grid.zs, 2, n, D)
            self.sent = jnp.where(first, take(total, 1 - x, 2), take(total, 1 - y, 0).swapaxes(0, 1))
            self.keep = jnp.where(first, take(total, x, 2), take(total, y, 0).swapaxes(0, 1))
            self.route = x_then_y
        elif self.stage == 1:
            at = jnp.where(first, y, x)
            self.sent, self.keep = take(total, 1 - at), take(total, at)
            self.route = y_then_x
        elif self.stage - 2 < len(self.bits):
            bit = self.bits[self.stage - 2]
            at = (grid.z // bit) % 2
            total = total.reshape(-1, 2, n, D)
            self.sent, self.keep = take(total, 1 - at, 1), take(total, at, 1)
            self.route = over_z(bit)
        else:
            return total[0]
        self.stage += 1
        return self.sent

    def finish(self):
        while self.stage - 2 < len(self.bits):
            self.step()
        return self.step()


def reduce_rows(grid, grads, n):
    view = grads.reshape(2, 2, grid.shards, n, D)
    return Reduction(grid, take(view, 1 - grid.c, 1), take(view, grid.c, 1))


def share_unit(grid, unit):
    pair = jnp.stack([unit, grid.move(unit, over_y)])
    both = jnp.stack([pair, grid.move(pair, over_core)], axis=1).reshape((4,) + unit.shape)
    return [take(both, jnp.bitwise_xor(grid.r, r)) for r in range(4)]


def reduce_small(grid, value):
    for route in [over_core, over_y, over_x] + [over_z(bit) for bit in z_bits(grid.zs)]:
        value = value + grid.move(value, route)
    return value


def norm_forward(values, scales, offset):
    center = values - jnp.mean(values, axis=-1, keepdims=True)
    inverse = lax.rsqrt(jnp.mean(center * center, axis=-1, keepdims=True) + norm_eps)
    norm_hat = center * inverse
    return (norm_hat * scales + offset, norm_hat, inverse)


def norm_backward(gradient, norm_hat, inverse, scales):
    hat_grad = gradient * scales
    value_grad = inverse * (
        hat_grad
        - jnp.mean(hat_grad, axis=-1, keepdims=True)
        - norm_hat * jnp.mean(hat_grad * norm_hat, axis=-1, keepdims=True)
    )
    return (value_grad, jnp.sum(gradient * norm_hat, axis=0), jnp.sum(gradient, axis=0))


def head_masks(rows):
    lane = lax.broadcasted_iota(jnp.int32, (rows, 128), 1)
    return (lane < HDIM, lane >= HDIM)


def dot_over(left, right, left_at, right_at):
    return lax.dot_general(
        left, right, (((left_at,), (right_at,)), ((), ())), preferred_element_type=f32
    )


def score_tile(keys, queries, tile, size):
    scores = dot_over(keys, queries, 1, 1)
    rows_at = lax.broadcasted_iota(jnp.int32, scores.shape, 0)
    cols_at = lax.broadcasted_iota(jnp.int32, scores.shape, 1) + tile * size
    return jnp.where(rows_at <= cols_at, scores, -1e30)


def attend_kernel(q_ref, k_ref, v_ref, c_ref, lse_ref):
    size = 256
    masks = head_masks(BLOCK)

    def slab(at, width, heads, first):
        columns = pl.ds(at, width)
        values = v_ref[:, columns]
        parts = []
        for h in range(heads):
            parts.append(jnp.where(masks[h], values, 0) if heads > 1 else values)
        for tile in range(BLOCK // size):
            extent = (tile + 1) * size
            keys = k_ref[pl.ds(0, extent), columns]
            queries = q_ref[pl.ds(tile * size, size), columns] * 0.125
            total = None
            for h in range(heads):
                mine = jnp.where(masks[h][:size], queries, 0) if heads > 1 else queries
                scores = score_tile(keys, mine, tile, size)
                top = jnp.max(scores, axis=0, keepdims=True)
                powers = jnp.exp(scores - top)
                norm = jnp.sum(powers, axis=0, keepdims=True)
                probs = (powers * (1.0 / norm)).astype(bf16)
                lse_ref[first + h, :, pl.ds(tile * size, size)] = top + jnp.log(norm)
                piece = dot_over(probs, parts[h][:extent], 0, 0)
                total = piece if total is None else total + piece
            c_ref[pl.ds(tile * size, size), columns] = total.astype(bf16)

    def pair(i, _):
        slab(pl.multiple_of(i * 128, 128), 128, 2, 2 * i)
        return 0

    lax.fori_loop(0, HEADS // 2, pair, 0)
    slab((HEADS - 1) * HDIM, HDIM, 1, HEADS - 1)


def attend_back_kernel(q_ref, k_ref, v_ref, lse_ref, dc_ref, dq_ref, dk_ref, dv_ref):
    size = 256
    masks = head_masks(BLOCK)

    def slab(at, width, heads, first):
        columns = pl.ds(at, width)
        keys_all = k_ref[:, columns]
        key_parts = [jnp.where(masks[h], keys_all, 0) if heads > 1 else keys_all for h in range(heads)]
        dk_total, dv_total = None, None
        for tile in reversed(range(BLOCK // size)):
            extent = (tile + 1) * size
            keys = keys_all[:extent]
            values = v_ref[pl.ds(0, extent), columns]
            queries = q_ref[pl.ds(tile * size, size), columns] * 0.125
            grads = dc_ref[pl.ds(tile * size, size), columns]
            dq_total, dk_tile, dv_tile = None, None, None
            for h in range(heads):
                my_q = jnp.where(masks[h][:size], queries, 0) if heads > 1 else queries
                my_g = jnp.where(masks[h][:size], grads, 0) if heads > 1 else grads
                scores = score_tile(keys, my_q, tile, size)
                probs = jnp.exp(scores - lse_ref[first + h, :, pl.ds(tile * size, size)])
                prob_grad = dot_over(values, my_g, 1, 1)
                inner = jnp.sum(probs * prob_grad, axis=0, keepdims=True)
                score_grad = (probs * (prob_grad - inner)).astype(bf16)
                dv = dot_over(probs.astype(bf16), my_g, 1, 0)
                dk = dot_over(score_grad, my_q, 1, 0)
                dq = dot_over(score_grad, key_parts[h][:extent], 0, 0)
                dv_tile = dv if dv_tile is None else dv_tile + dv
                dk_tile = dk if dk_tile is None else dk_tile + dk
                dq_total = dq if dq_total is None else dq_total + dq
            dq_ref[pl.ds(tile * size, size), columns] = (dq_total * 0.125).astype(bf16)
            if dk_total is None:
                dk_total, dv_total = dk_tile, dv_tile
            else:
                dk_total = jnp.concatenate([dk_total[:extent] + dk_tile, dk_total[extent:]])
                dv_total = jnp.concatenate([dv_total[:extent] + dv_tile, dv_total[extent:]])
        dk_ref[:, columns] = dk_total.astype(bf16)
        dv_ref[:, columns] = dv_total.astype(bf16)

    def pair(i, _):
        slab(pl.multiple_of(i * 128, 128), 128, 2, 2 * i)
        return 0

    lax.fori_loop(0, HEADS // 2, pair, 0)
    slab((HEADS - 1) * HDIM, HDIM, 1, HEADS - 1)


def attend(queries, keys, values):
    rows = queries.shape[0]
    block = pl.BlockSpec((BLOCK, D), lambda i: (i, 0))
    lse = pl.BlockSpec((HEADS, 1, BLOCK), lambda i: (0, 0, i))
    return pl.pallas_call(
        attend_kernel,
        grid=(rows // BLOCK,),
        in_specs=[block] * 3,
        out_specs=[block, lse],
        out_shape=[
            jax.ShapeDtypeStruct((rows, D), bf16),
            jax.ShapeDtypeStruct((HEADS, 1, rows), f32),
        ],
        compiler_params=pltpu.CompilerParams(vmem_limit_bytes=VMEM_LIMIT),
        cost_estimate=pl.CostEstimate(flops=14_000_000_000, bytes_accessed=9_000_000, transcendentals=0),
        name="attend",
    )(queries, keys, values)


def attend_back(queries, keys, values, lse, context_grad, ties=()):
    rows = queries.shape[0]
    block = pl.BlockSpec((BLOCK, D), lambda i: (i, 0))
    lse_block = pl.BlockSpec((HEADS, 1, BLOCK), lambda i: (0, 0, i))
    return call(
        attend_back_kernel,
        "attend_back",
        18_000_000_000,
        (queries, keys, values, lse, context_grad),
        ties,
        grid=(rows // BLOCK,),
        in_specs=[block] * 3 + [lse_block, block],
        out_specs=[block] * 3,
        out_shape=[jax.ShapeDtypeStruct((rows, D), bf16)] * 3,
    )


def call(kernel, name, flops, operands, ties=(), in_specs=(), **kw):
    count = len(operands)

    def body(*refs):
        kernel(*refs[:count], *refs[count + len(ties) :])

    return pl.pallas_call(
        body,
        in_specs=list(in_specs) + [pl.BlockSpec(memory_space=pl.ANY)] * len(ties),
        compiler_params=pltpu.CompilerParams(vmem_limit_bytes=VMEM_LIMIT),
        cost_estimate=pl.CostEstimate(flops=flops, bytes_accessed=20_000_000, transcendentals=0),
        name=name,
        **kw,
    )(*operands, *ties)


def weight_grad_kernel(left_ref, right_ref, out_ref):
    out_ref[...] = dot_over(left_ref[...], right_ref[...], 0, 0).astype(bf16)


def weight_grad(left, right, ties=()):
    rows, wide = left.shape
    tile = 512
    return call(
        weight_grad_kernel,
        "weight_grad",
        2 * rows * wide * D,
        (left, right),
        ties,
        grid=(pl.cdiv(wide, tile),),
        in_specs=[
            pl.BlockSpec((rows, tile), lambda i: (0, i)),
            pl.BlockSpec((rows, D), lambda i: (0, 0)),
        ],
        out_specs=pl.BlockSpec((tile, D), lambda i: (i, 0)),
        out_shape=jax.ShapeDtypeStruct((wide, D), bf16),
    )


def up_kernel(second_ref, up_ref, bias_ref, active_ref, slope_ref):
    pre = dot_over(second_ref[...], up_ref[...], 1, 1) + bias_ref[...]
    root = math.sqrt(2.0 / math.pi)
    square = pre * pre
    curve = jnp.tanh(pre * (root + (root * 0.044715) * square))
    half = 0.5 + 0.5 * curve
    active_ref[...] = (pre * half).astype(bf16)
    inner = root + (3.0 * root * 0.044715) * square
    slope_ref[...] = (half + (0.5 * pre) * (1.0 - curve * curve) * inner).astype(bf16)


def up_forward(second, up_full, bias, ties=()):
    rows, ff = second.shape[0], up_full.shape[0]
    tile = 512
    columns = pl.BlockSpec((rows, tile), lambda i: (0, i))
    return call(
        up_kernel,
        "up_forward",
        2 * rows * ff * D,
        (second, up_full, bias.reshape(1, ff)),
        ties,
        grid=(pl.cdiv(ff, tile),),
        in_specs=[
            pl.BlockSpec((rows, D), lambda i: (0, 0)),
            pl.BlockSpec((tile, D), lambda i: (i, 0)),
            pl.BlockSpec((1, tile), lambda i: (0, i)),
        ],
        out_specs=[columns, columns],
        out_shape=[jax.ShapeDtypeStruct((rows, ff), bf16)] * 2,
    )


def active_back_kernel(grad_ref, down_ref, slope_ref, out_ref, sum_ref):
    active_grad = dot_over(grad_ref[...], down_ref[...], 1, 1)
    low = (active_grad * slope_ref[...].astype(f32)).astype(bf16)
    out_ref[...] = low
    sum_ref[...] = jnp.sum(low.astype(f32), axis=0, keepdims=True)


def active_back(grad_low, down_full, slope, ties=()):
    rows, ff = slope.shape
    tile = 512
    columns = pl.BlockSpec((rows, tile), lambda i: (0, i))
    return call(
        active_back_kernel,
        "active_back",
        2 * rows * ff * D,
        (grad_low, down_full, slope),
        ties,
        grid=(pl.cdiv(ff, tile),),
        in_specs=[
            pl.BlockSpec((rows, D), lambda i: (0, 0)),
            pl.BlockSpec((tile, D), lambda i: (i, 0)),
            columns,
        ],
        out_specs=[columns, pl.BlockSpec((1, tile), lambda i: (0, i))],
        out_shape=[
            jax.ShapeDtypeStruct((rows, ff), bf16),
            jax.ShapeDtypeStruct((1, ff), f32),
        ],
    )


def row_mean(value):
    return jnp.sum(value, axis=-1, keepdims=True) * (1.0 / D)


def norm_back_rows(base, gradient, scales):
    center = base - row_mean(base)
    inverse = lax.rsqrt(row_mean(center * center) + norm_eps)
    hat = center * inverse
    scaled = gradient * scales
    back = inverse * (scaled - row_mean(scaled) - hat * row_mean(scaled * hat))
    return back, gradient * hat


def up_back_kernel(up_low_ref, up_ref, residual_ref, grad_ref, scale_ref, out_ref, low_ref, sums_ref):
    second_grad = dot_over(up_low_ref[...], up_ref[...], 1, 0)
    back, with_hat = norm_back_rows(residual_ref[...], second_grad, scale_ref[...])
    total = grad_ref[...].astype(f32) + back
    low = total.astype(bf16)
    out_ref[...] = total
    low_ref[...] = low

    @pl.when(pl.program_id(0) == 0)
    def _():
        sums_ref[...] = jnp.zeros_like(sums_ref)

    for at, value in enumerate([with_hat, second_grad, low.astype(f32)]):
        sums_ref[pl.ds(at, 1), :] += jnp.sum(value, axis=0, keepdims=True)


def up_back(up_low, up_full, residual, grad_low, scale, ties=()):
    rows, ff = up_low.shape
    size = 256
    block = pl.BlockSpec((size, D), lambda i: (i, 0))
    return call(
        up_back_kernel,
        "up_back",
        2 * rows * ff * D,
        (up_low, up_full, residual, grad_low, scale.reshape(1, D)),
        ties,
        grid=(rows // size,),
        in_specs=[
            pl.BlockSpec((size, ff), lambda i: (i, 0)),
            pl.BlockSpec((ff, D), lambda i: (0, 0)),
            block,
            block,
            pl.BlockSpec((1, D), lambda i: (0, 0)),
        ],
        out_specs=[block, block, pl.BlockSpec((8, D), lambda i: (0, 0))],
        out_shape=[
            jax.ShapeDtypeStruct((rows, D), f32),
            jax.ShapeDtypeStruct((rows, D), bf16),
            jax.ShapeDtypeStruct((8, D), f32),
        ],
    )


def adam_update(weight, mean_old, square_old, gradient, step_rate, decay_rate):
    mean_new = beta_first * mean_old + (1.0 - beta_first) * gradient
    square_new = beta_second * square_old + (1.0 - beta_second) * gradient * gradient
    mean_hat = mean_new / (1.0 - beta_first**STEP)
    square_hat = square_new / (1.0 - beta_second**STEP)
    weight_new = weight - step_rate * (
        mean_hat / (jnp.sqrt(square_hat) + adam_floor) + decay_rate * weight
    )
    return (weight_new, mean_new, square_new)


def per_device(
    hidden_in,
    cotangent,
    lengths,
    qkv_weight,
    qkv_mean,
    qkv_square,
    out_weight,
    out_mean,
    out_square,
    up_weight,
    up_mean,
    up_square,
    down_weight,
    down_mean,
    down_square,
    vectors,
    vectors_mean,
    vectors_square,
    upbias,
    upbias_mean,
    upbias_square,
):
    shards = (qkv_weight, out_weight, up_weight, down_weight, vectors, upbias)
    first_moments = (qkv_mean, out_mean, up_mean, down_mean, vectors_mean, upbias_mean)
    squares = (qkv_square, out_square, up_square, down_square, vectors_square, upbias_square)
    grid = Grid()
    n = D // grid.shards
    slots = hidden_in.shape[0]
    row_count = slots * BLOCK
    ff = 4 * D

    attn_units = jnp.stack(
        [qkv_weight[:, :D], qkv_weight[:, D : 2 * D], qkv_weight[:, 2 * D :], out_weight]
    )
    attn_unit = take(attn_units, grid.r).astype(bf16)
    small = jnp.concatenate([vectors.reshape(-1), upbias]).astype(bf16)
    small = jnp.pad(small, (0, EXTRA * D - small.shape[0])).reshape(EXTRA, D)
    attn_unit = jnp.concatenate([attn_unit, small])
    up_unit = lax.dynamic_slice_in_dim(up_weight, grid.r * n, n, 1).astype(bf16).T
    down_unit = lax.dynamic_slice_in_dim(down_weight, grid.r * n, n, 0).astype(bf16)

    got, offs = gather_z(grid, attn_unit)
    attn_z = [part[:, :n] for part in got]
    small_z = jnp.concatenate([part[:, n:] for part in got])
    up_z = gather_z(grid, after(up_unit, got[1]))[0]
    down_z = gather_z(grid, after(down_unit, up_z[1]))[0]
    attn_xy, attn_pieces = gather_rest(grid, attn_z)
    up_xy, up_pieces = gather_rest(grid, [after(jnp.concatenate(up_z), *attn_xy)])
    down_xy, down_pieces = gather_rest(grid, [after(jnp.concatenate(down_z), *up_xy)])
    joined = [offs[0] + offs[1]]
    attn_full = assemble(grid, attn_pieces, offs, n)
    up_full = assemble(grid, up_pieces, joined, n).reshape(ff, D)
    down_full = assemble(grid, down_pieces, joined, n).reshape(ff, D)

    own = small_z.reshape(grid.zs, EXTRA * D)[:, : 12 * n]
    pair = jnp.stack([own, grid.move(own, over_x)])
    pair = jnp.stack([take(pair, grid.x), take(pair, 1 - grid.x)])
    where_off = jnp.array([joined[0].index(z) for z in range(grid.zs)])
    pair = pair[:, where_off[jnp.bitwise_xor(grid.z, jnp.arange(grid.zs))]]
    smalls = pair.transpose(1, 0, 2).reshape(grid.shards, 12 * n)
    vec_values = (
        smalls[:, : 8 * n].reshape(grid.shards, 8, n).transpose(1, 0, 2).reshape(8, D).astype(f32)
    )
    bias_full = (
        smalls[:, 8 * n :].reshape(grid.shards, 4, n).transpose(1, 0, 2).reshape(ff).astype(f32)
    )

    attn_full = attn_full.reshape(4, D, D)
    qkv_full, out_full = attn_full[:3], attn_full[3]

    flat_in = hidden_in.reshape(row_count, D).astype(f32)
    positions = jnp.arange(BLOCK, dtype=jnp.int32)
    row_valid = (positions[None, :] < lengths[:, None]).astype(f32).reshape(row_count, 1)
    normed_one, hat_one, inv_one = norm_forward(flat_in, vec_values[0], vec_values[1])
    normed_low = normed_one.astype(bf16)
    bias_rows = jnp.stack([vec_values[2], jnp.zeros((D,), f32), vec_values[3]])
    qkv_rows = [
        (
            jnp.dot(normed_low, qkv_full[i], preferred_element_type=f32) + bias_rows[i]
        ).astype(bf16)
        for i in range(3)
    ]
    context_flat, logsum = attend(*qkv_rows)
    residual = (
        flat_in + jnp.dot(context_flat, out_full, preferred_element_type=f32) + vec_values[4]
    )
    second_low = norm_forward(residual, vec_values[5], vec_values[6])[0].astype(bf16)
    active_low, slope = up_forward(second_low, up_full, bias_full)
    down_out = jnp.dot(active_low, down_full, preferred_element_type=f32) + vec_values[7]
    output = ((residual + down_out) * row_valid).astype(bf16).reshape(slots, BLOCK, D)

    grad_out = cotangent.reshape(row_count, D).astype(f32) * row_valid
    grad_low = grad_out.astype(bf16)
    down_bias_grad = jnp.sum(grad_out, axis=0)
    down_sum = reduce_rows(grid, weight_grad(active_low, grad_low), n)
    up_low, upbias_grad = active_back(grad_low, down_full, slope, [down_sum.sent])
    down_sent = down_sum.step()
    up_sum = reduce_rows(grid, weight_grad(up_low, second_low, [down_sent]), n)
    resid_grad, branch_low, norm_sums = up_back(
        up_low, up_full, residual, grad_low, vec_values[5], [up_sum.sent]
    )
    scale_two_grad, offset_two_grad, out_bias_grad = norm_sums[0], norm_sums[1], norm_sums[2]
    down_sent, up_sent = down_sum.step(), up_sum.step()
    out_grad = jnp.einsum(
        "nd,ne->de", context_flat, branch_low, preferred_element_type=f32
    ).astype(bf16)
    context_grad = jnp.einsum("ne,de->nd", branch_low, out_full, preferred_element_type=f32)
    rows_grad = attend_back(
        *qkv_rows, logsum, context_grad.astype(bf16), [down_sent, up_sent, out_grad]
    )
    query_grad, key_grad, value_grad = [
        jnp.einsum("nd,ne->de", normed_low, part, preferred_element_type=f32).astype(bf16)
        for part in rows_grad
    ]
    first = grid.c == 0
    theirs = jnp.stack([jnp.where(first, key_grad, query_grad), jnp.where(first, out_grad, value_grad)])
    mine = jnp.stack([jnp.where(first, query_grad, key_grad), jnp.where(first, value_grad, out_grad)])
    split = (2, grid.shards, n, D)
    attn_sum = Reduction(grid, theirs.reshape(split), mine.reshape(split))
    down_unit_grad = down_sum.finish()
    up_unit_grad = up_sum.finish()
    attn_unit_grad = attn_sum.finish()
    normed_grad = sum(
        jnp.einsum("ne,de->nd", rows_grad[i], qkv_full[i], preferred_element_type=f32)
        for i in range(3)
    )
    input_norm_grad, scale_one_grad, offset_one_grad = norm_backward(
        normed_grad, hat_one, inv_one, vec_values[0]
    )
    input_grad = (resid_grad + input_norm_grad).reshape(slots, BLOCK, D)
    small_grad = jnp.concatenate(
        [
            jnp.stack(
                [
                    scale_one_grad,
                    offset_one_grad,
                    jnp.sum(rows_grad[0].astype(f32), axis=0),
                    jnp.sum(rows_grad[2].astype(f32), axis=0),
                    out_bias_grad,
                    scale_two_grad,
                    offset_two_grad,
                    down_bias_grad,
                ]
            ),
            upbias_grad.reshape(4, D),
        ]
    )
    small_grad = reduce_small(grid, small_grad)
    small_own = lax.dynamic_slice_in_dim(small_grad, (2 * grid.z + grid.x) * n, n, 1)

    down_parts = share_unit(grid, down_unit_grad)
    up_parts = share_unit(grid, up_unit_grad)
    attn_parts = share_unit(grid, attn_unit_grad)
    reduced = (
        jnp.concatenate(attn_parts[:3], axis=1).astype(f32),
        attn_parts[3].astype(f32),
        jnp.concatenate(up_parts).T.astype(f32),
        jnp.concatenate(down_parts).astype(f32),
        small_own[:8],
        small_own[8:].reshape(-1),
    )
    updates = []
    for group_index in range(6):
        updates.extend(
            adam_update(
                shards[group_index],
                first_moments[group_index],
                squares[group_index],
                reduced[group_index],
                step_rates[group_index],
                decay_rates[group_index],
            )
        )
    return (output, input_grad) + tuple(updates)


def solution(mesh):
    tokens = P(("fsdp", "dp"), None, None)
    rows, columns = P("fsdp", None), P(None, "fsdp")
    state = (rows,) * 6 + (columns,) * 3 + (rows,) * 3 + (columns,) * 3 + (P("fsdp"),) * 3
    return jax.shard_map(
        per_device,
        mesh=mesh,
        in_specs=(tokens, tokens, P(("fsdp", "dp"))) + state,
        out_specs=(tokens, tokens) + state,
        check_vma=False,
    )
```

```python
import functools
import math

import jax
import jax.numpy as jnp
from jax import lax
from jax.experimental import pallas as pl
from jax.experimental.pallas import tpu as pltpu
from jax.sharding import PartitionSpec as P

D = 1088
HEADS = 17
HDIM = 64
BLOCK = 512
STEP = 10
EXTRA = 8

norm_eps = 1e-05
beta_first = 0.9
beta_second = 0.999
adam_floor = 1e-08
step_rates = (0.05, 0.2, 0.05, 0.03, 0.5, 0.3)
decay_rates = (0.1, 0.1, 0.1, 0.1, 0.0, 0.0)

AXES = ("fsdp", "dp")
VMEM_LIMIT = 56 * 1024 * 1024
f32 = jnp.float32
bf16 = jnp.bfloat16


class Grid:
    def __init__(self):
        self.shards = lax.axis_size("fsdp")
        self.replicas = lax.axis_size("dp")
        self.zs = self.shards // 2
        self.ys = self.replicas // 2
        f, r = lax.axis_index("fsdp"), lax.axis_index("dp")
        self.z, self.x = f // 2, f % 2
        self.y, self.c = r // 2, r % 2
        self.r = r

    def move(self, value, route):
        pairs = []
        for z in range(self.zs):
            for x in range(2):
                for y in range(2):
                    for c in range(2):
                        to_z, to_x, to_y, to_c = route(z, x, y, c)
                        here = (2 * z + x) * 4 + 2 * y + c
                        pairs.append((here, (2 * to_z + to_x) * 4 + 2 * to_y + to_c))
        return lax.ppermute(value, AXES, pairs)


def over_z(bit):
    return lambda z, x, y, c: (z ^ bit, x, y, c)


def over_x(z, x, y, c):
    return (z, 1 - x, y, c)


def over_y(z, x, y, c):
    return (z, x, 1 - y, c)


def over_core(z, x, y, c):
    return (z, x, y, 1 - c)


def x_then_y(z, x, y, c):
    return (z, 1 - x, y, c) if c == 0 else (z, x, 1 - y, c)


def y_then_x(z, x, y, c):
    return (z, x, 1 - y, c) if c == 0 else (z, 1 - x, y, c)


def after(value, *others):
    return lax.optimization_barrier((value,) + others)[0]


def take(value, at, axis=0):
    return lax.dynamic_index_in_dim(value, at, axis, keepdims=False)


def z_bits(zs):
    return [1 << i for i in range(zs.bit_length() - 1)]


def gather_z(grid, unit):
    held, off = unit[None], [0]
    for bit in reversed(z_bits(grid.zs)[1:]):
        held = jnp.concatenate([held, grid.move(held, over_z(bit))])
        off = off + [z ^ bit for z in off]
    return [held, grid.move(held, over_z(1))], [off, [z ^ 1 for z in off]]


def gather_xy(grid, held):
    both = jnp.stack([held, grid.move(held, y_then_x)])
    return [both, grid.move(both, x_then_y)]


def gather_rest(grid, halves):
    pieces = [p for held in halves for p in gather_xy(grid, held)]
    return pieces, pieces + [grid.move(p, over_core) for p in pieces]


def assemble_kernel(zs, offs, *refs):
    count = 4 * len(offs)
    pieces, (out, held, in_sems, out_sem) = refs[:count], refs[count:]
    f, r = lax.axis_index("fsdp"), lax.axis_index("dp")
    z, x, y, c = f // 2, f % 2, r // 2, r % 2
    first, second = [], []
    for number in range(count):
        dc, late = number // (count // 2), number % 2
        off = offs[(number // 2) % len(offs)]
        core = c ^ dc
        for early in range(2):
            dx = late + core * (early - late)
            dy = early + core * (late - early)
            owner = 2 * (y ^ dy) + core
            for k in range(len(off)):
                place = (owner, 2 * (z ^ off[k]) + (x ^ dx))
                sem = in_sems.at[number]
                first.append(pltpu.make_async_copy(pieces[number].at[early, k], held.at[place], sem))
                second.append(pltpu.make_async_copy(held.at[place], out.at[place], out_sem))
    for copy in first:
        copy.start()
    each = len(first) // count
    for number in range(count):
        for copy in first[number * each : (number + 1) * each]:
            copy.wait()
        for copy in second[number * each : (number + 1) * each]:
            copy.start()
    for copy in second:
        copy.wait()


def assemble(grid, pieces, offs, rows):
    whole = (4, grid.shards, rows, D)
    return pl.pallas_call(
        functools.partial(assemble_kernel, grid.zs, offs),
        out_shape=jax.ShapeDtypeStruct(whole, bf16),
        in_specs=[pl.BlockSpec(memory_space=pl.ANY)] * len(pieces),
        out_specs=pl.BlockSpec(memory_space=pl.ANY),
        scratch_shapes=[
            pltpu.VMEM(whole, bf16),
            pltpu.SemaphoreType.DMA((len(pieces),)),
            pltpu.SemaphoreType.DMA(()),
        ],
        compiler_params=pltpu.CompilerParams(vmem_limit_bytes=VMEM_LIMIT),
        cost_estimate=pl.CostEstimate(flops=0, bytes_accessed=20_000_000, transcendentals=0),
        name="assemble",
    )(*pieces)


def add(first, second):
    return (first.astype(f32) + second.astype(f32)).astype(bf16)


class Reduction:
    def __init__(self, grid, theirs, mine):
        self.grid, self.n = grid, mine.shape[2]
        self.stage = 0
        self.bits = z_bits(grid.zs)
        self.keep, self.sent = mine, theirs
        self.route = over_core

    def step(self):
        grid, n = self.grid, self.n
        total = add(self.keep, grid.move(self.sent, self.route))
        first = grid.c == 0
        x, y = grid.x, grid.y
        if self.stage == 0:
            total = total.reshape(2, grid.zs, 2, n, D)
            self.sent = jnp.where(first, take(total, 1 - x, 2), take(total, 1 - y, 0).swapaxes(0, 1))
            self.keep = jnp.where(first, take(total, x, 2), take(total, y, 0).swapaxes(0, 1))
            self.route = x_then_y
        elif self.stage == 1:
            at = jnp.where(first, y, x)
            self.sent, self.keep = take(total, 1 - at), take(total, at)
            self.route = y_then_x
        elif self.stage - 2 < len(self.bits):
            bit = self.bits[self.stage - 2]
            at = (grid.z // bit) % 2
            total = total.reshape(-1, 2, n, D)
            self.sent, self.keep = take(total, 1 - at, 1), take(total, at, 1)
            self.route = over_z(bit)
        else:
            return total[0]
        self.stage += 1
        return self.sent

    def hold(self, *others):
        self.keep = after(self.keep, *others)

    def left(self):
        return self.stage - 2 < len(self.bits)

    def finish(self):
        while self.left():
            self.step()
        return self.step()


def reduce_rows(grid, grads, n):
    view = grads.reshape(2, 2, grid.shards, n, D)
    return Reduction(grid, take(view, 1 - grid.c, 1), take(view, grid.c, 1))


def share_unit(grid, unit):
    pair = jnp.stack([unit, grid.move(unit, over_y)])
    both = jnp.stack([pair, grid.move(pair, over_core)], axis=1).reshape((4,) + unit.shape)
    return [take(both, jnp.bitwise_xor(grid.r, r)) for r in range(4)]


def norm_forward(values, scales, offset):
    center = values - jnp.mean(values, axis=-1, keepdims=True)
    inverse = lax.rsqrt(jnp.mean(center * center, axis=-1, keepdims=True) + norm_eps)
    norm_hat = center * inverse
    return (norm_hat * scales + offset, norm_hat, inverse)


def norm_backward(gradient, norm_hat, inverse, scales):
    hat_grad = gradient * scales
    value_grad = inverse * (
        hat_grad
        - jnp.mean(hat_grad, axis=-1, keepdims=True)
        - norm_hat * jnp.mean(hat_grad * norm_hat, axis=-1, keepdims=True)
    )
    return (value_grad, jnp.sum(gradient * norm_hat, axis=0), jnp.sum(gradient, axis=0))


def head_masks(rows):
    lane = lax.broadcasted_iota(jnp.int32, (rows, 128), 1)
    return (lane < HDIM, lane >= HDIM)


def dot_over(left, right, left_at, right_at):
    return lax.dot_general(
        left, right, (((left_at,), (right_at,)), ((), ())), preferred_element_type=f32
    )


def score_tile(keys, queries, tile, size):
    scores = dot_over(keys, queries, 1, 1)
    rows_at = lax.broadcasted_iota(jnp.int32, scores.shape, 0)
    cols_at = lax.broadcasted_iota(jnp.int32, scores.shape, 1) + tile * size
    return jnp.where(rows_at <= cols_at, scores, -1e30)


def attend_kernel(q_ref, k_ref, v_ref, c_ref, lse_ref):
    size = 256
    masks = head_masks(BLOCK)

    def slab(at, width, heads, first):
        columns = pl.ds(at, width)
        values = v_ref[:, columns]
        parts = []
        for h in range(heads):
            parts.append(jnp.where(masks[h], values, 0) if heads > 1 else values)
        for tile in range(BLOCK // size):
            extent = (tile + 1) * size
            keys = k_ref[pl.ds(0, extent), columns]
            queries = q_ref[pl.ds(tile * size, size), columns] * 0.125
            total = None
            for h in range(heads):
                mine = jnp.where(masks[h][:size], queries, 0) if heads > 1 else queries
                scores = score_tile(keys, mine, tile, size)
                top = jnp.max(scores, axis=0, keepdims=True)
                powers = jnp.exp(scores - top)
                norm = jnp.sum(powers, axis=0, keepdims=True)
                probs = (powers * (1.0 / norm)).astype(bf16)
                lse_ref[first + h, :, pl.ds(tile * size, size)] = top + jnp.log(norm)
                piece = dot_over(probs, parts[h][:extent], 0, 0)
                total = piece if total is None else total + piece
            c_ref[pl.ds(tile * size, size), columns] = total.astype(bf16)

    def pair(i, _):
        slab(pl.multiple_of(i * 128, 128), 128, 2, 2 * i)
        return 0

    lax.fori_loop(0, HEADS // 2, pair, 0)
    slab((HEADS - 1) * HDIM, HDIM, 1, HEADS - 1)


def attend_back_kernel(q_ref, k_ref, v_ref, lse_ref, dc_ref, dq_ref, dk_ref, dv_ref):
    size = 256
    masks = head_masks(BLOCK)

    def slab(at, width, heads, first):
        columns = pl.ds(at, width)
        keys_all = k_ref[:, columns]
        key_parts = [jnp.where(masks[h], keys_all, 0) if heads > 1 else keys_all for h in range(heads)]
        dk_total, dv_total = None, None
        for tile in reversed(range(BLOCK // size)):
            extent = (tile + 1) * size
            keys = keys_all[:extent]
            values = v_ref[pl.ds(0, extent), columns]
            queries = q_ref[pl.ds(tile * size, size), columns] * 0.125
            grads = dc_ref[pl.ds(tile * size, size), columns]
            dq_total, dk_tile, dv_tile = None, None, None
            for h in range(heads):
                my_q = jnp.where(masks[h][:size], queries, 0) if heads > 1 else queries
                my_g = jnp.where(masks[h][:size], grads, 0) if heads > 1 else grads
                scores = score_tile(keys, my_q, tile, size)
                probs = jnp.exp(scores - lse_ref[first + h, :, pl.ds(tile * size, size)])
                prob_grad = dot_over(values, my_g, 1, 1)
                inner = jnp.sum(probs * prob_grad, axis=0, keepdims=True)
                score_grad = (probs * (prob_grad - inner)).astype(bf16)
                dv = dot_over(probs.astype(bf16), my_g, 1, 0)
                dk = dot_over(score_grad, my_q, 1, 0)
                dq = dot_over(score_grad, key_parts[h][:extent], 0, 0)
                dv_tile = dv if dv_tile is None else dv_tile + dv
                dk_tile = dk if dk_tile is None else dk_tile + dk
                dq_total = dq if dq_total is None else dq_total + dq
            dq_ref[pl.ds(tile * size, size), columns] = (dq_total * 0.125).astype(bf16)
            if dk_total is None:
                dk_total, dv_total = dk_tile, dv_tile
            else:
                dk_total = jnp.concatenate([dk_total[:extent] + dk_tile, dk_total[extent:]])
                dv_total = jnp.concatenate([dv_total[:extent] + dv_tile, dv_total[extent:]])
        dk_ref[:, columns] = dk_total.astype(bf16)
        dv_ref[:, columns] = dv_total.astype(bf16)

    def pair(i, _):
        slab(pl.multiple_of(i * 128, 128), 128, 2, 2 * i)
        return 0

    lax.fori_loop(0, HEADS // 2, pair, 0)
    slab((HEADS - 1) * HDIM, HDIM, 1, HEADS - 1)


def part_block(part):
    return pl.BlockSpec((None, BLOCK, D), lambda i: (part, i, 0))


def attend(qkv, ties=()):
    rows = qkv.shape[1]
    block = pl.BlockSpec((BLOCK, D), lambda i: (i, 0))
    lse = pl.BlockSpec((HEADS, 1, BLOCK), lambda i: (0, 0, i))
    return call(
        attend_kernel,
        "attend",
        14_000_000_000,
        (qkv, qkv, qkv),
        ties,
        grid=(rows // BLOCK,),
        in_specs=[part_block(0), part_block(1), part_block(2)],
        out_specs=[block, lse],
        out_shape=[
            jax.ShapeDtypeStruct((rows, D), bf16),
            jax.ShapeDtypeStruct((HEADS, 1, rows), f32),
        ],
    )


def attend_back(qkv, lse, context_grad, ties=()):
    rows = qkv.shape[1]
    block = pl.BlockSpec((BLOCK, D), lambda i: (i, 0))
    lse_block = pl.BlockSpec((HEADS, 1, BLOCK), lambda i: (0, 0, i))
    return call(
        attend_back_kernel,
        "attend_back",
        18_000_000_000,
        (qkv, qkv, qkv, lse, context_grad),
        ties,
        grid=(rows // BLOCK,),
        in_specs=[part_block(0), part_block(1), part_block(2), lse_block, block],
        out_specs=[block] * 3,
        out_shape=[jax.ShapeDtypeStruct((rows, D), bf16)] * 3,
    )


def call(kernel, name, flops, operands, ties=(), in_specs=(), **kw):
    count = len(operands)

    def body(*refs):
        kernel(*refs[:count], *refs[count + len(ties) :])

    return pl.pallas_call(
        body,
        in_specs=list(in_specs) + [pl.BlockSpec(memory_space=pl.ANY)] * len(ties),
        compiler_params=pltpu.CompilerParams(vmem_limit_bytes=VMEM_LIMIT),
        cost_estimate=pl.CostEstimate(flops=flops, bytes_accessed=20_000_000, transcendentals=0),
        name=name,
        **kw,
    )(*operands, *ties)


def weight_grad_kernel(left_ref, right_ref, out_ref):
    out_ref[...] = dot_over(left_ref[...], right_ref[...], 0, 0).astype(bf16)


def weight_grad(left, right, ties=()):
    rows, wide = left.shape
    tile = 512
    return call(
        weight_grad_kernel,
        "weight_grad",
        2 * rows * wide * D,
        (left, right),
        ties,
        grid=(pl.cdiv(wide, tile),),
        in_specs=[
            pl.BlockSpec((rows, tile), lambda i: (0, i)),
            pl.BlockSpec((rows, D), lambda i: (0, 0)),
        ],
        out_specs=pl.BlockSpec((tile, D), lambda i: (i, 0)),
        out_shape=jax.ShapeDtypeStruct((wide, D), bf16),
    )


def up_kernel(second_ref, up_ref, bias_ref, active_ref, slope_ref):
    pre = dot_over(second_ref[...], up_ref[...], 1, 1) + bias_ref[...]
    root = math.sqrt(2.0 / math.pi)
    square = pre * pre
    curve = jnp.tanh(pre * (root + (root * 0.044715) * square))
    half = 0.5 + 0.5 * curve
    active_ref[...] = (pre * half).astype(bf16)
    inner = root + (3.0 * root * 0.044715) * square
    slope_ref[...] = (half + (0.5 * pre) * (1.0 - curve * curve) * inner).astype(bf16)


def up_forward(second, up_full, bias, ties=()):
    rows, ff = second.shape[0], up_full.shape[0]
    tile = 512
    columns = pl.BlockSpec((rows, tile), lambda i: (0, i))
    return call(
        up_kernel,
        "up_forward",
        2 * rows * ff * D,
        (second, up_full, bias.reshape(1, ff)),
        ties,
        grid=(pl.cdiv(ff, tile),),
        in_specs=[
            pl.BlockSpec((rows, D), lambda i: (0, 0)),
            pl.BlockSpec((tile, D), lambda i: (i, 0)),
            pl.BlockSpec((1, tile), lambda i: (0, i)),
        ],
        out_specs=[columns, columns],
        out_shape=[jax.ShapeDtypeStruct((rows, ff), bf16)] * 2,
    )


def active_back_kernel(grad_ref, down_ref, slope_ref, out_ref, sum_ref):
    active_grad = dot_over(grad_ref[...], down_ref[...], 1, 1)
    low = (active_grad * slope_ref[...].astype(f32)).astype(bf16)
    out_ref[...] = low
    sum_ref[...] = jnp.sum(low.astype(f32), axis=0, keepdims=True)


def active_back(grad_low, down_full, slope, ties=()):
    rows, ff = slope.shape
    tile = 512
    columns = pl.BlockSpec((rows, tile), lambda i: (0, i))
    return call(
        active_back_kernel,
        "active_back",
        2 * rows * ff * D,
        (grad_low, down_full, slope),
        ties,
        grid=(pl.cdiv(ff, tile),),
        in_specs=[
            pl.BlockSpec((rows, D), lambda i: (0, 0)),
            pl.BlockSpec((tile, D), lambda i: (i, 0)),
            columns,
        ],
        out_specs=[columns, pl.BlockSpec((1, tile), lambda i: (0, i))],
        out_shape=[
            jax.ShapeDtypeStruct((rows, ff), bf16),
            jax.ShapeDtypeStruct((1, ff), f32),
        ],
    )


def row_mean(value):
    return jnp.sum(value, axis=-1, keepdims=True) * (1.0 / D)


def norm_back_rows(base, gradient, scales):
    center = base - row_mean(base)
    inverse = lax.rsqrt(row_mean(center * center) + norm_eps)
    hat = center * inverse
    scaled = gradient * scales
    back = inverse * (scaled - row_mean(scaled) - hat * row_mean(scaled * hat))
    return back, gradient * hat


def up_back_kernel(up_low_ref, up_ref, residual_ref, grad_ref, scale_ref, out_ref, low_ref, sums_ref):
    second_grad = dot_over(up_low_ref[...], up_ref[...], 1, 0)
    back, with_hat = norm_back_rows(residual_ref[...], second_grad, scale_ref[...])
    total = grad_ref[...].astype(f32) + back
    low = total.astype(bf16)
    out_ref[...] = total
    low_ref[...] = low

    @pl.when(pl.program_id(0) == 0)
    def _():
        sums_ref[...] = jnp.zeros_like(sums_ref)

    for at, value in enumerate([with_hat, second_grad, low.astype(f32)]):
        sums_ref[pl.ds(at, 1), :] += jnp.sum(value, axis=0, keepdims=True)


def up_back(up_low, up_full, residual, grad_low, scale, ties=()):
    rows, ff = up_low.shape
    size = 256
    block = pl.BlockSpec((size, D), lambda i: (i, 0))
    return call(
        up_back_kernel,
        "up_back",
        2 * rows * ff * D,
        (up_low, up_full, residual, grad_low, scale.reshape(1, D)),
        ties,
        grid=(rows // size,),
        in_specs=[
            pl.BlockSpec((size, ff), lambda i: (i, 0)),
            pl.BlockSpec((ff, D), lambda i: (0, 0)),
            block,
            block,
            pl.BlockSpec((1, D), lambda i: (0, 0)),
        ],
        out_specs=[block, block, pl.BlockSpec((8, D), lambda i: (0, 0))],
        out_shape=[
            jax.ShapeDtypeStruct((rows, D), f32),
            jax.ShapeDtypeStruct((rows, D), bf16),
            jax.ShapeDtypeStruct((8, D), f32),
        ],
    )


def qkv_kernel(normed_ref, weight_ref, bias_ref, out_ref):
    out_ref[...] = (dot_over(normed_ref[...], weight_ref[...], 1, 0) + bias_ref[...]).astype(bf16)


def qkv_forward(normed, attn_full, bias_rows):
    rows = normed.shape[0]
    return call(
        qkv_kernel,
        "qkv_forward",
        6 * rows * D * D,
        (normed, attn_full, bias_rows.reshape(3, 1, D)),
        grid=(3,),
        in_specs=[
            pl.BlockSpec((rows, D), lambda i: (0, 0)),
            pl.BlockSpec((None, D, D), lambda i: (i, 0, 0)),
            pl.BlockSpec((None, 1, D), lambda i: (i, 0, 0)),
        ],
        out_specs=pl.BlockSpec((None, rows, D), lambda i: (i, 0, 0)),
        out_shape=jax.ShapeDtypeStruct((3, rows, D), bf16),
    )


def qkv_back_kernel(dq_ref, dk_ref, dv_ref, weight_ref, base_ref, resid_ref, scale_ref, out_ref, sums_ref):
    normed_grad = dot_over(dq_ref[...], weight_ref[0], 1, 1)
    normed_grad += dot_over(dk_ref[...], weight_ref[1], 1, 1)
    normed_grad += dot_over(dv_ref[...], weight_ref[2], 1, 1)
    back, with_hat = norm_back_rows(base_ref[...].astype(f32), normed_grad, scale_ref[...])
    out_ref[...] = resid_ref[...] + back

    @pl.when(pl.program_id(0) == 0)
    def _():
        sums_ref[...] = jnp.zeros_like(sums_ref)

    totals = [with_hat, normed_grad, dq_ref[...].astype(f32), dv_ref[...].astype(f32)]
    for at, value in enumerate(totals):
        sums_ref[pl.ds(at, 1), :] += jnp.sum(value, axis=0, keepdims=True)


def qkv_back(rows_grad, attn_full, base, resid_grad, scale, ties=()):
    rows = base.shape[0]
    size = 256
    block = pl.BlockSpec((size, D), lambda i: (i, 0))
    return call(
        qkv_back_kernel,
        "qkv_back",
        6 * rows * D * D,
        (*rows_grad, attn_full, base, resid_grad, scale.reshape(1, D)),
        ties,
        grid=(rows // size,),
        in_specs=[block] * 3
        + [
            pl.BlockSpec((3, D, D), lambda i: (0, 0, 0)),
            block,
            block,
            pl.BlockSpec((1, D), lambda i: (0, 0)),
        ],
        out_specs=[block, pl.BlockSpec((8, D), lambda i: (0, 0))],
        out_shape=[
            jax.ShapeDtypeStruct((rows, D), f32),
            jax.ShapeDtypeStruct((8, D), f32),
        ],
    )


def plain_add_kernel(first_ref, second_ref, out_ref):
    out_ref[...] = first_ref[...] + second_ref[...]


def plain_add(first, second, ties=()):
    whole = pl.BlockSpec(first.shape, lambda: (0, 0))
    return call(
        plain_add_kernel,
        "plain_add",
        first.size,
        (first, second),
        ties,
        in_specs=[whole, whole],
        out_specs=whole,
        out_shape=jax.ShapeDtypeStruct(first.shape, f32),
    )


def adam_update(weight, mean_old, square_old, gradient, step_rate, decay_rate):
    mean_new = beta_first * mean_old + (1.0 - beta_first) * gradient
    square_new = beta_second * square_old + (1.0 - beta_second) * gradient * gradient
    mean_hat = mean_new / (1.0 - beta_first**STEP)
    square_hat = square_new / (1.0 - beta_second**STEP)
    weight_new = weight - step_rate * (
        mean_hat / (jnp.sqrt(square_hat) + adam_floor) + decay_rate * weight
    )
    return (weight_new, mean_new, square_new)


def per_device(
    hidden_in,
    cotangent,
    lengths,
    qkv_weight,
    qkv_mean,
    qkv_square,
    out_weight,
    out_mean,
    out_square,
    up_weight,
    up_mean,
    up_square,
    down_weight,
    down_mean,
    down_square,
    vectors,
    vectors_mean,
    vectors_square,
    upbias,
    upbias_mean,
    upbias_square,
):
    shards = (qkv_weight, out_weight, up_weight, down_weight, vectors, upbias)
    first_moments = (qkv_mean, out_mean, up_mean, down_mean, vectors_mean, upbias_mean)
    squares = (qkv_square, out_square, up_square, down_square, vectors_square, upbias_square)
    grid = Grid()
    n = D // grid.shards
    slots = hidden_in.shape[0]
    row_count = slots * BLOCK
    ff = 4 * D

    attn_units = jnp.stack(
        [qkv_weight[:, :D], qkv_weight[:, D : 2 * D], qkv_weight[:, 2 * D :], out_weight]
    )
    attn_unit = take(attn_units, grid.r).astype(bf16)
    small = jnp.concatenate([vectors.reshape(-1), upbias]).astype(bf16)
    small = jnp.pad(small, (0, EXTRA * D - small.shape[0])).reshape(EXTRA, D)
    attn_unit = jnp.concatenate([attn_unit, small])
    up_unit = lax.dynamic_slice_in_dim(up_weight, grid.r * n, n, 1).astype(bf16).T
    down_unit = lax.dynamic_slice_in_dim(down_weight, grid.r * n, n, 0).astype(bf16)

    got, offs = gather_z(grid, attn_unit)
    attn_z = [part[:, :n] for part in got]
    small_z = jnp.concatenate([part[:, n:] for part in got])
    up_z = gather_z(grid, after(up_unit, got[1]))[0]
    down_z = gather_z(grid, after(down_unit, up_z[1]))[0]
    attn_xy, attn_pieces = gather_rest(grid, attn_z)
    up_xy, up_pieces = gather_rest(grid, [after(jnp.concatenate(up_z), *attn_xy)])
    down_xy, down_pieces = gather_rest(grid, [after(jnp.concatenate(down_z), *up_xy)])
    joined = [offs[0] + offs[1]]
    attn_full = assemble(grid, attn_pieces, offs, n)
    up_full = assemble(grid, up_pieces, joined, n).reshape(ff, D)
    down_full = assemble(grid, down_pieces, joined, n).reshape(ff, D)

    own = small_z.reshape(grid.zs, EXTRA * D)[:, : 12 * n]
    pair = jnp.stack([own, grid.move(own, over_x)])
    pair = jnp.stack([take(pair, grid.x), take(pair, 1 - grid.x)])
    where_off = jnp.array([joined[0].index(z) for z in range(grid.zs)])
    pair = pair[:, where_off[jnp.bitwise_xor(grid.z, jnp.arange(grid.zs))]]
    smalls = pair.transpose(1, 0, 2).reshape(grid.shards, 12 * n)
    vec_values = (
        smalls[:, : 8 * n].reshape(grid.shards, 8, n).transpose(1, 0, 2).reshape(8, D).astype(f32)
    )
    bias_full = (
        smalls[:, 8 * n :].reshape(grid.shards, 4, n).transpose(1, 0, 2).reshape(ff).astype(f32)
    )

    attn_full = attn_full.reshape(4, D, D)
    out_full = attn_full[3]

    flat_in = hidden_in.reshape(row_count, D).astype(f32)
    positions = jnp.arange(BLOCK, dtype=jnp.int32)
    row_valid = (positions[None, :] < lengths[:, None]).astype(f32).reshape(row_count, 1)
    normed_one, hat_one, inv_one = norm_forward(flat_in, vec_values[0], vec_values[1])
    normed_low = normed_one.astype(bf16)
    bias_rows = jnp.stack([vec_values[2], jnp.zeros((D,), f32), vec_values[3]])
    qkv_rows = qkv_forward(normed_low, attn_full, bias_rows)
    context_flat, logsum = attend(qkv_rows, [up_xy[1]])
    residual = (
        flat_in + jnp.dot(context_flat, out_full, preferred_element_type=f32) + vec_values[4]
    )
    second_low = norm_forward(residual, vec_values[5], vec_values[6])[0].astype(bf16)
    active_low, slope = up_forward(second_low, up_full, bias_full, [down_xy[0]])
    down_out = jnp.dot(active_low, down_full, preferred_element_type=f32) + vec_values[7]
    output = ((residual + down_out) * row_valid).astype(bf16).reshape(slots, BLOCK, D)

    grad_out = cotangent.reshape(row_count, D).astype(f32) * row_valid
    grad_low = grad_out.astype(bf16)
    down_bias_grad = jnp.sum(grad_out, axis=0)
    down_sum = reduce_rows(grid, weight_grad(active_low, grad_low, [down_xy[1]]), n)
    up_low, upbias_grad = active_back(grad_low, down_full, slope, [down_sum.sent])
    down_sent = down_sum.step()
    up_sum = reduce_rows(grid, weight_grad(up_low, second_low, [down_sent]), n)
    resid_grad, branch_low, norm_sums = up_back(
        up_low, up_full, residual, grad_low, vec_values[5], [up_sum.sent]
    )
    scale_two_grad, offset_two_grad, out_bias_grad = norm_sums[0], norm_sums[1], norm_sums[2]
    down_sent, up_sent = down_sum.step(), up_sum.step()
    out_grad = jnp.einsum(
        "nd,ne->de", context_flat, branch_low, preferred_element_type=f32
    ).astype(bf16)
    context_grad = jnp.einsum("ne,de->nd", branch_low, out_full, preferred_element_type=f32)
    rows_grad = attend_back(
        qkv_rows, logsum, context_grad.astype(bf16), [down_sent, up_sent, out_grad]
    )
    query_grad, key_grad, value_grad = [
        jnp.einsum("nd,ne->de", normed_low, part, preferred_element_type=f32).astype(bf16)
        for part in rows_grad
    ]
    first = grid.c == 0
    theirs = jnp.stack([jnp.where(first, key_grad, query_grad), jnp.where(first, out_grad, value_grad)])
    mine = jnp.stack([jnp.where(first, query_grad, key_grad), jnp.where(first, value_grad, out_grad)])
    split = (2, grid.shards, n, D)
    attn_sum = Reduction(grid, theirs.reshape(split), mine.reshape(split))
    attn_sum.hold(up_sum.step(), down_sum.step())
    attn_sent = attn_sum.step()
    input_grad, first_sums = qkv_back(
        rows_grad,
        attn_full,
        hidden_in.reshape(row_count, D),
        resid_grad,
        vec_values[0],
        [attn_sent],
    )
    input_grad = input_grad.reshape(slots, BLOCK, D)
    small_grad = jnp.concatenate(
        [first_sums[:4], out_bias_grad[None], norm_sums[:2], down_bias_grad[None]]
        + [upbias_grad.reshape(4, D)]
    )
    for each in (attn_sum, up_sum, down_sum):
        each.hold(first_sums)
    waits = [output]
    routes = [over_core, over_y, over_x] + [over_z(bit) for bit in z_bits(grid.zs)]
    for route in routes:
        if attn_sum.left():
            attn_sent = attn_sum.step()
            if waits:
                attn_sum.hold(*waits)
            waits = []
        small_grad = plain_add(small_grad, grid.move(small_grad, route), [attn_sent])
    attn_unit_grad = attn_sum.finish()
    down_unit_grad = down_sum.finish()
    up_unit_grad = up_sum.finish()
    small_own = lax.dynamic_slice_in_dim(small_grad, (2 * grid.z + grid.x) * n, n, 1)

    down_parts = share_unit(grid, down_unit_grad)
    up_parts = share_unit(grid, up_unit_grad)
    attn_parts = share_unit(grid, attn_unit_grad)
    reduced = (
        jnp.concatenate(attn_parts[:3], axis=1).astype(f32),
        attn_parts[3].astype(f32),
        jnp.concatenate(up_parts).T.astype(f32),
        jnp.concatenate(down_parts).astype(f32),
        small_own[:8],
        small_own[8:].reshape(-1),
    )
    updates = []
    for group_index in range(6):
        updates.extend(
            adam_update(
                shards[group_index],
                first_moments[group_index],
                squares[group_index],
                reduced[group_index],
                step_rates[group_index],
                decay_rates[group_index],
            )
        )
    return (output, input_grad) + tuple(updates)


def solution(mesh):
    tokens = P(("fsdp", "dp"), None, None)
    rows, columns = P("fsdp", None), P(None, "fsdp")
    state = (rows,) * 6 + (columns,) * 3 + (rows,) * 3 + (columns,) * 3 + (P("fsdp"),) * 3
    return jax.shard_map(
        per_device,
        mesh=mesh,
        in_specs=(tokens, tokens, P(("fsdp", "dp"))) + state,
        out_specs=(tokens, tokens) + state,
        check_vma=False,
    )
```

```python
import functools
import math

import jax
import jax.numpy as jnp
from jax import lax
from jax.experimental import pallas as pl
from jax.experimental.pallas import tpu as pltpu
from jax.sharding import PartitionSpec as P

D = 1088
HEADS = 17
HDIM = 64
BLOCK = 512
STEP = 10
EXTRA = 8

norm_eps = 1e-05
beta_first = 0.9
beta_second = 0.999
adam_floor = 1e-08
step_rates = (0.05, 0.2, 0.05, 0.03, 0.5, 0.3)
decay_rates = (0.1, 0.1, 0.1, 0.1, 0.0, 0.0)

AXES = ("fsdp", "dp")
VMEM_LIMIT = 56 * 1024 * 1024
f32 = jnp.float32
bf16 = jnp.bfloat16


class Grid:
    def __init__(self):
        self.shards = lax.axis_size("fsdp")
        self.replicas = lax.axis_size("dp")
        self.zs = self.shards // 2
        self.ys = self.replicas // 2
        f, r = lax.axis_index("fsdp"), lax.axis_index("dp")
        self.z, self.x = f // 2, f % 2
        self.y, self.c = r // 2, r % 2
        self.r = r

    def move(self, value, route):
        pairs = []
        for z in range(self.zs):
            for x in range(2):
                for y in range(2):
                    for c in range(2):
                        to_z, to_x, to_y, to_c = route(z, x, y, c)
                        here = (2 * z + x) * 4 + 2 * y + c
                        pairs.append((here, (2 * to_z + to_x) * 4 + 2 * to_y + to_c))
        return lax.ppermute(value, AXES, pairs)


def over_z(bit):
    return lambda z, x, y, c: (z ^ bit, x, y, c)


def over_x(z, x, y, c):
    return (z, 1 - x, y, c)


def over_y(z, x, y, c):
    return (z, x, 1 - y, c)


def over_core(z, x, y, c):
    return (z, x, y, 1 - c)


def x_then_y(z, x, y, c):
    return (z, 1 - x, y, c) if c == 0 else (z, x, 1 - y, c)


def y_then_x(z, x, y, c):
    return (z, x, 1 - y, c) if c == 0 else (z, 1 - x, y, c)


def after(value, *others):
    return lax.optimization_barrier((value,) + others)[0]


def take(value, at, axis=0):
    return lax.dynamic_index_in_dim(value, at, axis, keepdims=False)


def z_bits(zs):
    return [1 << i for i in range(zs.bit_length() - 1)]


def gather_z(grid, unit):
    held, off = unit[None], [0]
    for bit in reversed(z_bits(grid.zs)[1:]):
        held = jnp.concatenate([held, grid.move(held, over_z(bit))])
        off = off + [z ^ bit for z in off]
    return [held, grid.move(held, over_z(1))], [off, [z ^ 1 for z in off]]


def gather_xy(grid, held):
    both = jnp.stack([held, grid.move(held, y_then_x)])
    return [both, grid.move(both, x_then_y)]


def gather_rest(grid, halves):
    pieces = [p for held in halves for p in gather_xy(grid, held)]
    return pieces, pieces + [grid.move(p, over_core) for p in pieces]


def assemble_kernel(zs, offs, *refs):
    count = 4 * len(offs)
    pieces, (out, held, in_sems, out_sem) = refs[:count], refs[count:]
    f, r = lax.axis_index("fsdp"), lax.axis_index("dp")
    z, x, y, c = f // 2, f % 2, r // 2, r % 2
    first, second = [], []
    for number in range(count):
        dc, late = number // (count // 2), number % 2
        off = offs[(number // 2) % len(offs)]
        core = c ^ dc
        for early in range(2):
            dx = late + core * (early - late)
            dy = early + core * (late - early)
            owner = 2 * (y ^ dy) + core
            for k in range(len(off)):
                place = (owner, 2 * (z ^ off[k]) + (x ^ dx))
                sem = in_sems.at[number]
                first.append(pltpu.make_async_copy(pieces[number].at[early, k], held.at[place], sem))
                second.append(pltpu.make_async_copy(held.at[place], out.at[place], out_sem))
    for copy in first:
        copy.start()
    each = len(first) // count
    for number in range(count):
        for copy in first[number * each : (number + 1) * each]:
            copy.wait()
        for copy in second[number * each : (number + 1) * each]:
            copy.start()
    for copy in second:
        copy.wait()


def assemble(grid, pieces, offs, rows):
    whole = (4, grid.shards, rows, D)
    return pl.pallas_call(
        functools.partial(assemble_kernel, grid.zs, offs),
        out_shape=jax.ShapeDtypeStruct(whole, bf16),
        in_specs=[pl.BlockSpec(memory_space=pl.ANY)] * len(pieces),
        out_specs=pl.BlockSpec(memory_space=pl.ANY),
        scratch_shapes=[
            pltpu.VMEM(whole, bf16),
            pltpu.SemaphoreType.DMA((len(pieces),)),
            pltpu.SemaphoreType.DMA(()),
        ],
        compiler_params=pltpu.CompilerParams(vmem_limit_bytes=VMEM_LIMIT),
        cost_estimate=pl.CostEstimate(flops=0, bytes_accessed=20_000_000, transcendentals=0),
        name="assemble",
    )(*pieces)


def add(first, second):
    return (first.astype(f32) + second.astype(f32)).astype(bf16)


class Reduction:
    def __init__(self, grid, theirs, mine):
        self.grid, self.n = grid, mine.shape[2]
        self.stage = 0
        self.bits = z_bits(grid.zs)
        self.keep, self.sent = mine, theirs
        self.route = over_core

    def step(self):
        grid, n = self.grid, self.n
        total = add(self.keep, grid.move(self.sent, self.route))
        first = grid.c == 0
        x, y = grid.x, grid.y
        if self.stage == 0:
            total = total.reshape(2, grid.zs, 2, n, D)
            self.sent = jnp.where(first, take(total, 1 - x, 2), take(total, 1 - y, 0).swapaxes(0, 1))
            self.keep = jnp.where(first, take(total, x, 2), take(total, y, 0).swapaxes(0, 1))
            self.route = x_then_y
        elif self.stage == 1:
            at = jnp.where(first, y, x)
            self.sent, self.keep = take(total, 1 - at), take(total, at)
            self.route = y_then_x
        elif self.stage - 2 < len(self.bits):
            bit = self.bits[self.stage - 2]
            at = (grid.z // bit) % 2
            total = total.reshape(-1, 2, n, D)
            self.sent, self.keep = take(total, 1 - at, 1), take(total, at, 1)
            self.route = over_z(bit)
        else:
            return total[0]
        self.stage += 1
        return self.sent

    def hold(self, *others):
        self.keep = after(self.keep, *others)

    def left(self):
        return self.stage - 2 < len(self.bits)

    def finish(self):
        while self.left():
            self.step()
        return self.step()


def reduce_rows(grid, grads, n):
    view = grads.reshape(2, 2, grid.shards, n, D)
    return Reduction(grid, take(view, 1 - grid.c, 1), take(view, grid.c, 1))


def share_unit(grid, unit):
    pair = jnp.stack([unit, grid.move(unit, over_y)])
    both = jnp.stack([pair, grid.move(pair, over_core)], axis=1).reshape((4,) + unit.shape)
    return [take(both, jnp.bitwise_xor(grid.r, r)) for r in range(4)]


def norm_forward(values, scales, offset):
    center = values - jnp.mean(values, axis=-1, keepdims=True)
    inverse = lax.rsqrt(jnp.mean(center * center, axis=-1, keepdims=True) + norm_eps)
    norm_hat = center * inverse
    return (norm_hat * scales + offset, norm_hat, inverse)


def norm_backward(gradient, norm_hat, inverse, scales):
    hat_grad = gradient * scales
    value_grad = inverse * (
        hat_grad
        - jnp.mean(hat_grad, axis=-1, keepdims=True)
        - norm_hat * jnp.mean(hat_grad * norm_hat, axis=-1, keepdims=True)
    )
    return (value_grad, jnp.sum(gradient * norm_hat, axis=0), jnp.sum(gradient, axis=0))


def head_masks(rows):
    lane = lax.broadcasted_iota(jnp.int32, (rows, 128), 1)
    return (lane < HDIM, lane >= HDIM)


def dot_over(left, right, left_at, right_at):
    return lax.dot_general(
        left, right, (((left_at,), (right_at,)), ((), ())), preferred_element_type=f32
    )


def score_tile(keys, queries, tile, size):
    scores = dot_over(keys, queries, 1, 1)
    rows_at = lax.broadcasted_iota(jnp.int32, scores.shape, 0)
    cols_at = lax.broadcasted_iota(jnp.int32, scores.shape, 1) + tile * size
    return jnp.where(rows_at <= cols_at, scores, -1e30)


def attend_kernel(q_ref, k_ref, v_ref, c_ref, lse_ref):
    size = 256
    masks = head_masks(BLOCK)

    def slab(at, width, heads, first):
        columns = pl.ds(at, width)
        values = v_ref[:, columns]
        parts = []
        for h in range(heads):
            parts.append(jnp.where(masks[h], values, 0) if heads > 1 else values)
        for tile in range(BLOCK // size):
            extent = (tile + 1) * size
            keys = k_ref[pl.ds(0, extent), columns]
            queries = q_ref[pl.ds(tile * size, size), columns] * 0.125
            total = None
            for h in range(heads):
                mine = jnp.where(masks[h][:size], queries, 0) if heads > 1 else queries
                scores = score_tile(keys, mine, tile, size)
                top = jnp.max(scores, axis=0, keepdims=True)
                powers = jnp.exp(scores - top)
                norm = jnp.sum(powers, axis=0, keepdims=True)
                probs = (powers * (1.0 / norm)).astype(bf16)
                lse_ref[first + h, :, pl.ds(tile * size, size)] = top + jnp.log(norm)
                piece = dot_over(probs, parts[h][:extent], 0, 0)
                total = piece if total is None else total + piece
            c_ref[pl.ds(tile * size, size), columns] = total.astype(bf16)

    def pair(i, _):
        slab(pl.multiple_of(i * 128, 128), 128, 2, 2 * i)
        return 0

    lax.fori_loop(0, HEADS // 2, pair, 0)
    slab((HEADS - 1) * HDIM, HDIM, 1, HEADS - 1)


def attend_back_kernel(q_ref, k_ref, v_ref, lse_ref, dc_ref, dq_ref, dk_ref, dv_ref):
    size = 256
    masks = head_masks(BLOCK)

    def slab(at, width, heads, first):
        columns = pl.ds(at, width)
        keys_all = k_ref[:, columns]
        key_parts = [jnp.where(masks[h], keys_all, 0) if heads > 1 else keys_all for h in range(heads)]
        dk_total, dv_total = None, None
        for tile in reversed(range(BLOCK // size)):
            extent = (tile + 1) * size
            keys = keys_all[:extent]
            values = v_ref[pl.ds(0, extent), columns]
            queries = q_ref[pl.ds(tile * size, size), columns] * 0.125
            grads = dc_ref[pl.ds(tile * size, size), columns]
            dq_total, dk_tile, dv_tile = None, None, None
            for h in range(heads):
                my_q = jnp.where(masks[h][:size], queries, 0) if heads > 1 else queries
                my_g = jnp.where(masks[h][:size], grads, 0) if heads > 1 else grads
                scores = score_tile(keys, my_q, tile, size)
                probs = jnp.exp(scores - lse_ref[first + h, :, pl.ds(tile * size, size)])
                prob_grad = dot_over(values, my_g, 1, 1)
                inner = jnp.sum(probs * prob_grad, axis=0, keepdims=True)
                score_grad = (probs * (prob_grad - inner)).astype(bf16)
                dv = dot_over(probs.astype(bf16), my_g, 1, 0)
                dk = dot_over(score_grad, my_q, 1, 0)
                dq = dot_over(score_grad, key_parts[h][:extent], 0, 0)
                dv_tile = dv if dv_tile is None else dv_tile + dv
                dk_tile = dk if dk_tile is None else dk_tile + dk
                dq_total = dq if dq_total is None else dq_total + dq
            dq_ref[pl.ds(tile * size, size), columns] = (dq_total * 0.125).astype(bf16)
            if dk_total is None:
                dk_total, dv_total = dk_tile, dv_tile
            else:
                dk_total = jnp.concatenate([dk_total[:extent] + dk_tile, dk_total[extent:]])
                dv_total = jnp.concatenate([dv_total[:extent] + dv_tile, dv_total[extent:]])
        dk_ref[:, columns] = dk_total.astype(bf16)
        dv_ref[:, columns] = dv_total.astype(bf16)

    def pair(i, _):
        slab(pl.multiple_of(i * 128, 128), 128, 2, 2 * i)
        return 0

    lax.fori_loop(0, HEADS // 2, pair, 0)
    slab((HEADS - 1) * HDIM, HDIM, 1, HEADS - 1)


def part_block(part):
    return pl.BlockSpec((None, BLOCK, D), lambda i: (part, i, 0))


def attend(qkv, ties=()):
    rows = qkv.shape[1]
    block = pl.BlockSpec((BLOCK, D), lambda i: (i, 0))
    lse = pl.BlockSpec((HEADS, 1, BLOCK), lambda i: (0, 0, i))
    return call(
        attend_kernel,
        "attend",
        14_000_000_000,
        (qkv, qkv, qkv),
        ties,
        grid=(rows // BLOCK,),
        in_specs=[part_block(0), part_block(1), part_block(2)],
        out_specs=[block, lse],
        out_shape=[
            jax.ShapeDtypeStruct((rows, D), bf16),
            jax.ShapeDtypeStruct((HEADS, 1, rows), f32),
        ],
    )


def attend_back(qkv, lse, context_grad, ties=()):
    rows = qkv.shape[1]
    block = pl.BlockSpec((BLOCK, D), lambda i: (i, 0))
    lse_block = pl.BlockSpec((HEADS, 1, BLOCK), lambda i: (0, 0, i))
    return call(
        attend_back_kernel,
        "attend_back",
        18_000_000_000,
        (qkv, qkv, qkv, lse, context_grad),
        ties,
        grid=(rows // BLOCK,),
        in_specs=[part_block(0), part_block(1), part_block(2), lse_block, block],
        out_specs=[block] * 3,
        out_shape=[jax.ShapeDtypeStruct((rows, D), bf16)] * 3,
    )


def call(kernel, name, flops, operands, ties=(), in_specs=(), **kw):
    count = len(operands)

    def body(*refs):
        kernel(*refs[:count], *refs[count + len(ties) :])

    return pl.pallas_call(
        body,
        in_specs=list(in_specs) + [pl.BlockSpec(memory_space=pl.ANY)] * len(ties),
        compiler_params=pltpu.CompilerParams(vmem_limit_bytes=VMEM_LIMIT),
        cost_estimate=pl.CostEstimate(flops=flops, bytes_accessed=20_000_000, transcendentals=0),
        name=name,
        **kw,
    )(*operands, *ties)


def weight_grad_kernel(left_ref, right_ref, out_ref):
    out_ref[...] = dot_over(left_ref[...], right_ref[...], 0, 0).astype(bf16)


def weight_grad(left, right, ties=()):
    rows, wide = left.shape
    tile = 512
    return call(
        weight_grad_kernel,
        "weight_grad",
        2 * rows * wide * D,
        (left, right),
        ties,
        grid=(pl.cdiv(wide, tile),),
        in_specs=[
            pl.BlockSpec((rows, tile), lambda i: (0, i)),
            pl.BlockSpec((rows, D), lambda i: (0, 0)),
        ],
        out_specs=pl.BlockSpec((tile, D), lambda i: (i, 0)),
        out_shape=jax.ShapeDtypeStruct((wide, D), bf16),
    )


def up_kernel(second_ref, up_ref, bias_ref, active_ref, slope_ref):
    pre = dot_over(second_ref[...], up_ref[...], 1, 1) + bias_ref[...]
    root = math.sqrt(2.0 / math.pi)
    square = pre * pre
    curve = jnp.tanh(pre * (root + (root * 0.044715) * square))
    half = 0.5 + 0.5 * curve
    active_ref[...] = (pre * half).astype(bf16)
    inner = root + (3.0 * root * 0.044715) * square
    slope_ref[...] = (half + (0.5 * pre) * (1.0 - curve * curve) * inner).astype(bf16)


def up_forward(second, up_full, bias, ties=()):
    rows, ff = second.shape[0], up_full.shape[0]
    tile = 512
    columns = pl.BlockSpec((rows, tile), lambda i: (0, i))
    return call(
        up_kernel,
        "up_forward",
        2 * rows * ff * D,
        (second, up_full, bias.reshape(1, ff)),
        ties,
        grid=(pl.cdiv(ff, tile),),
        in_specs=[
            pl.BlockSpec((rows, D), lambda i: (0, 0)),
            pl.BlockSpec((tile, D), lambda i: (i, 0)),
            pl.BlockSpec((1, tile), lambda i: (0, i)),
        ],
        out_specs=[columns, columns],
        out_shape=[jax.ShapeDtypeStruct((rows, ff), bf16)] * 2,
    )


def active_back_kernel(grad_ref, down_ref, slope_ref, out_ref, sum_ref):
    active_grad = dot_over(grad_ref[...], down_ref[...], 1, 1)
    low = (active_grad * slope_ref[...].astype(f32)).astype(bf16)
    out_ref[...] = low
    sum_ref[...] = jnp.sum(low.astype(f32), axis=0, keepdims=True)


def active_back(grad_low, down_full, slope, ties=()):
    rows, ff = slope.shape
    tile = 512
    columns = pl.BlockSpec((rows, tile), lambda i: (0, i))
    return call(
        active_back_kernel,
        "active_back",
        2 * rows * ff * D,
        (grad_low, down_full, slope),
        ties,
        grid=(pl.cdiv(ff, tile),),
        in_specs=[
            pl.BlockSpec((rows, D), lambda i: (0, 0)),
            pl.BlockSpec((tile, D), lambda i: (i, 0)),
            columns,
        ],
        out_specs=[columns, pl.BlockSpec((1, tile), lambda i: (0, i))],
        out_shape=[
            jax.ShapeDtypeStruct((rows, ff), bf16),
            jax.ShapeDtypeStruct((1, ff), f32),
        ],
    )


def row_mean(value):
    return jnp.sum(value, axis=-1, keepdims=True) * (1.0 / D)


def norm_back_rows(base, gradient, scales):
    center = base - row_mean(base)
    inverse = lax.rsqrt(row_mean(center * center) + norm_eps)
    hat = center * inverse
    scaled = gradient * scales
    back = inverse * (scaled - row_mean(scaled) - hat * row_mean(scaled * hat))
    return back, gradient * hat


def up_back_kernel(up_low_ref, up_ref, residual_ref, grad_ref, scale_ref, out_ref, low_ref, sums_ref):
    second_grad = dot_over(up_low_ref[...], up_ref[...], 1, 0)
    back, with_hat = norm_back_rows(residual_ref[...], second_grad, scale_ref[...])
    total = grad_ref[...].astype(f32) + back
    low = total.astype(bf16)
    out_ref[...] = total
    low_ref[...] = low

    @pl.when(pl.program_id(0) == 0)
    def _():
        sums_ref[...] = jnp.zeros_like(sums_ref)

    for at, value in enumerate([with_hat, second_grad, low.astype(f32)]):
        sums_ref[pl.ds(at, 1), :] += jnp.sum(value, axis=0, keepdims=True)


def up_back(up_low, up_full, residual, grad_low, scale, ties=()):
    rows, ff = up_low.shape
    size = 256
    block = pl.BlockSpec((size, D), lambda i: (i, 0))
    return call(
        up_back_kernel,
        "up_back",
        2 * rows * ff * D,
        (up_low, up_full, residual, grad_low, scale.reshape(1, D)),
        ties,
        grid=(rows // size,),
        in_specs=[
            pl.BlockSpec((size, ff), lambda i: (i, 0)),
            pl.BlockSpec((ff, D), lambda i: (0, 0)),
            block,
            block,
            pl.BlockSpec((1, D), lambda i: (0, 0)),
        ],
        out_specs=[block, block, pl.BlockSpec((8, D), lambda i: (0, 0))],
        out_shape=[
            jax.ShapeDtypeStruct((rows, D), f32),
            jax.ShapeDtypeStruct((rows, D), bf16),
            jax.ShapeDtypeStruct((8, D), f32),
        ],
    )


def qkv_kernel(normed_ref, weight_ref, bias_ref, out_ref):
    out_ref[...] = (dot_over(normed_ref[...], weight_ref[...], 1, 0) + bias_ref[...]).astype(bf16)


def qkv_forward(normed, attn_full, bias_rows, ties=()):
    rows = normed.shape[0]
    return call(
        qkv_kernel,
        "qkv_forward",
        6 * rows * D * D,
        (normed, attn_full, bias_rows.reshape(3, 1, D)),
        ties,
        grid=(3,),
        in_specs=[
            pl.BlockSpec((rows, D), lambda i: (0, 0)),
            pl.BlockSpec((None, D, D), lambda i: (i, 0, 0)),
            pl.BlockSpec((None, 1, D), lambda i: (i, 0, 0)),
        ],
        out_specs=pl.BlockSpec((None, rows, D), lambda i: (i, 0, 0)),
        out_shape=jax.ShapeDtypeStruct((3, rows, D), bf16),
    )


def qkv_back_kernel(dq_ref, dk_ref, dv_ref, weight_ref, base_ref, resid_ref, scale_ref, out_ref, sums_ref):
    normed_grad = dot_over(dq_ref[...], weight_ref[0], 1, 1)
    normed_grad += dot_over(dk_ref[...], weight_ref[1], 1, 1)
    normed_grad += dot_over(dv_ref[...], weight_ref[2], 1, 1)
    back, with_hat = norm_back_rows(base_ref[...].astype(f32), normed_grad, scale_ref[...])
    out_ref[...] = resid_ref[...] + back

    @pl.when(pl.program_id(0) == 0)
    def _():
        sums_ref[...] = jnp.zeros_like(sums_ref)

    totals = [with_hat, normed_grad, dq_ref[...].astype(f32), dv_ref[...].astype(f32)]
    for at, value in enumerate(totals):
        sums_ref[pl.ds(at, 1), :] += jnp.sum(value, axis=0, keepdims=True)


def qkv_back(rows_grad, attn_full, base, resid_grad, scale, ties=()):
    rows = base.shape[0]
    size = 256
    block = pl.BlockSpec((size, D), lambda i: (i, 0))
    return call(
        qkv_back_kernel,
        "qkv_back",
        6 * rows * D * D,
        (*rows_grad, attn_full, base, resid_grad, scale.reshape(1, D)),
        ties,
        grid=(rows // size,),
        in_specs=[block] * 3
        + [
            pl.BlockSpec((3, D, D), lambda i: (0, 0, 0)),
            block,
            block,
            pl.BlockSpec((1, D), lambda i: (0, 0)),
        ],
        out_specs=[block, pl.BlockSpec((8, D), lambda i: (0, 0))],
        out_shape=[
            jax.ShapeDtypeStruct((rows, D), f32),
            jax.ShapeDtypeStruct((8, D), f32),
        ],
    )


def plain_add_kernel(first_ref, second_ref, out_ref):
    out_ref[...] = first_ref[...] + second_ref[...]


def plain_add(first, second, ties=()):
    whole = pl.BlockSpec(first.shape, lambda: (0, 0))
    return call(
        plain_add_kernel,
        "plain_add",
        first.size,
        (first, second),
        ties,
        in_specs=[whole, whole],
        out_specs=whole,
        out_shape=jax.ShapeDtypeStruct(first.shape, f32),
    )


def adam_update(weight, mean_old, square_old, gradient, step_rate, decay_rate):
    mean_new = beta_first * mean_old + (1.0 - beta_first) * gradient
    square_new = beta_second * square_old + (1.0 - beta_second) * gradient * gradient
    mean_hat = mean_new / (1.0 - beta_first**STEP)
    square_hat = square_new / (1.0 - beta_second**STEP)
    weight_new = weight - step_rate * (
        mean_hat / (jnp.sqrt(square_hat) + adam_floor) + decay_rate * weight
    )
    return (weight_new, mean_new, square_new)


def per_device(
    hidden_in,
    cotangent,
    lengths,
    qkv_weight,
    qkv_mean,
    qkv_square,
    out_weight,
    out_mean,
    out_square,
    up_weight,
    up_mean,
    up_square,
    down_weight,
    down_mean,
    down_square,
    vectors,
    vectors_mean,
    vectors_square,
    upbias,
    upbias_mean,
    upbias_square,
):
    shards = (qkv_weight, out_weight, up_weight, down_weight, vectors, upbias)
    first_moments = (qkv_mean, out_mean, up_mean, down_mean, vectors_mean, upbias_mean)
    squares = (qkv_square, out_square, up_square, down_square, vectors_square, upbias_square)
    grid = Grid()
    n = D // grid.shards
    slots = hidden_in.shape[0]
    row_count = slots * BLOCK
    ff = 4 * D

    attn_units = jnp.stack(
        [qkv_weight[:, :D], qkv_weight[:, D : 2 * D], qkv_weight[:, 2 * D :], out_weight]
    )
    attn_unit = take(attn_units, grid.r).astype(bf16)
    small = jnp.concatenate([vectors.reshape(-1), upbias]).astype(bf16)
    small = jnp.pad(small, (0, EXTRA * D - small.shape[0])).reshape(EXTRA, D)
    attn_unit = jnp.concatenate([attn_unit, small])
    up_unit = lax.dynamic_slice_in_dim(up_weight, grid.r * n, n, 1).astype(bf16).T
    down_unit = lax.dynamic_slice_in_dim(down_weight, grid.r * n, n, 0).astype(bf16)

    got, offs = gather_z(grid, attn_unit)
    attn_z = [part[:, :n] for part in got]
    small_z = jnp.concatenate([part[:, n:] for part in got])
    up_z = gather_z(grid, after(up_unit, got[1]))[0]
    attn_xy, attn_pieces = gather_rest(grid, attn_z)
    up_held = after(jnp.concatenate(up_z), *attn_xy)
    up_both = jnp.stack([up_held, grid.move(up_held, y_then_x)])
    up_late = grid.move(up_both, x_then_y)
    down_unit = after(down_unit, *attn_pieces)
    joined = [offs[0] + offs[1]]
    attn_full = assemble(grid, attn_pieces, offs, n)

    own = small_z.reshape(grid.zs, EXTRA * D)[:, : 12 * n]
    pair = jnp.stack([own, grid.move(own, over_x)])
    pair = jnp.stack([take(pair, grid.x), take(pair, 1 - grid.x)])
    where_off = jnp.array([joined[0].index(z) for z in range(grid.zs)])
    pair = pair[:, where_off[jnp.bitwise_xor(grid.z, jnp.arange(grid.zs))]]
    smalls = pair.transpose(1, 0, 2).reshape(grid.shards, 12 * n)
    vec_values = (
        smalls[:, : 8 * n].reshape(grid.shards, 8, n).transpose(1, 0, 2).reshape(8, D).astype(f32)
    )
    bias_full = (
        smalls[:, 8 * n :].reshape(grid.shards, 4, n).transpose(1, 0, 2).reshape(ff).astype(f32)
    )

    attn_full = attn_full.reshape(4, D, D)
    out_full = attn_full[3]

    flat_in = hidden_in.reshape(row_count, D).astype(f32)
    positions = jnp.arange(BLOCK, dtype=jnp.int32)
    row_valid = (positions[None, :] < lengths[:, None]).astype(f32).reshape(row_count, 1)
    normed_one, hat_one, inv_one = norm_forward(flat_in, vec_values[0], vec_values[1])
    normed_low = normed_one.astype(bf16)
    bias_rows = jnp.stack([vec_values[2], jnp.zeros((D,), f32), vec_values[3]])
    qkv_rows = qkv_forward(normed_low, attn_full, bias_rows, [down_unit])
    up_late = after(up_late, qkv_rows)
    down_held = down_unit[None]
    for bit in reversed(z_bits(grid.zs)[1:]):
        down_held = jnp.concatenate([down_held, after(grid.move(down_held, over_z(bit)), qkv_rows)])
    context_flat, logsum = attend(qkv_rows, [up_late, down_held])
    up_pieces = [up_both, up_late] + [
        after(grid.move(p, over_core), context_flat) for p in (up_both, up_late)
    ]
    down_last = after(grid.move(down_held, over_z(1)), context_flat)
    context_flat = after(context_flat, down_last)
    down_held = jnp.concatenate([down_held, down_last])
    up_full = assemble(grid, up_pieces, joined, n).reshape(ff, D)
    residual = (
        flat_in + jnp.dot(context_flat, out_full, preferred_element_type=f32) + vec_values[4]
    )
    second_low = norm_forward(residual, vec_values[5], vec_values[6])[0].astype(bf16)
    down_got = after(grid.move(down_held, y_then_x), up_full, second_low)
    down_both = jnp.stack([down_held, down_got])
    active_low, slope = up_forward(second_low, up_full, bias_full, [down_both])
    down_late = after(grid.move(down_both, x_then_y), active_low)
    grad_out = cotangent.reshape(row_count, D).astype(f32) * row_valid
    grad_low = grad_out.astype(bf16)
    down_bias_grad = jnp.sum(grad_out, axis=0)
    down_grad = weight_grad(active_low, grad_low, [down_late])
    down_pieces = [down_both, down_late] + [
        after(grid.move(p, over_core), down_grad) for p in (down_both, down_late)
    ]
    down_full = assemble(grid, down_pieces, joined, n).reshape(ff, D)
    down_sum = reduce_rows(grid, after(down_grad, *down_pieces), n)
    down_out = jnp.dot(active_low, down_full, preferred_element_type=f32) + vec_values[7]
    output = ((residual + down_out) * row_valid).astype(bf16).reshape(slots, BLOCK, D)

    up_low, upbias_grad = active_back(grad_low, down_full, slope, [down_sum.sent])
    down_sum.hold(up_low)
    down_sent = down_sum.step()
    up_sum = reduce_rows(grid, weight_grad(up_low, second_low, [down_sent]), n)
    resid_grad, branch_low, norm_sums = up_back(
        up_low, up_full, residual, grad_low, vec_values[5], [up_sum.sent]
    )
    scale_two_grad, offset_two_grad, out_bias_grad = norm_sums[0], norm_sums[1], norm_sums[2]
    for each in (down_sum, up_sum):
        each.hold(branch_low)
    down_sent, up_sent = down_sum.step(), up_sum.step()
    out_grad = jnp.einsum(
        "nd,ne->de", context_flat, branch_low, preferred_element_type=f32
    ).astype(bf16)
    context_grad = jnp.einsum("ne,de->nd", branch_low, out_full, preferred_element_type=f32)
    rows_grad = attend_back(
        qkv_rows, logsum, context_grad.astype(bf16), [down_sent, up_sent, out_grad]
    )
    for each in (down_sum, up_sum):
        each.hold(rows_grad[0])
    rows_grad = after(tuple(rows_grad), up_sum.step(), down_sum.step())
    query_grad, key_grad, value_grad = [
        jnp.einsum("nd,ne->de", normed_low, part, preferred_element_type=f32).astype(bf16)
        for part in rows_grad
    ]
    first = grid.c == 0
    theirs = jnp.stack([jnp.where(first, key_grad, query_grad), jnp.where(first, out_grad, value_grad)])
    mine = jnp.stack([jnp.where(first, query_grad, key_grad), jnp.where(first, value_grad, out_grad)])
    split = (2, grid.shards, n, D)
    attn_sum = Reduction(grid, theirs.reshape(split), mine.reshape(split))
    attn_sent = attn_sum.step()
    input_grad, first_sums = qkv_back(
        rows_grad,
        attn_full,
        hidden_in.reshape(row_count, D),
        resid_grad,
        vec_values[0],
        [attn_sent],
    )
    input_grad = input_grad.reshape(slots, BLOCK, D)
    small_grad = jnp.concatenate(
        [first_sums[:4], out_bias_grad[None], norm_sums[:2], down_bias_grad[None]]
        + [upbias_grad.reshape(4, D)]
    )
    attn_sum.hold(first_sums)
    waits = [output]
    routes = [over_core, over_y, over_x] + [over_z(bit) for bit in z_bits(grid.zs)]
    for route in routes:
        if attn_sum.left():
            attn_sent = attn_sum.step()
            for each in (up_sum, down_sum):
                if each.left():
                    each.hold(attn_sent)
                    each.step()
            if waits:
                attn_sum.hold(*waits)
            waits = []
        small_grad = plain_add(small_grad, grid.move(small_grad, route), [attn_sent])
    attn_unit_grad = attn_sum.finish()
    down_unit_grad = down_sum.finish()
    up_unit_grad = up_sum.finish()
    small_own = lax.dynamic_slice_in_dim(small_grad, (2 * grid.z + grid.x) * n, n, 1)

    down_parts = share_unit(grid, down_unit_grad)
    up_parts = share_unit(grid, up_unit_grad)
    attn_parts = share_unit(grid, attn_unit_grad)
    reduced = (
        jnp.concatenate(attn_parts[:3], axis=1).astype(f32),
        attn_parts[3].astype(f32),
        jnp.concatenate(up_parts).T.astype(f32),
        jnp.concatenate(down_parts).astype(f32),
        small_own[:8],
        small_own[8:].reshape(-1),
    )
    updates = []
    for group_index in range(6):
        updates.extend(
            adam_update(
                shards[group_index],
                first_moments[group_index],
                squares[group_index],
                reduced[group_index],
                step_rates[group_index],
                decay_rates[group_index],
            )
        )
    return (output, input_grad) + tuple(updates)


def solution(mesh):
    tokens = P(("fsdp", "dp"), None, None)
    rows, columns = P("fsdp", None), P(None, "fsdp")
    state = (rows,) * 6 + (columns,) * 3 + (rows,) * 3 + (columns,) * 3 + (P("fsdp"),) * 3
    return jax.shard_map(
        per_device,
        mesh=mesh,
        in_specs=(tokens, tokens, P(("fsdp", "dp"))) + state,
        out_specs=(tokens, tokens) + state,
        check_vma=False,
    )
```

```python
import functools
import math

import jax
import jax.numpy as jnp
from jax import lax
from jax.experimental import pallas as pl
from jax.experimental.pallas import tpu as pltpu
from jax.sharding import PartitionSpec as P

D = 1088
HEADS = 17
HDIM = 64
BLOCK = 512
STEP = 10
EXTRA = 8

norm_eps = 1e-05
beta_first = 0.9
beta_second = 0.999
adam_floor = 1e-08
step_rates = (0.05, 0.2, 0.05, 0.03, 0.5, 0.3)
decay_rates = (0.1, 0.1, 0.1, 0.1, 0.0, 0.0)

AXES = ("fsdp", "dp")
VMEM_LIMIT = 56 * 1024 * 1024
f32 = jnp.float32
bf16 = jnp.bfloat16


class Grid:
    def __init__(self):
        self.shards = lax.axis_size("fsdp")
        self.replicas = lax.axis_size("dp")
        self.zs = self.shards // 2
        self.ys = self.replicas // 2
        f, r = lax.axis_index("fsdp"), lax.axis_index("dp")
        self.z, self.x = f // 2, f % 2
        self.y, self.c = r // 2, r % 2
        self.r = r

    def move(self, value, route):
        pairs = []
        for z in range(self.zs):
            for x in range(2):
                for y in range(2):
                    for c in range(2):
                        to_z, to_x, to_y, to_c = route(z, x, y, c)
                        here = (2 * z + x) * 4 + 2 * y + c
                        pairs.append((here, (2 * to_z + to_x) * 4 + 2 * to_y + to_c))
        return lax.ppermute(value, AXES, pairs)


def over_z(bit):
    return lambda z, x, y, c: (z ^ bit, x, y, c)


def over_x(z, x, y, c):
    return (z, 1 - x, y, c)


def over_y(z, x, y, c):
    return (z, x, 1 - y, c)


def over_core(z, x, y, c):
    return (z, x, y, 1 - c)


def x_then_y(z, x, y, c):
    return (z, 1 - x, y, c) if c == 0 else (z, x, 1 - y, c)


def y_then_x(z, x, y, c):
    return (z, x, 1 - y, c) if c == 0 else (z, 1 - x, y, c)


def after(value, *others):
    return lax.optimization_barrier((value,) + others)[0]


def take(value, at, axis=0):
    return lax.dynamic_index_in_dim(value, at, axis, keepdims=False)


def z_bits(zs):
    return [1 << i for i in range(zs.bit_length() - 1)]


def gather_z(grid, unit):
    held, off = unit[None], [0]
    for bit in reversed(z_bits(grid.zs)[1:]):
        held = jnp.concatenate([held, grid.move(held, over_z(bit))])
        off = off + [z ^ bit for z in off]
    return [held, grid.move(held, over_z(1))], [off, [z ^ 1 for z in off]]


def gather_xy(grid, held):
    both = jnp.stack([held, grid.move(held, y_then_x)])
    return [both, grid.move(both, x_then_y)]


def gather_rest(grid, halves):
    pieces = [p for held in halves for p in gather_xy(grid, held)]
    return pieces, pieces + [grid.move(p, over_core) for p in pieces]


def assemble_kernel(zs, offs, *refs):
    count = 4 * len(offs)
    pieces, (out, held, in_sems, out_sem) = refs[:count], refs[count:]
    f, r = lax.axis_index("fsdp"), lax.axis_index("dp")
    z, x, y, c = f // 2, f % 2, r // 2, r % 2
    first, second = [], []
    for number in range(count):
        dc, late = number // (count // 2), number % 2
        off = offs[(number // 2) % len(offs)]
        core = c ^ dc
        for early in range(2):
            dx = late + core * (early - late)
            dy = early + core * (late - early)
            owner = 2 * (y ^ dy) + core
            for k in range(len(off)):
                place = (owner, 2 * (z ^ off[k]) + (x ^ dx))
                sem = in_sems.at[number]
                first.append(pltpu.make_async_copy(pieces[number].at[early, k], held.at[place], sem))
                second.append(pltpu.make_async_copy(held.at[place], out.at[place], out_sem))
    for copy in first:
        copy.start()
    each = len(first) // count
    for number in range(count):
        for copy in first[number * each : (number + 1) * each]:
            copy.wait()
        for copy in second[number * each : (number + 1) * each]:
            copy.start()
    for copy in second:
        copy.wait()


def assemble(grid, pieces, offs, rows):
    whole = (4, grid.shards, rows, D)
    return pl.pallas_call(
        functools.partial(assemble_kernel, grid.zs, offs),
        out_shape=jax.ShapeDtypeStruct(whole, bf16),
        in_specs=[pl.BlockSpec(memory_space=pl.ANY)] * len(pieces),
        out_specs=pl.BlockSpec(memory_space=pl.ANY),
        scratch_shapes=[
            pltpu.VMEM(whole, bf16),
            pltpu.SemaphoreType.DMA((len(pieces),)),
            pltpu.SemaphoreType.DMA(()),
        ],
        compiler_params=pltpu.CompilerParams(vmem_limit_bytes=VMEM_LIMIT),
        cost_estimate=pl.CostEstimate(flops=0, bytes_accessed=20_000_000, transcendentals=0),
        name="assemble",
    )(*pieces)


def add(first, second):
    return (first.astype(f32) + second.astype(f32)).astype(bf16)


class Reduction:
    def __init__(self, grid, theirs, mine):
        self.grid, self.n = grid, mine.shape[2]
        self.stage = 0
        self.bits = z_bits(grid.zs)
        self.keep, self.sent = mine, theirs
        self.route = over_core

    def step(self):
        grid, n = self.grid, self.n
        mine, got = self.keep, grid.move(self.sent, self.route)
        first = grid.c == 0
        x, y = grid.x, grid.y
        if self.stage == 0:
            shape = (2, grid.zs, 2, n, D)

            def pick(value, at_x, at_y):
                value = value.reshape(shape)
                return jnp.where(first, take(value, at_x, 2), take(value, at_y, 0).swapaxes(0, 1))

            self.sent = add(pick(mine, 1 - x, 1 - y), pick(got, 1 - x, 1 - y))
            mine, got = after(mine, self.sent), after(got, self.sent)
            self.keep = add(pick(mine, x, y), pick(got, x, y))
            self.route = x_then_y
        elif self.stage == 1:
            at = jnp.where(first, y, x)
            self.sent = add(take(mine, 1 - at), take(got, 1 - at))
            self.keep = add(take(mine, at), take(got, at))
            self.route = y_then_x
        elif self.stage - 2 < len(self.bits):
            bit = self.bits[self.stage - 2]
            at = (grid.z // bit) % 2
            mine, got = mine.reshape(-1, 2, n, D), got.reshape(-1, 2, n, D)
            self.sent = add(take(mine, 1 - at, 1), take(got, 1 - at, 1))
            self.keep = add(take(mine, at, 1), take(got, at, 1))
            self.route = over_z(bit)
        else:
            return add(mine, got)[0]
        self.stage += 1
        return self.sent

    def hold(self, *others):
        self.keep = after(self.keep, *others)

    def left(self):
        return self.stage - 2 < len(self.bits)

    def finish(self):
        while self.left():
            self.step()
        return self.step()


def reduce_rows(grid, grads, n):
    view = grads.reshape(2, 2, grid.shards, n, D)
    return Reduction(grid, take(view, 1 - grid.c, 1), take(view, grid.c, 1))


def share_unit(grid, unit):
    pair = jnp.stack([unit, grid.move(unit, over_y)])
    both = jnp.stack([pair, grid.move(pair, over_core)], axis=1).reshape((4,) + unit.shape)
    return [take(both, jnp.bitwise_xor(grid.r, r)) for r in range(4)]


def norm_forward(values, scales, offset):
    center = values - jnp.mean(values, axis=-1, keepdims=True)
    inverse = lax.rsqrt(jnp.mean(center * center, axis=-1, keepdims=True) + norm_eps)
    norm_hat = center * inverse
    return (norm_hat * scales + offset, norm_hat, inverse)


def norm_backward(gradient, norm_hat, inverse, scales):
    hat_grad = gradient * scales
    value_grad = inverse * (
        hat_grad
        - jnp.mean(hat_grad, axis=-1, keepdims=True)
        - norm_hat * jnp.mean(hat_grad * norm_hat, axis=-1, keepdims=True)
    )
    return (value_grad, jnp.sum(gradient * norm_hat, axis=0), jnp.sum(gradient, axis=0))


def head_masks(rows):
    lane = lax.broadcasted_iota(jnp.int32, (rows, 128), 1)
    return (lane < HDIM, lane >= HDIM)


def dot_over(left, right, left_at, right_at):
    return lax.dot_general(
        left, right, (((left_at,), (right_at,)), ((), ())), preferred_element_type=f32
    )


def score_tile(keys, queries, tile, size):
    scores = dot_over(keys, queries, 1, 1)
    rows_at = lax.broadcasted_iota(jnp.int32, scores.shape, 0)
    cols_at = lax.broadcasted_iota(jnp.int32, scores.shape, 1) + tile * size
    return jnp.where(rows_at <= cols_at, scores, -1e30)


def attend_kernel(q_ref, k_ref, v_ref, c_ref, lse_ref):
    size = 256
    masks = head_masks(BLOCK)

    def slab(at, width, heads, first):
        columns = pl.ds(at, width)
        values = v_ref[:, columns]
        parts = []
        for h in range(heads):
            parts.append(jnp.where(masks[h], values, 0) if heads > 1 else values)
        for tile in range(BLOCK // size):
            extent = (tile + 1) * size
            keys = k_ref[pl.ds(0, extent), columns]
            queries = q_ref[pl.ds(tile * size, size), columns] * 0.125
            total = None
            for h in range(heads):
                mine = jnp.where(masks[h][:size], queries, 0) if heads > 1 else queries
                scores = score_tile(keys, mine, tile, size)
                top = jnp.max(scores, axis=0, keepdims=True)
                powers = jnp.exp(scores - top)
                norm = jnp.sum(powers, axis=0, keepdims=True)
                probs = (powers * (1.0 / norm)).astype(bf16)
                lse_ref[first + h, :, pl.ds(tile * size, size)] = top + jnp.log(norm)
                piece = dot_over(probs, parts[h][:extent], 0, 0)
                total = piece if total is None else total + piece
            c_ref[pl.ds(tile * size, size), columns] = total.astype(bf16)

    def pair(i, _):
        slab(pl.multiple_of(i * 128, 128), 128, 2, 2 * i)
        return 0

    lax.fori_loop(0, HEADS // 2, pair, 0)
    slab((HEADS - 1) * HDIM, HDIM, 1, HEADS - 1)


def attend_back_kernel(q_ref, k_ref, v_ref, lse_ref, dc_ref, dq_ref, dk_ref, dv_ref):
    size = 256
    masks = head_masks(BLOCK)

    def slab(at, width, heads, first):
        columns = pl.ds(at, width)
        keys_all = k_ref[:, columns]
        key_parts = [jnp.where(masks[h], keys_all, 0) if heads > 1 else keys_all for h in range(heads)]
        dk_total, dv_total = None, None
        for tile in reversed(range(BLOCK // size)):
            extent = (tile + 1) * size
            keys = keys_all[:extent]
            values = v_ref[pl.ds(0, extent), columns]
            queries = q_ref[pl.ds(tile * size, size), columns] * 0.125
            grads = dc_ref[pl.ds(tile * size, size), columns]
            dq_total, dk_tile, dv_tile = None, None, None
            for h in range(heads):
                my_q = jnp.where(masks[h][:size], queries, 0) if heads > 1 else queries
                my_g = jnp.where(masks[h][:size], grads, 0) if heads > 1 else grads
                scores = score_tile(keys, my_q, tile, size)
                probs = jnp.exp(scores - lse_ref[first + h, :, pl.ds(tile * size, size)])
                prob_grad = dot_over(values, my_g, 1, 1)
                inner = jnp.sum(probs * prob_grad, axis=0, keepdims=True)
                score_grad = (probs * (prob_grad - inner)).astype(bf16)
                dv = dot_over(probs.astype(bf16), my_g, 1, 0)
                dk = dot_over(score_grad, my_q, 1, 0)
                dq = dot_over(score_grad, key_parts[h][:extent], 0, 0)
                dv_tile = dv if dv_tile is None else dv_tile + dv
                dk_tile = dk if dk_tile is None else dk_tile + dk
                dq_total = dq if dq_total is None else dq_total + dq
            dq_ref[pl.ds(tile * size, size), columns] = (dq_total * 0.125).astype(bf16)
            if dk_total is None:
                dk_total, dv_total = dk_tile, dv_tile
            else:
                dk_total = jnp.concatenate([dk_total[:extent] + dk_tile, dk_total[extent:]])
                dv_total = jnp.concatenate([dv_total[:extent] + dv_tile, dv_total[extent:]])
        dk_ref[:, columns] = dk_total.astype(bf16)
        dv_ref[:, columns] = dv_total.astype(bf16)

    def pair(i, _):
        slab(pl.multiple_of(i * 128, 128), 128, 2, 2 * i)
        return 0

    lax.fori_loop(0, HEADS // 2, pair, 0)
    slab((HEADS - 1) * HDIM, HDIM, 1, HEADS - 1)


def part_block(part):
    return pl.BlockSpec((None, BLOCK, D), lambda i: (part, i, 0))


def attend(qkv, ties=()):
    rows = qkv.shape[1]
    block = pl.BlockSpec((BLOCK, D), lambda i: (i, 0))
    lse = pl.BlockSpec((HEADS, 1, BLOCK), lambda i: (0, 0, i))
    return call(
        attend_kernel,
        "attend",
        14_000_000_000,
        (qkv, qkv, qkv),
        ties,
        grid=(rows // BLOCK,),
        in_specs=[part_block(0), part_block(1), part_block(2)],
        out_specs=[block, lse],
        out_shape=[
            jax.ShapeDtypeStruct((rows, D), bf16),
            jax.ShapeDtypeStruct((HEADS, 1, rows), f32),
        ],
    )


def attend_back(qkv, lse, context_grad, ties=()):
    rows = qkv.shape[1]
    block = pl.BlockSpec((BLOCK, D), lambda i: (i, 0))
    lse_block = pl.BlockSpec((HEADS, 1, BLOCK), lambda i: (0, 0, i))
    return call(
        attend_back_kernel,
        "attend_back",
        18_000_000_000,
        (qkv, qkv, qkv, lse, context_grad),
        ties,
        grid=(rows // BLOCK,),
        in_specs=[part_block(0), part_block(1), part_block(2), lse_block, block],
        out_specs=[block] * 3,
        out_shape=[jax.ShapeDtypeStruct((rows, D), bf16)] * 3,
    )


def call(kernel, name, flops, operands, ties=(), in_specs=(), **kw):
    count = len(operands)

    def body(*refs):
        kernel(*refs[:count], *refs[count + len(ties) :])

    return pl.pallas_call(
        body,
        in_specs=list(in_specs) + [pl.BlockSpec(memory_space=pl.ANY)] * len(ties),
        compiler_params=pltpu.CompilerParams(vmem_limit_bytes=VMEM_LIMIT),
        cost_estimate=pl.CostEstimate(flops=flops, bytes_accessed=20_000_000, transcendentals=0),
        name=name,
        **kw,
    )(*operands, *ties)


def weight_grad_kernel(left_ref, right_ref, out_ref):
    out_ref[...] = dot_over(left_ref[...], right_ref[...], 0, 0).astype(bf16)


def weight_grad(left, right, ties=()):
    rows, wide = left.shape
    tile = 512
    return call(
        weight_grad_kernel,
        "weight_grad",
        2 * rows * wide * D,
        (left, right),
        ties,
        grid=(pl.cdiv(wide, tile),),
        in_specs=[
            pl.BlockSpec((rows, tile), lambda i: (0, i)),
            pl.BlockSpec((rows, D), lambda i: (0, 0)),
        ],
        out_specs=pl.BlockSpec((tile, D), lambda i: (i, 0)),
        out_shape=jax.ShapeDtypeStruct((wide, D), bf16),
    )


def times_transposed_kernel(left_ref, right_ref, out_ref):
    out_ref[...] = dot_over(left_ref[...], right_ref[...], 1, 1).astype(bf16)


def times_transposed(left, right):
    rows, size = left.shape[0], BLOCK
    block = pl.BlockSpec((size, D), lambda i: (i, 0))
    return call(
        times_transposed_kernel,
        "times_transposed",
        2 * rows * D * D,
        (left, right),
        grid=(rows // size,),
        in_specs=[block, pl.BlockSpec((D, D), lambda i: (0, 0))],
        out_specs=block,
        out_shape=jax.ShapeDtypeStruct((rows, D), bf16),
    )


def up_kernel(second_ref, up_ref, bias_ref, active_ref, slope_ref):
    pre = dot_over(second_ref[...], up_ref[...], 1, 1) + bias_ref[...]
    root = math.sqrt(2.0 / math.pi)
    square = pre * pre
    curve = jnp.tanh(pre * (root + (root * 0.044715) * square))
    half = 0.5 + 0.5 * curve
    active_ref[...] = (pre * half).astype(bf16)
    inner = root + (3.0 * root * 0.044715) * square
    slope_ref[...] = (half + (0.5 * pre) * (1.0 - curve * curve) * inner).astype(bf16)


def up_forward(second, up_full, bias, ties=()):
    rows, ff = second.shape[0], up_full.shape[0]
    tile = 512
    columns = pl.BlockSpec((rows, tile), lambda i: (0, i))
    return call(
        up_kernel,
        "up_forward",
        2 * rows * ff * D,
        (second, up_full, bias.reshape(1, ff)),
        ties,
        grid=(pl.cdiv(ff, tile),),
        in_specs=[
            pl.BlockSpec((rows, D), lambda i: (0, 0)),
            pl.BlockSpec((tile, D), lambda i: (i, 0)),
            pl.BlockSpec((1, tile), lambda i: (0, i)),
        ],
        out_specs=[columns, columns],
        out_shape=[jax.ShapeDtypeStruct((rows, ff), bf16)] * 2,
    )


def active_back_kernel(grad_ref, down_ref, slope_ref, out_ref, sum_ref):
    active_grad = dot_over(grad_ref[...], down_ref[...], 1, 1)
    low = (active_grad * slope_ref[...].astype(f32)).astype(bf16)
    out_ref[...] = low
    sum_ref[...] = jnp.sum(low.astype(f32), axis=0, keepdims=True)


def active_back(grad_low, down_full, slope, ties=()):
    rows, ff = slope.shape
    tile = 512
    columns = pl.BlockSpec((rows, tile), lambda i: (0, i))
    return call(
        active_back_kernel,
        "active_back",
        2 * rows * ff * D,
        (grad_low, down_full, slope),
        ties,
        grid=(pl.cdiv(ff, tile),),
        in_specs=[
            pl.BlockSpec((rows, D), lambda i: (0, 0)),
            pl.BlockSpec((tile, D), lambda i: (i, 0)),
            columns,
        ],
        out_specs=[columns, pl.BlockSpec((1, tile), lambda i: (0, i))],
        out_shape=[
            jax.ShapeDtypeStruct((rows, ff), bf16),
            jax.ShapeDtypeStruct((1, ff), f32),
        ],
    )


def row_mean(value):
    return jnp.sum(value, axis=-1, keepdims=True) * (1.0 / D)


def norm_back_rows(base, gradient, scales):
    center = base - row_mean(base)
    inverse = lax.rsqrt(row_mean(center * center) + norm_eps)
    hat = center * inverse
    scaled = gradient * scales
    back = inverse * (scaled - row_mean(scaled) - hat * row_mean(scaled * hat))
    return back, gradient * hat


def up_back_kernel(up_low_ref, up_ref, residual_ref, grad_ref, scale_ref, out_ref, low_ref, sums_ref):
    second_grad = dot_over(up_low_ref[...], up_ref[...], 1, 0)
    back, with_hat = norm_back_rows(residual_ref[...], second_grad, scale_ref[...])
    total = grad_ref[...].astype(f32) + back
    low = total.astype(bf16)
    out_ref[...] = total
    low_ref[...] = low

    @pl.when(pl.program_id(0) == 0)
    def _():
        sums_ref[...] = jnp.zeros_like(sums_ref)

    for at, value in enumerate([with_hat, second_grad, low.astype(f32)]):
        sums_ref[pl.ds(at, 1), :] += jnp.sum(value, axis=0, keepdims=True)


def up_back(up_low, up_full, residual, grad_low, scale, ties=()):
    rows, ff = up_low.shape
    size = 256
    block = pl.BlockSpec((size, D), lambda i: (i, 0))
    return call(
        up_back_kernel,
        "up_back",
        2 * rows * ff * D,
        (up_low, up_full, residual, grad_low, scale.reshape(1, D)),
        ties,
        grid=(rows // size,),
        in_specs=[
            pl.BlockSpec((size, ff), lambda i: (i, 0)),
            pl.BlockSpec((ff, D), lambda i: (0, 0)),
            block,
            block,
            pl.BlockSpec((1, D), lambda i: (0, 0)),
        ],
        out_specs=[block, block, pl.BlockSpec((8, D), lambda i: (0, 0))],
        out_shape=[
            jax.ShapeDtypeStruct((rows, D), f32),
            jax.ShapeDtypeStruct((rows, D), bf16),
            jax.ShapeDtypeStruct((8, D), f32),
        ],
    )


def qkv_kernel(normed_ref, weight_ref, bias_ref, out_ref):
    out_ref[...] = (dot_over(normed_ref[...], weight_ref[...], 1, 0) + bias_ref[...]).astype(bf16)


def qkv_forward(normed, attn_full, bias_rows, ties=()):
    rows = normed.shape[0]
    return call(
        qkv_kernel,
        "qkv_forward",
        6 * rows * D * D,
        (normed, attn_full, bias_rows.reshape(3, 1, D)),
        ties,
        grid=(3,),
        in_specs=[
            pl.BlockSpec((rows, D), lambda i: (0, 0)),
            pl.BlockSpec((None, D, D), lambda i: (i, 0, 0)),
            pl.BlockSpec((None, 1, D), lambda i: (i, 0, 0)),
        ],
        out_specs=pl.BlockSpec((None, rows, D), lambda i: (i, 0, 0)),
        out_shape=jax.ShapeDtypeStruct((3, rows, D), bf16),
    )


def qkv_back_kernel(dq_ref, dk_ref, dv_ref, weight_ref, base_ref, resid_ref, scale_ref, out_ref, sums_ref):
    normed_grad = dot_over(dq_ref[...], weight_ref[0], 1, 1)
    normed_grad += dot_over(dk_ref[...], weight_ref[1], 1, 1)
    normed_grad += dot_over(dv_ref[...], weight_ref[2], 1, 1)
    back, with_hat = norm_back_rows(base_ref[...].astype(f32), normed_grad, scale_ref[...])
    out_ref[...] = resid_ref[...] + back

    @pl.when(pl.program_id(0) == 0)
    def _():
        sums_ref[...] = jnp.zeros_like(sums_ref)

    totals = [with_hat, normed_grad, dq_ref[...].astype(f32), dv_ref[...].astype(f32)]
    for at, value in enumerate(totals):
        sums_ref[pl.ds(at, 1), :] += jnp.sum(value, axis=0, keepdims=True)


def qkv_back(rows_grad, attn_full, base, resid_grad, scale, ties=()):
    rows = base.shape[0]
    size = 256
    block = pl.BlockSpec((size, D), lambda i: (i, 0))
    return call(
        qkv_back_kernel,
        "qkv_back",
        6 * rows * D * D,
        (*rows_grad, attn_full, base, resid_grad, scale.reshape(1, D)),
        ties,
        grid=(rows // size,),
        in_specs=[block] * 3
        + [
            pl.BlockSpec((3, D, D), lambda i: (0, 0, 0)),
            block,
            block,
            pl.BlockSpec((1, D), lambda i: (0, 0)),
        ],
        out_specs=[block, pl.BlockSpec((8, D), lambda i: (0, 0))],
        out_shape=[
            jax.ShapeDtypeStruct((rows, D), f32),
            jax.ShapeDtypeStruct((8, D), f32),
        ],
    )


def plain_add_kernel(first_ref, second_ref, out_ref):
    out_ref[...] = first_ref[...] + second_ref[...]


def plain_add(first, second, ties=()):
    whole = pl.BlockSpec(first.shape, lambda: (0, 0))
    return call(
        plain_add_kernel,
        "plain_add",
        first.size,
        (first, second),
        ties,
        in_specs=[whole, whole],
        out_specs=whole,
        out_shape=jax.ShapeDtypeStruct(first.shape, f32),
    )


def adam_update(weight, mean_old, square_old, gradient, step_rate, decay_rate):
    mean_new = beta_first * mean_old + (1.0 - beta_first) * gradient
    square_new = beta_second * square_old + (1.0 - beta_second) * gradient * gradient
    mean_hat = mean_new / (1.0 - beta_first**STEP)
    square_hat = square_new / (1.0 - beta_second**STEP)
    weight_new = weight - step_rate * (
        mean_hat / (jnp.sqrt(square_hat) + adam_floor) + decay_rate * weight
    )
    return (weight_new, mean_new, square_new)


def per_device(
    hidden_in,
    cotangent,
    lengths,
    qkv_weight,
    qkv_mean,
    qkv_square,
    out_weight,
    out_mean,
    out_square,
    up_weight,
    up_mean,
    up_square,
    down_weight,
    down_mean,
    down_square,
    vectors,
    vectors_mean,
    vectors_square,
    upbias,
    upbias_mean,
    upbias_square,
):
    shards = (qkv_weight, out_weight, up_weight, down_weight, vectors, upbias)
    first_moments = (qkv_mean, out_mean, up_mean, down_mean, vectors_mean, upbias_mean)
    squares = (qkv_square, out_square, up_square, down_square, vectors_square, upbias_square)
    grid = Grid()
    n = D // grid.shards
    slots = hidden_in.shape[0]
    row_count = slots * BLOCK
    ff = 4 * D

    attn_units = jnp.stack(
        [qkv_weight[:, :D], qkv_weight[:, D : 2 * D], qkv_weight[:, 2 * D :], out_weight]
    )
    attn_unit = take(attn_units, grid.r).astype(bf16)
    small = jnp.concatenate([vectors.reshape(-1), upbias]).astype(bf16)
    small = jnp.pad(small, (0, EXTRA * D - small.shape[0])).reshape(EXTRA, D)
    attn_unit = jnp.concatenate([attn_unit, small])
    up_unit = lax.dynamic_slice_in_dim(up_weight, grid.r * n, n, 1).astype(bf16).T
    down_unit = lax.dynamic_slice_in_dim(down_weight, grid.r * n, n, 0).astype(bf16)

    positions = jnp.arange(BLOCK, dtype=jnp.int32)
    row_valid = (positions[None, :] < lengths[:, None]).astype(f32).reshape(row_count, 1)
    grad_out = cotangent.reshape(row_count, D).astype(f32) * row_valid
    grad_low = grad_out.astype(bf16)

    got, offs = gather_z(grid, attn_unit)
    attn_z = [part[:, :n] for part in got]
    small_z = jnp.concatenate([part[:, n:] for part in got])
    own = small_z.reshape(grid.zs, EXTRA * D)[:, : 12 * n]
    other = grid.move(own, over_x)
    up_z = gather_z(grid, after(up_unit, got[1], grad_low))[0]
    attn_xy, attn_pieces = gather_rest(grid, attn_z)
    up_held = after(jnp.concatenate(up_z), *attn_xy, other)
    up_both = jnp.stack([up_held, grid.move(up_held, y_then_x)])
    up_late = grid.move(up_both, x_then_y)
    down_unit = after(down_unit, *attn_pieces)
    joined = [offs[0] + offs[1]]
    attn_full = assemble(grid, attn_pieces, offs, n)

    pair = jnp.stack([own, other])
    pair = jnp.stack([take(pair, grid.x), take(pair, 1 - grid.x)])
    where_off = jnp.array([joined[0].index(z) for z in range(grid.zs)])
    pair = pair[:, where_off[jnp.bitwise_xor(grid.z, jnp.arange(grid.zs))]]
    smalls = pair.transpose(1, 0, 2).reshape(grid.shards, 12 * n)
    vec_values = (
        smalls[:, : 8 * n].reshape(grid.shards, 8, n).transpose(1, 0, 2).reshape(8, D).astype(f32)
    )
    bias_full = (
        smalls[:, 8 * n :].reshape(grid.shards, 4, n).transpose(1, 0, 2).reshape(ff).astype(f32)
    )

    attn_full = attn_full.reshape(4, D, D)
    out_full = attn_full[3]

    flat_in = hidden_in.reshape(row_count, D).astype(f32)
    normed_one, hat_one, inv_one = norm_forward(flat_in, vec_values[0], vec_values[1])
    normed_low = normed_one.astype(bf16)
    bias_rows = jnp.stack([vec_values[2], jnp.zeros((D,), f32), vec_values[3]])
    qkv_rows = qkv_forward(normed_low, attn_full, bias_rows, [down_unit])
    up_late = after(up_late, qkv_rows)
    down_held = down_unit[None]
    for bit in reversed(z_bits(grid.zs)[1:]):
        down_held = jnp.concatenate([down_held, after(grid.move(down_held, over_z(bit)), qkv_rows)])
    context_flat, logsum = attend(qkv_rows, [up_late, down_held])
    up_pieces = [up_both, up_late] + [
        after(grid.move(p, over_core), context_flat) for p in (up_both, up_late)
    ]
    down_last = after(grid.move(down_held, over_z(1)), context_flat)
    context_flat = after(context_flat, down_last)
    down_held = jnp.concatenate([down_held, down_last])
    up_full = assemble(grid, up_pieces, joined, n).reshape(ff, D)
    residual = (
        flat_in + jnp.dot(context_flat, out_full, preferred_element_type=f32) + vec_values[4]
    )
    second_low = norm_forward(residual, vec_values[5], vec_values[6])[0].astype(bf16)
    down_got = after(grid.move(down_held, y_then_x), up_full, second_low)
    down_both = jnp.stack([down_held, down_got])
    active_low, slope = up_forward(second_low, up_full, bias_full, [down_both])
    down_late = after(grid.move(down_both, x_then_y), active_low)
    down_bias_grad = jnp.sum(grad_out, axis=0)
    down_grad = weight_grad(active_low, grad_low, [down_late])
    down_pieces = [down_both, down_late] + [
        after(grid.move(p, over_core), down_grad) for p in (down_both, down_late)
    ]
    down_full = assemble(grid, down_pieces, joined, n).reshape(ff, D)
    down_sum = reduce_rows(grid, after(down_grad, *down_pieces), n)
    up_low, upbias_grad = active_back(grad_low, down_full, slope, [down_sum.sent])
    down_sum.hold(up_low)
    down_sent = down_sum.step()
    up_grad = weight_grad(up_low, second_low, [down_sent])
    down_sum.hold(up_grad)
    up_sum = reduce_rows(grid, after(up_grad, down_sum.step()), n)
    resid_grad, branch_low, norm_sums = up_back(
        up_low, up_full, residual, grad_low, vec_values[5], [up_sum.sent, down_sum.sent]
    )
    scale_two_grad, offset_two_grad, out_bias_grad = norm_sums[0], norm_sums[1], norm_sums[2]
    for each in (down_sum, up_sum):
        each.hold(branch_low)
    down_sent, up_sent = down_sum.step(), up_sum.step()
    out_grad = jnp.einsum(
        "nd,ne->de", context_flat, branch_low, preferred_element_type=f32
    ).astype(bf16)
    context_grad = times_transposed(branch_low, out_full)
    rows_grad = attend_back(
        qkv_rows, logsum, context_grad, [down_sent, up_sent, out_grad]
    )
    for each in (down_sum, up_sum):
        each.hold(rows_grad[0])
    rows_grad = after(tuple(rows_grad), up_sum.step(), down_sum.step())
    query_grad, key_grad, value_grad = [
        jnp.einsum("nd,ne->de", normed_low, part, preferred_element_type=f32).astype(bf16)
        for part in rows_grad
    ]
    first = grid.c == 0
    for each in (down_sum, up_sum):
        each.hold(value_grad)
    if down_sum.left():
        down_sum.step()
        down_ready = down_sum.sent
    else:
        down_ready = down_unit_grad = down_sum.step()
    value_grad = after(value_grad, up_sum.step(), down_ready)
    theirs = jnp.stack([jnp.where(first, key_grad, query_grad), jnp.where(first, out_grad, value_grad)])
    mine = jnp.stack([jnp.where(first, query_grad, key_grad), jnp.where(first, value_grad, out_grad)])
    split = (2, grid.shards, n, D)
    attn_sum = Reduction(grid, theirs.reshape(split), mine.reshape(split))
    attn_sent = attn_sum.step()
    input_grad, first_sums = qkv_back(
        rows_grad,
        attn_full,
        hidden_in.reshape(row_count, D),
        resid_grad,
        vec_values[0],
        [attn_sent],
    )
    input_grad = input_grad.reshape(slots, BLOCK, D)
    small_grad = jnp.concatenate(
        [first_sums[:4], out_bias_grad[None], norm_sums[:2], down_bias_grad[None]]
        + [upbias_grad.reshape(4, D)]
    )
    small_grad = jnp.concatenate(
        [first_sums[:4], out_bias_grad[None], norm_sums[:2], down_bias_grad[None]]
        + [upbias_grad.reshape(4, D)]
    )
    attn_sum.hold(first_sums)
    attn_sent = attn_sum.step()
    down_out = jnp.dot(
        after(active_low, attn_sent), down_full, preferred_element_type=f32
    ) + vec_values[7]
    output = ((residual + down_out) * row_valid).astype(bf16).reshape(slots, BLOCK, D)
    up_sum.hold(attn_sent)
    up_sum.step()
    routes = [over_core, over_y, over_x] + [over_z(bit) for bit in z_bits(grid.zs)]
    ties = [attn_sent]
    for at, route in enumerate(routes):
        if at >= 2 and attn_sum.left():
            attn_sum.hold(output)
            ties = [attn_sum.step()]
        small_grad = plain_add(small_grad, grid.move(small_grad, route), ties)
        ties = [output]
    if down_sum.left():
        down_unit_grad = down_sum.finish()
    up_sum.hold(attn_sum.sent)
    up_unit_grad = up_sum.finish()
    attn_unit_grad = attn_sum.finish()
    small_own = lax.dynamic_slice_in_dim(small_grad, (2 * grid.z + grid.x) * n, n, 1)

    down_parts = share_unit(grid, down_unit_grad)
    up_parts = share_unit(grid, up_unit_grad)
    attn_parts = share_unit(grid, attn_unit_grad)
    reduced = (
        jnp.concatenate(attn_parts[:3], axis=1).astype(f32),
        attn_parts[3].astype(f32),
        jnp.concatenate(up_parts).T.astype(f32),
        jnp.concatenate(down_parts).astype(f32),
        small_own[:8],
        small_own[8:].reshape(-1),
    )
    updates = []
    for group_index in range(6):
        updates.extend(
            adam_update(
                shards[group_index],
                first_moments[group_index],
                squares[group_index],
                reduced[group_index],
                step_rates[group_index],
                decay_rates[group_index],
            )
        )
    return (output, input_grad) + tuple(updates)


def solution(mesh):
    tokens = P(("fsdp", "dp"), None, None)
    rows, columns = P("fsdp", None), P(None, "fsdp")
    state = (rows,) * 6 + (columns,) * 3 + (rows,) * 3 + (columns,) * 3 + (P("fsdp"),) * 3
    return jax.shard_map(
        per_device,
        mesh=mesh,
        in_specs=(tokens, tokens, P(("fsdp", "dp"))) + state,
        out_specs=(tokens, tokens) + state,
        check_vma=False,
    )
```

```python
import functools
import math

import jax
import jax.numpy as jnp
from jax import lax
from jax.experimental import pallas as pl
from jax.experimental.pallas import tpu as pltpu
from jax.sharding import PartitionSpec as P

D = 1088
HEADS = 17
HDIM = 64
BLOCK = 512
STEP = 10
EXTRA = 8

norm_eps = 1e-05
beta_first = 0.9
beta_second = 0.999
adam_floor = 1e-08
step_rates = (0.05, 0.2, 0.05, 0.03, 0.5, 0.3)
decay_rates = (0.1, 0.1, 0.1, 0.1, 0.0, 0.0)

AXES = ("fsdp", "dp")
VMEM_LIMIT = 56 * 1024 * 1024
f32 = jnp.float32
bf16 = jnp.bfloat16


class Grid:
    def __init__(self):
        self.shards = lax.axis_size("fsdp")
        self.replicas = lax.axis_size("dp")
        self.zs = self.shards // 2
        self.ys = self.replicas // 2
        f, r = lax.axis_index("fsdp"), lax.axis_index("dp")
        self.z, self.x = f // 2, f % 2
        self.y, self.c = r // 2, r % 2
        self.r = r

    def move(self, value, route):
        pairs = []
        for z in range(self.zs):
            for x in range(2):
                for y in range(2):
                    for c in range(2):
                        to_z, to_x, to_y, to_c = route(z, x, y, c)
                        here = (2 * z + x) * 4 + 2 * y + c
                        pairs.append((here, (2 * to_z + to_x) * 4 + 2 * to_y + to_c))
        return lax.ppermute(value, AXES, pairs)


def over_z(bit):
    return lambda z, x, y, c: (z ^ bit, x, y, c)


def over_x(z, x, y, c):
    return (z, 1 - x, y, c)


def over_y(z, x, y, c):
    return (z, x, 1 - y, c)


def over_core(z, x, y, c):
    return (z, x, y, 1 - c)


def x_then_y(z, x, y, c):
    return (z, 1 - x, y, c) if c == 0 else (z, x, 1 - y, c)


def y_then_x(z, x, y, c):
    return (z, x, 1 - y, c) if c == 0 else (z, 1 - x, y, c)


def after(value, *others):
    return lax.optimization_barrier((value,) + others)[0]


def take(value, at, axis=0):
    return lax.dynamic_index_in_dim(value, at, axis, keepdims=False)


def z_bits(zs):
    return [1 << i for i in range(zs.bit_length() - 1)]


def gather_z(grid, unit):
    held, off = unit[None], [0]
    for bit in reversed(z_bits(grid.zs)[1:]):
        held = jnp.concatenate([held, grid.move(held, over_z(bit))])
        off = off + [z ^ bit for z in off]
    return [held, grid.move(held, over_z(1))], [off, [z ^ 1 for z in off]]


def gather_xy(grid, held):
    both = jnp.stack([held, grid.move(held, y_then_x)])
    return [both, grid.move(both, x_then_y)]


def gather_rest(grid, halves):
    pieces = [p for held in halves for p in gather_xy(grid, held)]
    return pieces, pieces + [grid.move(p, over_core) for p in pieces]


def assemble_kernel(zs, offs, *refs):
    count = 4 * len(offs)
    pieces, (out, held, in_sems, out_sem) = refs[:count], refs[count:]
    f, r = lax.axis_index("fsdp"), lax.axis_index("dp")
    z, x, y, c = f // 2, f % 2, r // 2, r % 2
    first, second = [], []
    for number in range(count):
        dc, late = number // (count // 2), number % 2
        off = offs[(number // 2) % len(offs)]
        core = c ^ dc
        for early in range(2):
            dx = late + core * (early - late)
            dy = early + core * (late - early)
            owner = 2 * (y ^ dy) + core
            for k in range(len(off)):
                place = (owner, 2 * (z ^ off[k]) + (x ^ dx))
                sem = in_sems.at[number]
                first.append(pltpu.make_async_copy(pieces[number].at[early, k], held.at[place], sem))
                second.append(pltpu.make_async_copy(held.at[place], out.at[place], out_sem))
    for copy in first:
        copy.start()
    each = len(first) // count
    for number in range(count):
        for copy in first[number * each : (number + 1) * each]:
            copy.wait()
        for copy in second[number * each : (number + 1) * each]:
            copy.start()
    for copy in second:
        copy.wait()


def assemble(grid, pieces, offs, rows):
    whole = (4, grid.shards, rows, D)
    return pl.pallas_call(
        functools.partial(assemble_kernel, grid.zs, offs),
        out_shape=jax.ShapeDtypeStruct(whole, bf16),
        in_specs=[pl.BlockSpec(memory_space=pl.ANY)] * len(pieces),
        out_specs=pl.BlockSpec(memory_space=pl.ANY),
        scratch_shapes=[
            pltpu.VMEM(whole, bf16),
            pltpu.SemaphoreType.DMA((len(pieces),)),
            pltpu.SemaphoreType.DMA(()),
        ],
        compiler_params=pltpu.CompilerParams(vmem_limit_bytes=VMEM_LIMIT),
        cost_estimate=pl.CostEstimate(flops=0, bytes_accessed=20_000_000, transcendentals=0),
        name="assemble",
    )(*pieces)


def add(first, second):
    return (first.astype(f32) + second.astype(f32)).astype(bf16)


class Reduction:
    def __init__(self, grid, theirs, mine):
        self.grid, self.n = grid, mine.shape[2]
        self.stage = 0
        self.bits = z_bits(grid.zs)
        self.keep, self.sent = mine, theirs
        self.route = over_core

    def step(self):
        grid, n = self.grid, self.n
        mine, got = self.keep, grid.move(self.sent, self.route)
        first = grid.c == 0
        x, y = grid.x, grid.y
        if self.stage == 0:
            shape = (2, grid.zs, 2, n, D)

            def pick(value, at_x, at_y):
                value = value.reshape(shape)
                return jnp.where(first, take(value, at_x, 2), take(value, at_y, 0).swapaxes(0, 1))

            self.sent = add(pick(mine, 1 - x, 1 - y), pick(got, 1 - x, 1 - y))
            mine = after(mine, self.sent)
            got = after(got, self.sent)
            self.keep = add(pick(mine, x, y), pick(got, x, y))
            self.route = x_then_y
        elif self.stage == 1:
            at = jnp.where(first, y, x)
            self.sent = add(take(mine, 1 - at), take(got, 1 - at))
            self.keep = add(take(mine, at), take(got, at))
            self.route = y_then_x
        elif self.stage - 2 < len(self.bits):
            bit = self.bits[self.stage - 2]
            at = (grid.z // bit) % 2
            mine, got = mine.reshape(-1, 2, n, D), got.reshape(-1, 2, n, D)
            self.sent = add(take(mine, 1 - at, 1), take(got, 1 - at, 1))
            self.keep = add(take(mine, at, 1), take(got, at, 1))
            self.route = over_z(bit)
        else:
            return add(mine, got)[0]
        self.stage += 1
        return self.sent

    def hold(self, *others):
        self.keep = after(self.keep, *others)

    def left(self):
        return self.stage - 2 < len(self.bits)

    def finish(self):
        while self.left():
            self.step()
        return self.step()


def reduce_rows(grid, grads, n):
    view = grads.reshape(2, 2, grid.shards, n, D)
    return Reduction(grid, take(view, 1 - grid.c, 1), take(view, grid.c, 1))


def share_unit(grid, unit, others=()):
    got = grid.move(unit, over_y)
    if others:
        got = after(got, *others)
    pair = jnp.stack([unit, got])
    both = jnp.stack([pair, grid.move(pair, over_core)], axis=1).reshape((4,) + unit.shape)
    return [take(both, jnp.bitwise_xor(grid.r, r)) for r in range(4)]


def norm_forward(values, scales, offset):
    center = values - jnp.mean(values, axis=-1, keepdims=True)
    inverse = lax.rsqrt(jnp.mean(center * center, axis=-1, keepdims=True) + norm_eps)
    norm_hat = center * inverse
    return (norm_hat * scales + offset, norm_hat, inverse)


def norm_backward(gradient, norm_hat, inverse, scales):
    hat_grad = gradient * scales
    value_grad = inverse * (
        hat_grad
        - jnp.mean(hat_grad, axis=-1, keepdims=True)
        - norm_hat * jnp.mean(hat_grad * norm_hat, axis=-1, keepdims=True)
    )
    return (value_grad, jnp.sum(gradient * norm_hat, axis=0), jnp.sum(gradient, axis=0))


def head_masks(rows):
    lane = lax.broadcasted_iota(jnp.int32, (rows, 128), 1)
    return (lane < HDIM, lane >= HDIM)


def dot_over(left, right, left_at, right_at):
    return lax.dot_general(
        left, right, (((left_at,), (right_at,)), ((), ())), preferred_element_type=f32
    )


def score_tile(keys, queries, tile, size):
    scores = dot_over(keys, queries, 1, 1)
    rows_at = lax.broadcasted_iota(jnp.int32, scores.shape, 0)
    cols_at = lax.broadcasted_iota(jnp.int32, scores.shape, 1) + tile * size
    return jnp.where(rows_at <= cols_at, scores, -1e30)


def attend_kernel(q_ref, k_ref, v_ref, c_ref, lse_ref):
    size = 256
    masks = head_masks(BLOCK)

    def slab(at, width, heads, first):
        columns = pl.ds(at, width)
        values = v_ref[:, columns]
        parts = []
        for h in range(heads):
            parts.append(jnp.where(masks[h], values, 0) if heads > 1 else values)
        for tile in range(BLOCK // size):
            extent = (tile + 1) * size
            keys = k_ref[pl.ds(0, extent), columns]
            queries = q_ref[pl.ds(tile * size, size), columns] * 0.125
            total = None
            for h in range(heads):
                mine = jnp.where(masks[h][:size], queries, 0) if heads > 1 else queries
                scores = score_tile(keys, mine, tile, size)
                top = jnp.max(scores, axis=0, keepdims=True)
                powers = jnp.exp(scores - top)
                norm = jnp.sum(powers, axis=0, keepdims=True)
                probs = (powers * (1.0 / norm)).astype(bf16)
                lse_ref[first + h, :, pl.ds(tile * size, size)] = top + jnp.log(norm)
                piece = dot_over(probs, parts[h][:extent], 0, 0)
                total = piece if total is None else total + piece
            c_ref[pl.ds(tile * size, size), columns] = total.astype(bf16)

    def pair(i, _):
        slab(pl.multiple_of(i * 128, 128), 128, 2, 2 * i)
        return 0

    lax.fori_loop(0, HEADS // 2, pair, 0)
    slab((HEADS - 1) * HDIM, HDIM, 1, HEADS - 1)


def attend_back_kernel(q_ref, k_ref, v_ref, lse_ref, dc_ref, dq_ref, dk_ref, dv_ref):
    size = 256
    masks = head_masks(BLOCK)

    def slab(at, width, heads, first):
        columns = pl.ds(at, width)
        keys_all = k_ref[:, columns]
        key_parts = [jnp.where(masks[h], keys_all, 0) if heads > 1 else keys_all for h in range(heads)]
        dk_total, dv_total = None, None
        for tile in reversed(range(BLOCK // size)):
            extent = (tile + 1) * size
            keys = keys_all[:extent]
            values = v_ref[pl.ds(0, extent), columns]
            queries = q_ref[pl.ds(tile * size, size), columns] * 0.125
            grads = dc_ref[pl.ds(tile * size, size), columns]
            dq_total, dk_tile, dv_tile = None, None, None
            for h in range(heads):
                my_q = jnp.where(masks[h][:size], queries, 0) if heads > 1 else queries
                my_g = jnp.where(masks[h][:size], grads, 0) if heads > 1 else grads
                scores = score_tile(keys, my_q, tile, size)
                probs = jnp.exp(scores - lse_ref[first + h, :, pl.ds(tile * size, size)])
                prob_grad = dot_over(values, my_g, 1, 1)
                inner = jnp.sum(probs * prob_grad, axis=0, keepdims=True)
                score_grad = (probs * (prob_grad - inner)).astype(bf16)
                dv = dot_over(probs.astype(bf16), my_g, 1, 0)
                dk = dot_over(score_grad, my_q, 1, 0)
                dq = dot_over(score_grad, key_parts[h][:extent], 0, 0)
                dv_tile = dv if dv_tile is None else dv_tile + dv
                dk_tile = dk if dk_tile is None else dk_tile + dk
                dq_total = dq if dq_total is None else dq_total + dq
            dq_ref[pl.ds(tile * size, size), columns] = (dq_total * 0.125).astype(bf16)
            if dk_total is None:
                dk_total, dv_total = dk_tile, dv_tile
            else:
                dk_total = jnp.concatenate([dk_total[:extent] + dk_tile, dk_total[extent:]])
                dv_total = jnp.concatenate([dv_total[:extent] + dv_tile, dv_total[extent:]])
        dk_ref[:, columns] = dk_total.astype(bf16)
        dv_ref[:, columns] = dv_total.astype(bf16)

    def pair(i, _):
        slab(pl.multiple_of(i * 128, 128), 128, 2, 2 * i)
        return 0

    lax.fori_loop(0, HEADS // 2, pair, 0)
    slab((HEADS - 1) * HDIM, HDIM, 1, HEADS - 1)


def part_block(part):
    return pl.BlockSpec((None, BLOCK, D), lambda i: (part, i, 0))


def attend(qkv, ties=()):
    rows = qkv.shape[1]
    block = pl.BlockSpec((BLOCK, D), lambda i: (i, 0))
    lse = pl.BlockSpec((HEADS, 1, BLOCK), lambda i: (0, 0, i))
    return call(
        attend_kernel,
        "attend",
        14_000_000_000,
        (qkv, qkv, qkv),
        ties,
        grid=(rows // BLOCK,),
        in_specs=[part_block(0), part_block(1), part_block(2)],
        out_specs=[block, lse],
        out_shape=[
            jax.ShapeDtypeStruct((rows, D), bf16),
            jax.ShapeDtypeStruct((HEADS, 1, rows), f32),
        ],
    )


def attend_back(qkv, lse, context_grad, ties=()):
    rows = qkv.shape[1]
    block = pl.BlockSpec((BLOCK, D), lambda i: (i, 0))
    lse_block = pl.BlockSpec((HEADS, 1, BLOCK), lambda i: (0, 0, i))
    return call(
        attend_back_kernel,
        "attend_back",
        18_000_000_000,
        (qkv, qkv, qkv, lse, context_grad),
        ties,
        grid=(rows // BLOCK,),
        in_specs=[part_block(0), part_block(1), part_block(2), lse_block, block],
        out_specs=[block] * 3,
        out_shape=[jax.ShapeDtypeStruct((rows, D), bf16)] * 3,
    )


def call(kernel, name, flops, operands, ties=(), in_specs=(), **kw):
    count = len(operands)

    def body(*refs):
        kernel(*refs[:count], *refs[count + len(ties) :])

    return pl.pallas_call(
        body,
        in_specs=list(in_specs) + [pl.BlockSpec(memory_space=pl.ANY)] * len(ties),
        compiler_params=pltpu.CompilerParams(vmem_limit_bytes=VMEM_LIMIT),
        cost_estimate=pl.CostEstimate(flops=flops, bytes_accessed=20_000_000, transcendentals=0),
        name=name,
        **kw,
    )(*operands, *ties)


def weight_grad_kernel(left_ref, right_ref, out_ref):
    out_ref[...] = dot_over(left_ref[...], right_ref[...], 0, 0).astype(bf16)


def weight_grad(left, right, ties=()):
    rows, wide = left.shape
    tile = 512
    return call(
        weight_grad_kernel,
        "weight_grad",
        2 * rows * wide * D,
        (left, right),
        ties,
        grid=(pl.cdiv(wide, tile),),
        in_specs=[
            pl.BlockSpec((rows, tile), lambda i: (0, i)),
            pl.BlockSpec((rows, D), lambda i: (0, 0)),
        ],
        out_specs=pl.BlockSpec((tile, D), lambda i: (i, 0)),
        out_shape=jax.ShapeDtypeStruct((wide, D), bf16),
    )


def times_transposed_kernel(left_ref, right_ref, out_ref):
    out_ref[...] = dot_over(left_ref[...], right_ref[...], 1, 1).astype(bf16)


def times_transposed(left, right):
    rows, size = left.shape[0], BLOCK
    block = pl.BlockSpec((size, D), lambda i: (i, 0))
    return call(
        times_transposed_kernel,
        "times_transposed",
        2 * rows * D * D,
        (left, right),
        grid=(rows // size,),
        in_specs=[block, pl.BlockSpec((D, D), lambda i: (0, 0))],
        out_specs=block,
        out_shape=jax.ShapeDtypeStruct((rows, D), bf16),
    )


def up_kernel(second_ref, up_ref, bias_ref, active_ref, slope_ref):
    pre = dot_over(second_ref[...], up_ref[...], 1, 1) + bias_ref[...]
    root = math.sqrt(2.0 / math.pi)
    square = pre * pre
    curve = jnp.tanh(pre * (root + (root * 0.044715) * square))
    half = 0.5 + 0.5 * curve
    active_ref[...] = (pre * half).astype(bf16)
    inner = root + (3.0 * root * 0.044715) * square
    slope_ref[...] = (half + (0.5 * pre) * (1.0 - curve * curve) * inner).astype(bf16)


def up_forward(second, up_full, bias, ties=()):
    rows, ff = second.shape[0], up_full.shape[0]
    tile = 512
    columns = pl.BlockSpec((rows, tile), lambda i: (0, i))
    return call(
        up_kernel,
        "up_forward",
        2 * rows * ff * D,
        (second, up_full, bias.reshape(1, ff)),
        ties,
        grid=(pl.cdiv(ff, tile),),
        in_specs=[
            pl.BlockSpec((rows, D), lambda i: (0, 0)),
            pl.BlockSpec((tile, D), lambda i: (i, 0)),
            pl.BlockSpec((1, tile), lambda i: (0, i)),
        ],
        out_specs=[columns, columns],
        out_shape=[jax.ShapeDtypeStruct((rows, ff), bf16)] * 2,
    )


def active_back_kernel(grad_ref, down_ref, slope_ref, out_ref, sum_ref):
    active_grad = dot_over(grad_ref[...], down_ref[...], 1, 1)
    low = (active_grad * slope_ref[...].astype(f32)).astype(bf16)
    out_ref[...] = low
    sum_ref[...] = jnp.sum(low.astype(f32), axis=0, keepdims=True)


def active_back(grad_low, down_full, slope, ties=()):
    rows, ff = slope.shape
    tile = 512
    columns = pl.BlockSpec((rows, tile), lambda i: (0, i))
    return call(
        active_back_kernel,
        "active_back",
        2 * rows * ff * D,
        (grad_low, down_full, slope),
        ties,
        grid=(pl.cdiv(ff, tile),),
        in_specs=[
            pl.BlockSpec((rows, D), lambda i: (0, 0)),
            pl.BlockSpec((tile, D), lambda i: (i, 0)),
            columns,
        ],
        out_specs=[columns, pl.BlockSpec((1, tile), lambda i: (0, i))],
        out_shape=[
            jax.ShapeDtypeStruct((rows, ff), bf16),
            jax.ShapeDtypeStruct((1, ff), f32),
        ],
    )


def row_mean(value):
    return jnp.sum(value, axis=-1, keepdims=True) * (1.0 / D)


def norm_back_rows(base, gradient, scales):
    center = base - row_mean(base)
    inverse = lax.rsqrt(row_mean(center * center) + norm_eps)
    hat = center * inverse
    scaled = gradient * scales
    back = inverse * (scaled - row_mean(scaled) - hat * row_mean(scaled * hat))
    return back, gradient * hat


def up_back_kernel(up_low_ref, up_ref, residual_ref, grad_ref, scale_ref, out_ref, low_ref, sums_ref):
    second_grad = dot_over(up_low_ref[...], up_ref[...], 1, 0)
    back, with_hat = norm_back_rows(residual_ref[...], second_grad, scale_ref[...])
    total = grad_ref[...].astype(f32) + back
    low = total.astype(bf16)
    out_ref[...] = total
    low_ref[...] = low

    @pl.when(pl.program_id(0) == 0)
    def _():
        sums_ref[...] = jnp.zeros_like(sums_ref)

    for at, value in enumerate([with_hat, second_grad, low.astype(f32)]):
        sums_ref[pl.ds(at, 1), :] += jnp.sum(value, axis=0, keepdims=True)


def up_back(up_low, up_full, residual, grad_low, scale, ties=()):
    rows, ff = up_low.shape
    size = 256
    block = pl.BlockSpec((size, D), lambda i: (i, 0))
    return call(
        up_back_kernel,
        "up_back",
        2 * rows * ff * D,
        (up_low, up_full, residual, grad_low, scale.reshape(1, D)),
        ties,
        grid=(rows // size,),
        in_specs=[
            pl.BlockSpec((size, ff), lambda i: (i, 0)),
            pl.BlockSpec((ff, D), lambda i: (0, 0)),
            block,
            block,
            pl.BlockSpec((1, D), lambda i: (0, 0)),
        ],
        out_specs=[block, block, pl.BlockSpec((8, D), lambda i: (0, 0))],
        out_shape=[
            jax.ShapeDtypeStruct((rows, D), f32),
            jax.ShapeDtypeStruct((rows, D), bf16),
            jax.ShapeDtypeStruct((8, D), f32),
        ],
    )


def qkv_kernel(normed_ref, weight_ref, bias_ref, out_ref):
    out_ref[...] = (dot_over(normed_ref[...], weight_ref[...], 1, 0) + bias_ref[...]).astype(bf16)


def qkv_forward(normed, attn_full, bias_rows, ties=()):
    rows = normed.shape[0]
    return call(
        qkv_kernel,
        "qkv_forward",
        6 * rows * D * D,
        (normed, attn_full, bias_rows.reshape(3, 1, D)),
        ties,
        grid=(3,),
        in_specs=[
            pl.BlockSpec((rows, D), lambda i: (0, 0)),
            pl.BlockSpec((None, D, D), lambda i: (i, 0, 0)),
            pl.BlockSpec((None, 1, D), lambda i: (i, 0, 0)),
        ],
        out_specs=pl.BlockSpec((None, rows, D), lambda i: (i, 0, 0)),
        out_shape=jax.ShapeDtypeStruct((3, rows, D), bf16),
    )


def qkv_back_kernel(dq_ref, dk_ref, dv_ref, weight_ref, base_ref, resid_ref, scale_ref, out_ref, sums_ref):
    normed_grad = dot_over(dq_ref[...], weight_ref[0], 1, 1)
    normed_grad += dot_over(dk_ref[...], weight_ref[1], 1, 1)
    normed_grad += dot_over(dv_ref[...], weight_ref[2], 1, 1)
    back, with_hat = norm_back_rows(base_ref[...].astype(f32), normed_grad, scale_ref[...])
    out_ref[...] = resid_ref[...] + back

    @pl.when(pl.program_id(0) == 0)
    def _():
        sums_ref[...] = jnp.zeros_like(sums_ref)

    totals = [with_hat, normed_grad, dq_ref[...].astype(f32), dv_ref[...].astype(f32)]
    for at, value in enumerate(totals):
        sums_ref[pl.ds(at, 1), :] += jnp.sum(value, axis=0, keepdims=True)


def qkv_back(rows_grad, attn_full, base, resid_grad, scale, ties=()):
    rows = base.shape[0]
    size = 256
    block = pl.BlockSpec((size, D), lambda i: (i, 0))
    return call(
        qkv_back_kernel,
        "qkv_back",
        6 * rows * D * D,
        (*rows_grad, attn_full, base, resid_grad, scale.reshape(1, D)),
        ties,
        grid=(rows // size,),
        in_specs=[block] * 3
        + [
            pl.BlockSpec((3, D, D), lambda i: (0, 0, 0)),
            block,
            block,
            pl.BlockSpec((1, D), lambda i: (0, 0)),
        ],
        out_specs=[block, pl.BlockSpec((8, D), lambda i: (0, 0))],
        out_shape=[
            jax.ShapeDtypeStruct((rows, D), f32),
            jax.ShapeDtypeStruct((8, D), f32),
        ],
    )


def plain_add_kernel(first_ref, second_ref, out_ref):
    out_ref[...] = first_ref[...] + second_ref[...]


def plain_add(first, second, ties=()):
    whole = pl.BlockSpec(first.shape, lambda: (0, 0))
    return call(
        plain_add_kernel,
        "plain_add",
        first.size,
        (first, second),
        ties,
        in_specs=[whole, whole],
        out_specs=whole,
        out_shape=jax.ShapeDtypeStruct(first.shape, f32),
    )


def adam_update(weight, mean_old, square_old, gradient, step_rate, decay_rate):
    mean_new = beta_first * mean_old + (1.0 - beta_first) * gradient
    square_new = beta_second * square_old + (1.0 - beta_second) * gradient * gradient
    mean_hat = mean_new / (1.0 - beta_first**STEP)
    square_hat = square_new / (1.0 - beta_second**STEP)
    weight_new = weight - step_rate * (
        mean_hat / (jnp.sqrt(square_hat) + adam_floor) + decay_rate * weight
    )
    return (weight_new, mean_new, square_new)


def per_device(
    hidden_in,
    cotangent,
    lengths,
    qkv_weight,
    qkv_mean,
    qkv_square,
    out_weight,
    out_mean,
    out_square,
    up_weight,
    up_mean,
    up_square,
    down_weight,
    down_mean,
    down_square,
    vectors,
    vectors_mean,
    vectors_square,
    upbias,
    upbias_mean,
    upbias_square,
):
    shards = (qkv_weight, out_weight, up_weight, down_weight, vectors, upbias)
    first_moments = (qkv_mean, out_mean, up_mean, down_mean, vectors_mean, upbias_mean)
    squares = (qkv_square, out_square, up_square, down_square, vectors_square, upbias_square)
    grid = Grid()
    n = D // grid.shards
    slots = hidden_in.shape[0]
    row_count = slots * BLOCK
    ff = 4 * D

    attn_units = jnp.stack(
        [qkv_weight[:, :D], qkv_weight[:, D : 2 * D], qkv_weight[:, 2 * D :], out_weight]
    )
    attn_unit = take(attn_units, grid.r).astype(bf16)
    small = jnp.concatenate([vectors.reshape(-1), upbias]).astype(bf16)
    small = jnp.pad(small, (0, EXTRA * D - small.shape[0])).reshape(EXTRA, D)
    attn_unit = jnp.concatenate([attn_unit, small])
    up_unit = lax.dynamic_slice_in_dim(up_weight, grid.r * n, n, 1).astype(bf16).T
    down_unit = lax.dynamic_slice_in_dim(down_weight, grid.r * n, n, 0).astype(bf16)

    positions = jnp.arange(BLOCK, dtype=jnp.int32)
    row_valid = (positions[None, :] < lengths[:, None]).astype(f32).reshape(row_count, 1)
    grad_out = cotangent.reshape(row_count, D).astype(f32) * row_valid
    grad_low = grad_out.astype(bf16)

    got, offs = gather_z(grid, attn_unit)
    attn_z = [part[:, :n] for part in got]
    small_z = jnp.concatenate([part[:, n:] for part in got])
    own = small_z.reshape(grid.zs, EXTRA * D)[:, : 12 * n]
    other = grid.move(own, over_x)
    up_z = gather_z(grid, after(up_unit, got[1], grad_low))[0]
    attn_xy, attn_pieces = gather_rest(grid, attn_z)
    up_held = after(jnp.concatenate(up_z), *attn_xy, other)
    up_both = jnp.stack([up_held, grid.move(up_held, y_then_x)])
    up_late = grid.move(up_both, x_then_y)
    down_unit = after(down_unit, *attn_pieces)
    joined = [offs[0] + offs[1]]
    attn_full = assemble(grid, attn_pieces, offs, n)

    pair = jnp.stack([own, other])
    pair = jnp.stack([take(pair, grid.x), take(pair, 1 - grid.x)])
    where_off = jnp.array([joined[0].index(z) for z in range(grid.zs)])
    pair = pair[:, where_off[jnp.bitwise_xor(grid.z, jnp.arange(grid.zs))]]
    smalls = pair.transpose(1, 0, 2).reshape(grid.shards, 12 * n)
    vec_values = (
        smalls[:, : 8 * n].reshape(grid.shards, 8, n).transpose(1, 0, 2).reshape(8, D).astype(f32)
    )
    bias_full = (
        smalls[:, 8 * n :].reshape(grid.shards, 4, n).transpose(1, 0, 2).reshape(ff).astype(f32)
    )

    attn_full = attn_full.reshape(4, D, D)
    out_full = attn_full[3]

    flat_in = hidden_in.reshape(row_count, D).astype(f32)
    normed_one, hat_one, inv_one = norm_forward(flat_in, vec_values[0], vec_values[1])
    normed_low = normed_one.astype(bf16)
    bias_rows = jnp.stack([vec_values[2], jnp.zeros((D,), f32), vec_values[3]])
    qkv_rows = qkv_forward(normed_low, attn_full, bias_rows, [down_unit])
    up_late = after(up_late, qkv_rows)
    down_held = down_unit[None]
    for bit in reversed(z_bits(grid.zs)[1:]):
        down_held = jnp.concatenate([down_held, after(grid.move(down_held, over_z(bit)), qkv_rows)])
    context_flat, logsum = attend(qkv_rows, [up_late, down_held])
    up_pieces = [up_both, up_late] + [
        after(grid.move(p, over_core), context_flat) for p in (up_both, up_late)
    ]
    down_last = after(grid.move(down_held, over_z(1)), context_flat)
    context_flat = after(context_flat, down_last)
    down_held = jnp.concatenate([down_held, down_last])
    up_full = assemble(grid, up_pieces, joined, n).reshape(ff, D)
    residual = (
        flat_in + jnp.dot(context_flat, out_full, preferred_element_type=f32) + vec_values[4]
    )
    second_low = norm_forward(residual, vec_values[5], vec_values[6])[0].astype(bf16)
    down_got = after(grid.move(down_held, y_then_x), up_full, second_low)
    down_both = jnp.stack([down_held, down_got])
    active_low, slope = up_forward(second_low, up_full, bias_full, [down_both])
    down_late = after(grid.move(down_both, x_then_y), active_low)
    down_bias_grad = jnp.sum(grad_out, axis=0)
    down_grad = weight_grad(active_low, grad_low, [down_late])
    down_pieces = [down_both, down_late] + [
        after(grid.move(p, over_core), down_grad) for p in (down_both, down_late)
    ]
    down_full = assemble(grid, down_pieces, joined, n).reshape(ff, D)
    down_sum = reduce_rows(grid, after(down_grad, *down_pieces), n)
    up_low, upbias_grad = active_back(grad_low, down_full, slope, [down_sum.sent])
    down_sum.hold(up_low)
    down_sent = down_sum.step()
    up_grad = weight_grad(up_low, second_low, [down_sent])
    down_sum.hold(up_grad)
    up_sum = reduce_rows(grid, after(up_grad, down_sum.step()), n)
    resid_grad, branch_low, norm_sums = up_back(
        up_low, up_full, residual, grad_low, vec_values[5], [up_sum.sent, down_sum.sent]
    )
    scale_two_grad, offset_two_grad, out_bias_grad = norm_sums[0], norm_sums[1], norm_sums[2]
    for each in (down_sum, up_sum):
        each.hold(branch_low)
    down_sent, up_sent = down_sum.step(), up_sum.step()
    out_grad = jnp.einsum(
        "nd,ne->de", context_flat, branch_low, preferred_element_type=f32
    ).astype(bf16)
    context_grad = times_transposed(branch_low, out_full)
    rows_grad = attend_back(
        qkv_rows, logsum, context_grad, [down_sent, up_sent, out_grad]
    )
    for each in (down_sum, up_sum):
        each.hold(rows_grad[0])
    rows_grad = after(tuple(rows_grad), up_sum.step(), down_sum.step())
    query_grad, key_grad, value_grad = [
        jnp.einsum("nd,ne->de", normed_low, part, preferred_element_type=f32).astype(bf16)
        for part in rows_grad
    ]
    first = grid.c == 0
    up_sum.hold(value_grad)
    value_grad = after(value_grad, up_sum.step())
    theirs = jnp.stack([jnp.where(first, key_grad, query_grad), jnp.where(first, out_grad, value_grad)])
    mine = jnp.stack([jnp.where(first, query_grad, key_grad), jnp.where(first, value_grad, out_grad)])
    split = (2, grid.shards, n, D)
    attn_sum = Reduction(grid, theirs.reshape(split), mine.reshape(split))
    attn_sent = attn_sum.step()
    down_sum.hold(attn_sent)
    input_grad, first_sums = qkv_back(
        rows_grad,
        attn_full,
        hidden_in.reshape(row_count, D),
        resid_grad,
        vec_values[0],
        [attn_sent],
    )
    input_grad = input_grad.reshape(slots, BLOCK, D)
    small_grad = jnp.concatenate(
        [first_sums[:4], out_bias_grad[None], norm_sums[:2], down_bias_grad[None]]
        + [upbias_grad.reshape(4, D)]
    )
    small_grad = jnp.concatenate(
        [first_sums[:4], out_bias_grad[None], norm_sums[:2], down_bias_grad[None]]
        + [upbias_grad.reshape(4, D)]
    )
    attn_sum.hold(first_sums)
    attn_sent = attn_sum.step()
    down_out = jnp.dot(
        after(active_low, attn_sent), down_full, preferred_element_type=f32
    ) + vec_values[7]
    output = ((residual + down_out) * row_valid).astype(bf16).reshape(slots, BLOCK, D)
    up_sum.hold(attn_sent)
    up_sum.step()
    routes = [over_core, over_y, over_x] + [over_z(bit) for bit in z_bits(grid.zs)]
    ties = [attn_sent]
    for at, route in enumerate(routes):
        if at >= 2 and attn_sum.left():
            attn_sum.hold(output, small_grad)
            ties = [attn_sum.step()]
        small_grad = plain_add(small_grad, grid.move(small_grad, route), ties)
        ties = [output]
    def update(at, gradient):
        return adam_update(
            shards[at], first_moments[at], squares[at], gradient, step_rates[at], decay_rates[at]
        )

    down_new = update(3, jnp.concatenate(share_unit(grid, down_sum.finish())).astype(f32))
    up_sum.hold(attn_sum.sent)
    up_unit_grad = up_sum.finish()
    while attn_sum.left():
        attn_sum.step()
    attn_sum.hold(small_grad)
    attn_unit_grad = attn_sum.finish()
    up_new = update(2, jnp.concatenate(share_unit(grid, up_unit_grad)).T.astype(f32))
    attn_parts = share_unit(grid, attn_unit_grad, [up_new[0], down_new[0]])
    small_own = lax.dynamic_slice_in_dim(small_grad, (2 * grid.z + grid.x) * n, n, 1)

    updates = (
        *update(0, jnp.concatenate(attn_parts[:3], axis=1).astype(f32)),
        *update(1, attn_parts[3].astype(f32)),
        *up_new,
        *down_new,
        *update(4, small_own[:8]),
        *update(5, small_own[8:].reshape(-1)),
    )
    return (output, input_grad) + updates


def solution(mesh):
    tokens = P(("fsdp", "dp"), None, None)
    rows, columns = P("fsdp", None), P(None, "fsdp")
    state = (rows,) * 6 + (columns,) * 3 + (rows,) * 3 + (columns,) * 3 + (P("fsdp"),) * 3
    return jax.shard_map(
        per_device,
        mesh=mesh,
        in_specs=(tokens, tokens, P(("fsdp", "dp"))) + state,
        out_specs=(tokens, tokens) + state,
        check_vma=False,
    )
```

```python
import functools
import math

import jax
import jax.numpy as jnp
from jax import lax
from jax.experimental import pallas as pl
from jax.experimental.pallas import tpu as pltpu
from jax.sharding import PartitionSpec as P

D = 1088
HEADS = 17
HDIM = 64
BLOCK = 512
STEP = 10
EXTRA = 8

norm_eps = 1e-05
beta_first = 0.9
beta_second = 0.999
adam_floor = 1e-08
step_rates = (0.05, 0.2, 0.05, 0.03, 0.5, 0.3)
decay_rates = (0.1, 0.1, 0.1, 0.1, 0.0, 0.0)

AXES = ("fsdp", "dp")
VMEM_LIMIT = 56 * 1024 * 1024
f32 = jnp.float32
bf16 = jnp.bfloat16


class Grid:
    def __init__(self):
        self.shards = lax.axis_size("fsdp")
        self.replicas = lax.axis_size("dp")
        self.zs = self.shards // 2
        self.ys = self.replicas // 2
        f, r = lax.axis_index("fsdp"), lax.axis_index("dp")
        self.z, self.x = f // 2, f % 2
        self.y, self.c = r // 2, r % 2
        self.r = r

    def move(self, value, route):
        pairs = []
        for z in range(self.zs):
            for x in range(2):
                for y in range(2):
                    for c in range(2):
                        to_z, to_x, to_y, to_c = route(z, x, y, c)
                        here = (2 * z + x) * 4 + 2 * y + c
                        pairs.append((here, (2 * to_z + to_x) * 4 + 2 * to_y + to_c))
        return lax.ppermute(value, AXES, pairs)


def over_z(bit):
    return lambda z, x, y, c: (z ^ bit, x, y, c)


def over_x(z, x, y, c):
    return (z, 1 - x, y, c)


def over_y(z, x, y, c):
    return (z, x, 1 - y, c)


def over_core(z, x, y, c):
    return (z, x, y, 1 - c)


def x_then_y(z, x, y, c):
    return (z, 1 - x, y, c) if c == 0 else (z, x, 1 - y, c)


def y_then_x(z, x, y, c):
    return (z, x, 1 - y, c) if c == 0 else (z, 1 - x, y, c)


def after(value, *others):
    return lax.optimization_barrier((value,) + others)[0]


def take(value, at, axis=0):
    return lax.dynamic_index_in_dim(value, at, axis, keepdims=False)


def z_bits(zs):
    return [1 << i for i in range(zs.bit_length() - 1)]


def gather_z(grid, unit):
    held, off = unit[None], [0]
    for bit in reversed(z_bits(grid.zs)[1:]):
        held = jnp.concatenate([held, grid.move(held, over_z(bit))])
        off = off + [z ^ bit for z in off]
    return [held, grid.move(held, over_z(1))], [off, [z ^ 1 for z in off]]


def gather_xy(grid, held):
    both = jnp.stack([held, grid.move(held, y_then_x)])
    return [both, grid.move(both, x_then_y)]


def gather_rest(grid, halves):
    pieces = [p for held in halves for p in gather_xy(grid, held)]
    return pieces, pieces + [grid.move(p, over_core) for p in pieces]


def assemble_kernel(zs, offs, *refs):
    count = 4 * len(offs)
    pieces, (out, held, in_sems, out_sem) = refs[:count], refs[count:]
    f, r = lax.axis_index("fsdp"), lax.axis_index("dp")
    z, x, y, c = f // 2, f % 2, r // 2, r % 2
    first, second = [], []
    for number in range(count):
        dc, late = number // (count // 2), number % 2
        off = offs[(number // 2) % len(offs)]
        core = c ^ dc
        for early in range(2):
            dx = late + core * (early - late)
            dy = early + core * (late - early)
            owner = 2 * (y ^ dy) + core
            for k in range(len(off)):
                place = (owner, 2 * (z ^ off[k]) + (x ^ dx))
                sem = in_sems.at[number]
                first.append(pltpu.make_async_copy(pieces[number].at[early, k], held.at[place], sem))
                second.append(pltpu.make_async_copy(held.at[place], out.at[place], out_sem))
    for copy in first:
        copy.start()
    each = len(first) // count
    for number in range(count):
        for copy in first[number * each : (number + 1) * each]:
            copy.wait()
        for copy in second[number * each : (number + 1) * each]:
            copy.start()
    for copy in second:
        copy.wait()


def assemble(grid, pieces, offs, rows):
    whole = (4, grid.shards, rows, D)
    return pl.pallas_call(
        functools.partial(assemble_kernel, grid.zs, offs),
        out_shape=jax.ShapeDtypeStruct(whole, bf16),
        in_specs=[pl.BlockSpec(memory_space=pl.ANY)] * len(pieces),
        out_specs=pl.BlockSpec(memory_space=pl.ANY),
        scratch_shapes=[
            pltpu.VMEM(whole, bf16),
            pltpu.SemaphoreType.DMA((len(pieces),)),
            pltpu.SemaphoreType.DMA(()),
        ],
        compiler_params=pltpu.CompilerParams(vmem_limit_bytes=VMEM_LIMIT),
        cost_estimate=pl.CostEstimate(flops=0, bytes_accessed=20_000_000, transcendentals=0),
        name="assemble",
    )(*pieces)


def add(first, second):
    return (first.astype(f32) + second.astype(f32)).astype(bf16)


class Reduction:
    def __init__(self, grid, theirs, mine):
        self.grid, self.n = grid, mine.shape[2]
        self.stage = 0
        self.bits = z_bits(grid.zs)
        self.keep, self.sent = mine, theirs
        self.route = over_core

    def step(self):
        grid, n = self.grid, self.n
        mine, got = self.keep, grid.move(self.sent, self.route)
        first = grid.c == 0
        x, y = grid.x, grid.y
        if self.stage == 0:
            shape = (2, grid.zs, 2, n, D)

            def pick(value, at_x, at_y):
                value = value.reshape(shape)
                return jnp.where(first, take(value, at_x, 2), take(value, at_y, 0).swapaxes(0, 1))

            self.sent = add(pick(mine, 1 - x, 1 - y), pick(got, 1 - x, 1 - y))
            mine, got = after(mine, self.sent), after(got, self.sent)
            self.keep = add(pick(mine, x, y), pick(got, x, y))
            self.route = x_then_y
        elif self.stage == 1:
            at = jnp.where(first, y, x)
            self.sent = add(take(mine, 1 - at), take(got, 1 - at))
            self.keep = add(take(mine, at), take(got, at))
            self.route = y_then_x
        elif self.stage - 2 < len(self.bits):
            bit = self.bits[self.stage - 2]
            at = (grid.z // bit) % 2
            mine, got = mine.reshape(-1, 2, n, D), got.reshape(-1, 2, n, D)
            self.sent = add(take(mine, 1 - at, 1), take(got, 1 - at, 1))
            self.keep = add(take(mine, at, 1), take(got, at, 1))
            self.route = over_z(bit)
        else:
            return add(mine, got)[0]
        self.stage += 1
        return self.sent

    def hold(self, *others):
        self.keep = after(self.keep, *others)

    def left(self):
        return self.stage - 2 < len(self.bits)

    def finish(self):
        while self.left():
            self.step()
        return self.step()


def reduce_rows(grid, grads, n):
    view = grads.reshape(2, 2, grid.shards, n, D)
    return Reduction(grid, take(view, 1 - grid.c, 1), take(view, grid.c, 1))


def share_unit(grid, unit, others=()):
    got = grid.move(unit, over_y)
    if others:
        got = after(got, *others)
    pair = jnp.stack([unit, got])
    both = jnp.stack([pair, grid.move(pair, over_core)], axis=1).reshape((4,) + unit.shape)
    return [take(both, jnp.bitwise_xor(grid.r, r)) for r in range(4)]


def norm_forward(values, scales, offset):
    center = values - jnp.mean(values, axis=-1, keepdims=True)
    inverse = lax.rsqrt(jnp.mean(center * center, axis=-1, keepdims=True) + norm_eps)
    norm_hat = center * inverse
    return (norm_hat * scales + offset, norm_hat, inverse)


def norm_backward(gradient, norm_hat, inverse, scales):
    hat_grad = gradient * scales
    value_grad = inverse * (
        hat_grad
        - jnp.mean(hat_grad, axis=-1, keepdims=True)
        - norm_hat * jnp.mean(hat_grad * norm_hat, axis=-1, keepdims=True)
    )
    return (value_grad, jnp.sum(gradient * norm_hat, axis=0), jnp.sum(gradient, axis=0))


def head_masks(rows):
    lane = lax.broadcasted_iota(jnp.int32, (rows, 128), 1)
    return (lane < HDIM, lane >= HDIM)


def dot_over(left, right, left_at, right_at):
    return lax.dot_general(
        left, right, (((left_at,), (right_at,)), ((), ())), preferred_element_type=f32
    )


def score_tile(keys, queries, tile, size):
    scores = dot_over(keys, queries, 1, 1)
    rows_at = lax.broadcasted_iota(jnp.int32, scores.shape, 0)
    cols_at = lax.broadcasted_iota(jnp.int32, scores.shape, 1) + tile * size
    return jnp.where(rows_at <= cols_at, scores, -1e30)


def attend_kernel(q_ref, k_ref, v_ref, c_ref, lse_ref):
    size = 256
    masks = head_masks(BLOCK)

    def slab(at, width, heads, first):
        columns = pl.ds(at, width)
        values = v_ref[:, columns]
        parts = []
        for h in range(heads):
            parts.append(jnp.where(masks[h], values, 0) if heads > 1 else values)
        for tile in range(BLOCK // size):
            extent = (tile + 1) * size
            keys = k_ref[pl.ds(0, extent), columns]
            queries = q_ref[pl.ds(tile * size, size), columns] * 0.125
            total = None
            for h in range(heads):
                mine = jnp.where(masks[h][:size], queries, 0) if heads > 1 else queries
                scores = score_tile(keys, mine, tile, size)
                top = jnp.max(scores, axis=0, keepdims=True)
                powers = jnp.exp(scores - top)
                norm = jnp.sum(powers, axis=0, keepdims=True)
                probs = (powers * (1.0 / norm)).astype(bf16)
                lse_ref[first + h, :, pl.ds(tile * size, size)] = top + jnp.log(norm)
                piece = dot_over(probs, parts[h][:extent], 0, 0)
                total = piece if total is None else total + piece
            c_ref[pl.ds(tile * size, size), columns] = total.astype(bf16)

    def pair(i, _):
        slab(pl.multiple_of(i * 128, 128), 128, 2, 2 * i)
        return 0

    lax.fori_loop(0, HEADS // 2, pair, 0)
    slab((HEADS - 1) * HDIM, HDIM, 1, HEADS - 1)


def attend_back_kernel(q_ref, k_ref, v_ref, lse_ref, dc_ref, dq_ref, dk_ref, dv_ref):
    size = 256
    masks = head_masks(BLOCK)

    def slab(at, width, heads, first):
        columns = pl.ds(at, width)
        keys_all = k_ref[:, columns]
        key_parts = [jnp.where(masks[h], keys_all, 0) if heads > 1 else keys_all for h in range(heads)]
        dk_total, dv_total = None, None
        for tile in reversed(range(BLOCK // size)):
            extent = (tile + 1) * size
            keys = keys_all[:extent]
            values = v_ref[pl.ds(0, extent), columns]
            queries = q_ref[pl.ds(tile * size, size), columns] * 0.125
            grads = dc_ref[pl.ds(tile * size, size), columns]
            dq_total, dk_tile, dv_tile = None, None, None
            for h in range(heads):
                my_q = jnp.where(masks[h][:size], queries, 0) if heads > 1 else queries
                my_g = jnp.where(masks[h][:size], grads, 0) if heads > 1 else grads
                scores = score_tile(keys, my_q, tile, size)
                probs = jnp.exp(scores - lse_ref[first + h, :, pl.ds(tile * size, size)])
                prob_grad = dot_over(values, my_g, 1, 1)
                inner = jnp.sum(probs * prob_grad, axis=0, keepdims=True)
                score_grad = (probs * (prob_grad - inner)).astype(bf16)
                dv = dot_over(probs.astype(bf16), my_g, 1, 0)
                dk = dot_over(score_grad, my_q, 1, 0)
                dq = dot_over(score_grad, key_parts[h][:extent], 0, 0)
                dv_tile = dv if dv_tile is None else dv_tile + dv
                dk_tile = dk if dk_tile is None else dk_tile + dk
                dq_total = dq if dq_total is None else dq_total + dq
            dq_ref[pl.ds(tile * size, size), columns] = (dq_total * 0.125).astype(bf16)
            if dk_total is None:
                dk_total, dv_total = dk_tile, dv_tile
            else:
                dk_total = jnp.concatenate([dk_total[:extent] + dk_tile, dk_total[extent:]])
                dv_total = jnp.concatenate([dv_total[:extent] + dv_tile, dv_total[extent:]])
        dk_ref[:, columns] = dk_total.astype(bf16)
        dv_ref[:, columns] = dv_total.astype(bf16)

    def pair(i, _):
        slab(pl.multiple_of(i * 128, 128), 128, 2, 2 * i)
        return 0

    lax.fori_loop(0, HEADS // 2, pair, 0)
    slab((HEADS - 1) * HDIM, HDIM, 1, HEADS - 1)


def part_block(part):
    return pl.BlockSpec((None, BLOCK, D), lambda i: (part, i, 0))


def attend(qkv, ties=()):
    rows = qkv.shape[1]
    block = pl.BlockSpec((BLOCK, D), lambda i: (i, 0))
    lse = pl.BlockSpec((HEADS, 1, BLOCK), lambda i: (0, 0, i))
    return call(
        attend_kernel,
        "attend",
        14_000_000_000,
        (qkv, qkv, qkv),
        ties,
        grid=(rows // BLOCK,),
        in_specs=[part_block(0), part_block(1), part_block(2)],
        out_specs=[block, lse],
        out_shape=[
            jax.ShapeDtypeStruct((rows, D), bf16),
            jax.ShapeDtypeStruct((HEADS, 1, rows), f32),
        ],
    )


def attend_back(qkv, lse, context_grad, ties=()):
    rows = qkv.shape[1]
    block = pl.BlockSpec((BLOCK, D), lambda i: (i, 0))
    lse_block = pl.BlockSpec((HEADS, 1, BLOCK), lambda i: (0, 0, i))
    return call(
        attend_back_kernel,
        "attend_back",
        18_000_000_000,
        (qkv, qkv, qkv, lse, context_grad),
        ties,
        grid=(rows // BLOCK,),
        in_specs=[part_block(0), part_block(1), part_block(2), lse_block, block],
        out_specs=[block] * 3,
        out_shape=[jax.ShapeDtypeStruct((rows, D), bf16)] * 3,
    )


def call(kernel, name, flops, operands, ties=(), in_specs=(), **kw):
    count = len(operands)

    def body(*refs):
        kernel(*refs[:count], *refs[count + len(ties) :])

    return pl.pallas_call(
        body,
        in_specs=list(in_specs) + [pl.BlockSpec(memory_space=pl.ANY)] * len(ties),
        compiler_params=pltpu.CompilerParams(vmem_limit_bytes=VMEM_LIMIT),
        cost_estimate=pl.CostEstimate(flops=flops, bytes_accessed=20_000_000, transcendentals=0),
        name=name,
        **kw,
    )(*operands, *ties)


def weight_grad_kernel(left_ref, right_ref, out_ref):
    out_ref[...] = dot_over(left_ref[...], right_ref[...], 0, 0).astype(bf16)


def weight_grad(left, right, ties=()):
    rows, wide = left.shape
    tile = 512
    return call(
        weight_grad_kernel,
        "weight_grad",
        2 * rows * wide * D,
        (left, right),
        ties,
        grid=(pl.cdiv(wide, tile),),
        in_specs=[
            pl.BlockSpec((rows, tile), lambda i: (0, i)),
            pl.BlockSpec((rows, D), lambda i: (0, 0)),
        ],
        out_specs=pl.BlockSpec((tile, D), lambda i: (i, 0)),
        out_shape=jax.ShapeDtypeStruct((wide, D), bf16),
    )


def times_transposed_kernel(left_ref, right_ref, out_ref):
    out_ref[...] = dot_over(left_ref[...], right_ref[...], 1, 1).astype(bf16)


def times_transposed(left, right):
    rows, size = left.shape[0], BLOCK
    block = pl.BlockSpec((size, D), lambda i: (i, 0))
    return call(
        times_transposed_kernel,
        "times_transposed",
        2 * rows * D * D,
        (left, right),
        grid=(rows // size,),
        in_specs=[block, pl.BlockSpec((D, D), lambda i: (0, 0))],
        out_specs=block,
        out_shape=jax.ShapeDtypeStruct((rows, D), bf16),
    )


def up_kernel(second_ref, up_ref, bias_ref, active_ref, slope_ref):
    pre = dot_over(second_ref[...], up_ref[...], 1, 1) + bias_ref[...]
    root = math.sqrt(2.0 / math.pi)
    square = pre * pre
    curve = jnp.tanh(pre * (root + (root * 0.044715) * square))
    half = 0.5 + 0.5 * curve
    active_ref[...] = (pre * half).astype(bf16)
    inner = root + (3.0 * root * 0.044715) * square
    slope_ref[...] = (half + (0.5 * pre) * (1.0 - curve * curve) * inner).astype(bf16)


def up_forward(second, up_full, bias, ties=()):
    rows, ff = second.shape[0], up_full.shape[0]
    tile = 512
    columns = pl.BlockSpec((rows, tile), lambda i: (0, i))
    return call(
        up_kernel,
        "up_forward",
        2 * rows * ff * D,
        (second, up_full, bias.reshape(1, ff)),
        ties,
        grid=(pl.cdiv(ff, tile),),
        in_specs=[
            pl.BlockSpec((rows, D), lambda i: (0, 0)),
            pl.BlockSpec((tile, D), lambda i: (i, 0)),
            pl.BlockSpec((1, tile), lambda i: (0, i)),
        ],
        out_specs=[columns, columns],
        out_shape=[jax.ShapeDtypeStruct((rows, ff), bf16)] * 2,
    )


def active_back_kernel(grad_ref, down_ref, slope_ref, out_ref, sum_ref):
    active_grad = dot_over(grad_ref[...], down_ref[...], 1, 1)
    low = (active_grad * slope_ref[...].astype(f32)).astype(bf16)
    out_ref[...] = low
    sum_ref[...] = jnp.sum(low.astype(f32), axis=0, keepdims=True)


def active_back(grad_low, down_full, slope, ties=()):
    rows, ff = slope.shape
    tile = 512
    columns = pl.BlockSpec((rows, tile), lambda i: (0, i))
    return call(
        active_back_kernel,
        "active_back",
        2 * rows * ff * D,
        (grad_low, down_full, slope),
        ties,
        grid=(pl.cdiv(ff, tile),),
        in_specs=[
            pl.BlockSpec((rows, D), lambda i: (0, 0)),
            pl.BlockSpec((tile, D), lambda i: (i, 0)),
            columns,
        ],
        out_specs=[columns, pl.BlockSpec((1, tile), lambda i: (0, i))],
        out_shape=[
            jax.ShapeDtypeStruct((rows, ff), bf16),
            jax.ShapeDtypeStruct((1, ff), f32),
        ],
    )


def row_mean(value):
    return jnp.sum(value, axis=-1, keepdims=True) * (1.0 / D)


def norm_back_rows(base, gradient, scales):
    center = base - row_mean(base)
    inverse = lax.rsqrt(row_mean(center * center) + norm_eps)
    hat = center * inverse
    scaled = gradient * scales
    back = inverse * (scaled - row_mean(scaled) - hat * row_mean(scaled * hat))
    return back, gradient * hat


def up_back_kernel(up_low_ref, up_ref, residual_ref, grad_ref, scale_ref, out_ref, low_ref, sums_ref):
    second_grad = dot_over(up_low_ref[...], up_ref[...], 1, 0)
    back, with_hat = norm_back_rows(residual_ref[...], second_grad, scale_ref[...])
    total = grad_ref[...].astype(f32) + back
    low = total.astype(bf16)
    out_ref[...] = total
    low_ref[...] = low

    @pl.when(pl.program_id(0) == 0)
    def _():
        sums_ref[...] = jnp.zeros_like(sums_ref)

    for at, value in enumerate([with_hat, second_grad, low.astype(f32)]):
        sums_ref[pl.ds(at, 1), :] += jnp.sum(value, axis=0, keepdims=True)


def up_back(up_low, up_full, residual, grad_low, scale, ties=()):
    rows, ff = up_low.shape
    size = 256
    block = pl.BlockSpec((size, D), lambda i: (i, 0))
    return call(
        up_back_kernel,
        "up_back",
        2 * rows * ff * D,
        (up_low, up_full, residual, grad_low, scale.reshape(1, D)),
        ties,
        grid=(rows // size,),
        in_specs=[
            pl.BlockSpec((size, ff), lambda i: (i, 0)),
            pl.BlockSpec((ff, D), lambda i: (0, 0)),
            block,
            block,
            pl.BlockSpec((1, D), lambda i: (0, 0)),
        ],
        out_specs=[block, block, pl.BlockSpec((8, D), lambda i: (0, 0))],
        out_shape=[
            jax.ShapeDtypeStruct((rows, D), f32),
            jax.ShapeDtypeStruct((rows, D), bf16),
            jax.ShapeDtypeStruct((8, D), f32),
        ],
    )


def qkv_kernel(normed_ref, weight_ref, bias_ref, out_ref):
    out_ref[...] = (dot_over(normed_ref[...], weight_ref[...], 1, 0) + bias_ref[...]).astype(bf16)


def qkv_forward(normed, attn_full, bias_rows, ties=()):
    rows = normed.shape[0]
    return call(
        qkv_kernel,
        "qkv_forward",
        6 * rows * D * D,
        (normed, attn_full, bias_rows.reshape(3, 1, D)),
        ties,
        grid=(3,),
        in_specs=[
            pl.BlockSpec((rows, D), lambda i: (0, 0)),
            pl.BlockSpec((None, D, D), lambda i: (i, 0, 0)),
            pl.BlockSpec((None, 1, D), lambda i: (i, 0, 0)),
        ],
        out_specs=pl.BlockSpec((None, rows, D), lambda i: (i, 0, 0)),
        out_shape=jax.ShapeDtypeStruct((3, rows, D), bf16),
    )


def qkv_back_kernel(dq_ref, dk_ref, dv_ref, weight_ref, base_ref, resid_ref, scale_ref, out_ref, sums_ref):
    normed_grad = dot_over(dq_ref[...], weight_ref[0], 1, 1)
    normed_grad += dot_over(dk_ref[...], weight_ref[1], 1, 1)
    normed_grad += dot_over(dv_ref[...], weight_ref[2], 1, 1)
    back, with_hat = norm_back_rows(base_ref[...].astype(f32), normed_grad, scale_ref[...])
    out_ref[...] = resid_ref[...] + back

    @pl.when(pl.program_id(0) == 0)
    def _():
        sums_ref[...] = jnp.zeros_like(sums_ref)

    totals = [with_hat, normed_grad, dq_ref[...].astype(f32), dv_ref[...].astype(f32)]
    for at, value in enumerate(totals):
        sums_ref[pl.ds(at, 1), :] += jnp.sum(value, axis=0, keepdims=True)


def qkv_back(rows_grad, attn_full, base, resid_grad, scale, ties=()):
    rows = base.shape[0]
    size = 256
    block = pl.BlockSpec((size, D), lambda i: (i, 0))
    return call(
        qkv_back_kernel,
        "qkv_back",
        6 * rows * D * D,
        (*rows_grad, attn_full, base, resid_grad, scale.reshape(1, D)),
        ties,
        grid=(rows // size,),
        in_specs=[block] * 3
        + [
            pl.BlockSpec((3, D, D), lambda i: (0, 0, 0)),
            block,
            block,
            pl.BlockSpec((1, D), lambda i: (0, 0)),
        ],
        out_specs=[block, pl.BlockSpec((8, D), lambda i: (0, 0))],
        out_shape=[
            jax.ShapeDtypeStruct((rows, D), f32),
            jax.ShapeDtypeStruct((8, D), f32),
        ],
    )


def plain_add_kernel(first_ref, second_ref, out_ref):
    out_ref[...] = first_ref[...] + second_ref[...]


def plain_add(first, second, ties=()):
    whole = pl.BlockSpec(first.shape, lambda: (0, 0))
    return call(
        plain_add_kernel,
        "plain_add",
        first.size,
        (first, second),
        ties,
        in_specs=[whole, whole],
        out_specs=whole,
        out_shape=jax.ShapeDtypeStruct(first.shape, f32),
    )


def adam_update(weight, mean_old, square_old, gradient, step_rate, decay_rate):
    mean_new = beta_first * mean_old + (1.0 - beta_first) * gradient
    square_new = beta_second * square_old + (1.0 - beta_second) * gradient * gradient
    mean_hat = mean_new / (1.0 - beta_first**STEP)
    square_hat = square_new / (1.0 - beta_second**STEP)
    weight_new = weight - step_rate * (
        mean_hat / (jnp.sqrt(square_hat) + adam_floor) + decay_rate * weight
    )
    return (weight_new, mean_new, square_new)


def per_device(
    hidden_in,
    cotangent,
    lengths,
    qkv_weight,
    qkv_mean,
    qkv_square,
    out_weight,
    out_mean,
    out_square,
    up_weight,
    up_mean,
    up_square,
    down_weight,
    down_mean,
    down_square,
    vectors,
    vectors_mean,
    vectors_square,
    upbias,
    upbias_mean,
    upbias_square,
):
    shards = (qkv_weight, out_weight, up_weight, down_weight, vectors, upbias)
    first_moments = (qkv_mean, out_mean, up_mean, down_mean, vectors_mean, upbias_mean)
    squares = (qkv_square, out_square, up_square, down_square, vectors_square, upbias_square)
    grid = Grid()
    n = D // grid.shards
    slots = hidden_in.shape[0]
    row_count = slots * BLOCK
    ff = 4 * D

    attn_units = jnp.stack(
        [qkv_weight[:, :D], qkv_weight[:, D : 2 * D], qkv_weight[:, 2 * D :], out_weight]
    )
    attn_unit = take(attn_units, grid.r).astype(bf16)
    small = jnp.concatenate([vectors.reshape(-1), upbias]).astype(bf16)
    small = jnp.pad(small, (0, EXTRA * D - small.shape[0])).reshape(EXTRA, D)
    attn_unit = jnp.concatenate([attn_unit, small])
    up_unit = lax.dynamic_slice_in_dim(up_weight, grid.r * n, n, 1).astype(bf16).T
    down_unit = lax.dynamic_slice_in_dim(down_weight, grid.r * n, n, 0).astype(bf16)

    positions = jnp.arange(BLOCK, dtype=jnp.int32)
    row_valid = (positions[None, :] < lengths[:, None]).astype(f32).reshape(row_count, 1)
    grad_out = cotangent.reshape(row_count, D).astype(f32) * row_valid
    grad_low = grad_out.astype(bf16)

    got, offs = gather_z(grid, attn_unit)
    attn_z = [part[:, :n] for part in got]
    small_z = jnp.concatenate([part[:, n:] for part in got])
    own = small_z.reshape(grid.zs, EXTRA * D)[:, : 12 * n]
    other = grid.move(own, over_x)
    up_z = gather_z(grid, after(up_unit, got[1], grad_low))[0]
    attn_xy, attn_pieces = gather_rest(grid, attn_z)
    up_held = after(jnp.concatenate(up_z), *attn_xy, other)
    up_both = jnp.stack([up_held, grid.move(up_held, y_then_x)])
    up_late = grid.move(up_both, x_then_y)
    down_unit = after(down_unit, *attn_pieces)
    joined = [offs[0] + offs[1]]
    attn_full = assemble(grid, attn_pieces, offs, n)

    pair = jnp.stack([own, other])
    pair = jnp.stack([take(pair, grid.x), take(pair, 1 - grid.x)])
    where_off = jnp.array([joined[0].index(z) for z in range(grid.zs)])
    pair = pair[:, where_off[jnp.bitwise_xor(grid.z, jnp.arange(grid.zs))]]
    smalls = pair.transpose(1, 0, 2).reshape(grid.shards, 12 * n)
    vec_values = (
        smalls[:, : 8 * n].reshape(grid.shards, 8, n).transpose(1, 0, 2).reshape(8, D).astype(f32)
    )
    bias_full = (
        smalls[:, 8 * n :].reshape(grid.shards, 4, n).transpose(1, 0, 2).reshape(ff).astype(f32)
    )

    attn_full = attn_full.reshape(4, D, D)
    out_full = attn_full[3]

    flat_in = hidden_in.reshape(row_count, D).astype(f32)
    normed_one, hat_one, inv_one = norm_forward(flat_in, vec_values[0], vec_values[1])
    normed_low = normed_one.astype(bf16)
    bias_rows = jnp.stack([vec_values[2], jnp.zeros((D,), f32), vec_values[3]])
    qkv_rows = qkv_forward(normed_low, attn_full, bias_rows, [down_unit])
    up_late = after(up_late, qkv_rows)
    down_held = down_unit[None]
    for bit in reversed(z_bits(grid.zs)[1:]):
        down_held = jnp.concatenate([down_held, after(grid.move(down_held, over_z(bit)), qkv_rows)])
    context_flat, logsum = attend(qkv_rows, [up_late, down_held])
    up_pieces = [up_both, up_late] + [
        after(grid.move(p, over_core), context_flat) for p in (up_both, up_late)
    ]
    down_last = after(grid.move(down_held, over_z(1)), context_flat)
    context_flat = after(context_flat, down_last)
    down_held = jnp.concatenate([down_held, down_last])
    up_full = assemble(grid, up_pieces, joined, n).reshape(ff, D)
    residual = (
        flat_in + jnp.dot(context_flat, out_full, preferred_element_type=f32) + vec_values[4]
    )
    second_low = norm_forward(residual, vec_values[5], vec_values[6])[0].astype(bf16)
    down_got = after(grid.move(down_held, y_then_x), up_full, second_low)
    down_both = jnp.stack([down_held, down_got])
    active_low, slope = up_forward(second_low, up_full, bias_full, [down_both])
    down_late = after(grid.move(down_both, x_then_y), active_low)
    down_bias_grad = jnp.sum(grad_out, axis=0)
    down_grad = weight_grad(active_low, grad_low, [down_late])
    down_pieces = [down_both, down_late] + [
        after(grid.move(p, over_core), down_grad) for p in (down_both, down_late)
    ]
    down_full = assemble(grid, down_pieces, joined, n).reshape(ff, D)
    down_sum = reduce_rows(grid, after(down_grad, *down_pieces), n)
    up_low, upbias_grad = active_back(grad_low, down_full, slope, [down_sum.sent])
    down_sum.hold(up_low)
    down_sent = down_sum.step()
    up_grad = weight_grad(up_low, second_low, [down_sent])
    down_sum.hold(up_grad)
    up_sum = reduce_rows(grid, after(up_grad, down_sum.step()), n)
    resid_grad, branch_low, norm_sums = up_back(
        up_low, up_full, residual, grad_low, vec_values[5], [up_sum.sent, down_sum.sent]
    )
    scale_two_grad, offset_two_grad, out_bias_grad = norm_sums[0], norm_sums[1], norm_sums[2]
    for each in (down_sum, up_sum):
        each.hold(branch_low)
    down_sent, up_sent = down_sum.step(), up_sum.step()
    out_grad = jnp.einsum(
        "nd,ne->de", context_flat, branch_low, preferred_element_type=f32
    ).astype(bf16)
    context_grad = times_transposed(branch_low, out_full)
    rows_grad = attend_back(
        qkv_rows, logsum, context_grad, [down_sent, up_sent, out_grad]
    )
    for each in (down_sum, up_sum):
        each.hold(rows_grad[0])
    rows_grad = after(tuple(rows_grad), up_sum.step(), down_sum.step())
    query_grad, key_grad, value_grad = [
        jnp.einsum("nd,ne->de", normed_low, part, preferred_element_type=f32).astype(bf16)
        for part in rows_grad
    ]
    first = grid.c == 0
    for each in (down_sum, up_sum):
        each.hold(value_grad)
    if down_sum.left():
        down_sum.step()
        down_ready = down_sum.sent
    else:
        down_ready = down_unit_grad = down_sum.step()
    value_grad = after(value_grad, up_sum.step(), down_ready)
    theirs = jnp.stack([jnp.where(first, key_grad, query_grad), jnp.where(first, out_grad, value_grad)])
    mine = jnp.stack([jnp.where(first, query_grad, key_grad), jnp.where(first, value_grad, out_grad)])
    split = (2, grid.shards, n, D)
    attn_sum = Reduction(grid, theirs.reshape(split), mine.reshape(split))
    attn_sent = attn_sum.step()
    input_grad, first_sums = qkv_back(
        rows_grad,
        attn_full,
        hidden_in.reshape(row_count, D),
        resid_grad,
        vec_values[0],
        [attn_sent],
    )
    input_grad = input_grad.reshape(slots, BLOCK, D)
    small_grad = jnp.concatenate(
        [first_sums[:4], out_bias_grad[None], norm_sums[:2], down_bias_grad[None]]
        + [upbias_grad.reshape(4, D)]
    )
    small_grad = jnp.concatenate(
        [first_sums[:4], out_bias_grad[None], norm_sums[:2], down_bias_grad[None]]
        + [upbias_grad.reshape(4, D)]
    )
    attn_sum.hold(first_sums)
    attn_sent = attn_sum.step()
    down_out = jnp.dot(
        after(active_low, attn_sent), down_full, preferred_element_type=f32
    ) + vec_values[7]
    output = ((residual + down_out) * row_valid).astype(bf16).reshape(slots, BLOCK, D)
    up_sum.hold(attn_sent)
    up_sum.step()
    routes = [over_core, over_y, over_x] + [over_z(bit) for bit in z_bits(grid.zs)]
    ties = [attn_sent]
    for at, route in enumerate(routes):
        if at >= 2 and attn_sum.left():
            attn_sum.hold(output)
            ties = [attn_sum.step()]
        small_grad = plain_add(small_grad, grid.move(small_grad, route), ties)
        ties = [output]
    if down_sum.left():
        down_unit_grad = down_sum.finish()
    up_sum.hold(attn_sum.sent)
    up_unit_grad = up_sum.finish()
    attn_unit_grad = attn_sum.finish()
    small_own = lax.dynamic_slice_in_dim(small_grad, (2 * grid.z + grid.x) * n, n, 1)

    def update(at, gradient):
        return adam_update(
            shards[at], first_moments[at], squares[at], gradient, step_rates[at], decay_rates[at]
        )

    down_new = update(3, jnp.concatenate(share_unit(grid, down_unit_grad)).astype(f32))
    up_new = update(2, jnp.concatenate(share_unit(grid, up_unit_grad)).T.astype(f32))
    attn_parts = share_unit(grid, attn_unit_grad, [up_new[0], down_new[0]])
    updates = (
        *update(0, jnp.concatenate(attn_parts[:3], axis=1).astype(f32)),
        *update(1, attn_parts[3].astype(f32)),
        *up_new,
        *down_new,
        *update(4, small_own[:8]),
        *update(5, small_own[8:].reshape(-1)),
    )
    return (output, input_grad) + updates


def solution(mesh):
    tokens = P(("fsdp", "dp"), None, None)
    rows, columns = P("fsdp", None), P(None, "fsdp")
    state = (rows,) * 6 + (columns,) * 3 + (rows,) * 3 + (columns,) * 3 + (P("fsdp"),) * 3
    return jax.shard_map(
        per_device,
        mesh=mesh,
        in_specs=(tokens, tokens, P(("fsdp", "dp"))) + state,
        out_specs=(tokens, tokens) + state,
        check_vma=False,
    )
```
